128 devices in a mesh: dp: 32 (over z, y, x_hi), mp: 4 (over x_lo, core).
Axes of the slice: x: 4 (x_hi: 2, x_lo: 2; x = x_hi * 2 + x_lo), y: 4, z: 4, core: 2. Of those that a mesh axis runs over, the one named last changes fastest.
Arguments:
- gen_input: bfloat16 [12288, 3072], P(('dp', 'mp')), may hold values from -6 to 6
- noise_score: bfloat16 [12288, 3072], P(('dp', 'mp')), may hold values from -24 to 24
- gen_steps: int32 [12], replicated, may hold values from 0 to 999
- score_steps: int32 [12], replicated, may hold values from 20 to 979
- base_up: bfloat16 [3072, 6144], P('dp', 'mp'), may hold values from -0.109375 to 0.109375
- base_down: bfloat16 [6144, 3072], P('mp', 'dp'), may hold values from -0.078125 to 0.078125
- gen_adapt_in: bfloat16 [3072, 64], replicated, may hold values from -0.109375 to 0.109375
- gen_adapt_out: bfloat16 [64, 6144], P(None, 'mp'), may hold values from -0.75 to 0.75
- fake_adapt_in: bfloat16 [3072, 64], replicated, may hold values from -0.109375 to 0.109375
- fake_adapt_out: bfloat16 [64, 6144], P(None, 'mp'), may hold values from -0.75 to 0.75
- modulation_scale: float32 [3072], replicated, may hold values from -1.8 to 1.8
- modulation_shift: float32 [3072], replicated, may hold values from -1.8 to 1.8
- output_gate: float32 [3072], replicated, may hold values from 0.5 to 1.5
Outputs:
- score_diff: bfloat16 [12288, 3072], P(('dp', 'mp'))
- gen_grad_in: float32 [3072, 64], P(('dp', 'mp'))
- gen_grad_out: float32 [64, 6144], P('dp', 'mp')
- fake_grad_in: float32 [3072, 64], P(('dp', 'mp'))
- fake_grad_out: float32 [64, 6144], P('dp', 'mp')
The draws below stay inside these ranges and needn't reach their ends.
All inputs are finite; a program needn't handle non-finite values.
Results may differ from the reference program's by a relative error of at most 0.035.
Values may be sent and summed in bfloat16 or wider, within the bound.
No kernel may reach another device: no remote copies, remote signals or barrier semaphores. Data moves between devices by JAX's collectives and lax.ppermute only.
A program may use at most 128 MiB of HBM per device.

```python
import math
import jax
import jax.numpy as jnp
from jax import lax

D = 3072
H = 6144
R = 64
IMG_TOK = 1024
TOKENS = 12288
IMAGES = 12


def place_ends(result, stream_key, low, top_value):
    longest = result.shape.index(max(result.shape))
    spots = []
    for shift in (0, 1):
        where = [jax.random.randint(jax.random.fold_in(stream_key, axis), (), 0, length) for axis, length in enumerate(result.shape)]
        where[longest] = (where[longest] + shift) % result.shape[longest]
        spots.append(tuple(where))
    return result.at[spots[0]].set(low).at[spots[1]].set(top_value)


def raised(result, key, source, target, shards_of, factor):
    owner, partner = [(jnp.arange(result.shape[axis_at]) // (result.shape[axis_at] // shards_of)).reshape([-1 if axis == axis_at else 1 for axis in range(result.ndim)]) for axis_at in (source, target)]
    chosen = jax.random.permutation(key, shards_of)[partner]
    strong = (owner == chosen) | (owner == (partner + shards_of // 2) % shards_of)
    return jnp.where(strong, factor * result, result)


def block_levels(own_key, shape, shards, smallest, high):
    factor_of, own = 1.0, jax.random.fold_in(own_key, 6)
    for dim, blocks in shards:
        heights = jnp.exp(jax.random.uniform(jax.random.fold_in(own, dim), (blocks,), jnp.float32, smallest / len(shards), high / len(shards)))
        factor_of = factor_of * jnp.repeat(heights, shape[dim] // blocks).reshape([-1 if axis == dim else 1 for axis in range(len(shape))])
    return factor_of


def noise(own_key, dims, deviation, bound, cuts=(), kind=jnp.bfloat16):
    loudness = block_levels(own_key, dims, cuts, -0.22, 0.18) if cuts else 1.0
    drawn = jax.random.normal(own_key, dims, jnp.float32) * deviation * loudness
    return jnp.minimum(jnp.maximum(drawn, -bound), bound).astype(kind)


def gaussian_with(stream_key, dims, scale, reach, pieces, heavy, kind=jnp.bfloat16):
    result = scale * jax.random.normal(stream_key, dims, jnp.float32)
    if pieces:
        result = result * block_levels(stream_key, dims, pieces, -0.22, 0.18)
    return jnp.clip(raised(result, jax.random.fold_in(stream_key, 3), *heavy), -reach, reach).astype(kind)


def setup_inputs(seed: int = 0) -> dict:
    streams_of = jax.random.split(jax.random.key(seed), 14)
    return {
        "gen_input": noise(streams_of[0], (TOKENS, D), 1.0, 6.0, ((0, 128),)),
        "noise_score": gaussian_with(streams_of[1], (TOKENS, D), 1.0, 24.0, ((0, 128),), (0, 1, 128, 5.5)),
        "gen_steps": place_ends(jax.random.randint(streams_of[2], (IMAGES,), 0, 1000), jax.random.fold_in(streams_of[2], 1), 0, 999).astype(jnp.int32),
        "score_steps": place_ends(jax.random.randint(streams_of[3], (IMAGES,), 20, 980), jax.random.fold_in(streams_of[3], 1), 20, 979).astype(jnp.int32),
        "base_up": noise(streams_of[4], (D, H), D ** -0.5, 0.109375, ((0, 32), (1, 4))),
        "base_down": noise(streams_of[5], (H, D), H ** -0.5, 0.078125, ((0, 4), (1, 32))),
        "gen_adapt_in": noise(streams_of[6], (D, R), D ** -0.5, 0.109375),
        "gen_adapt_out": noise(streams_of[7], (R, H), R ** -0.5, 0.75, ((1, 4),)),
        "fake_adapt_in": noise(streams_of[8], (D, R), D ** -0.5, 0.109375),
        "fake_adapt_out": noise(streams_of[9], (R, H), R ** -0.5, 0.75, ((1, 4),)),
        "modulation_scale": noise(streams_of[10], (D,), 0.3, 1.8, (), jnp.float32),
        "modulation_shift": noise(streams_of[11], (D,), 0.3, 1.8, (), jnp.float32),
        "output_gate": jnp.clip(1.0 + 0.1 * jax.random.normal(streams_of[12], (D,), jnp.float32), 0.5, 1.5),
    }


gelu_coef = 0.044715
root_two_pi = math.sqrt(2.0 / math.pi)

def gelu_value(pre):
    inner_arg = root_two_pi * (pre + gelu_coef * pre * pre * pre)
    return 0.5 * pre * (1.0 + jnp.tanh(inner_arg))

def gelu_slope(pre):
    tanh_val = jnp.tanh(root_two_pi * (pre + gelu_coef * pre * pre * pre))
    return 0.5 * (1.0 + tanh_val) + 0.5 * pre * (1.0 - tanh_val * tanh_val) * root_two_pi * (1.0 + 3.0 * gelu_coef * pre * pre)

def embedding(steps, feature_count):
    half_width = feature_count // 2
    frequency = jnp.exp(-math.log(10000.0) * jnp.arange(half_width, dtype=jnp.float32) / half_width)
    phase_angle = steps.astype(jnp.float32)[:, None] * frequency[None, :]
    return jnp.concatenate([jnp.sin(phase_angle), jnp.cos(phase_angle)], axis=1)

def modulate(rows, embed, modulation_scale, modulation_shift):
    widened = rows.astype(jnp.float32)
    normed = widened * lax.rsqrt(lax.optimization_barrier(jnp.mean(widened * widened, axis=1, keepdims=True)) + 1e-06)
    return (normed * (1.0 + modulation_scale * embed) + modulation_shift * embed).astype(jnp.bfloat16)

def matmul(left, right):
    return jnp.dot(left, right, preferred_element_type=jnp.float32)

def contract(left, right, left_dim, right_dim):
    return lax.dot_general(left, right, (((left_dim,), (right_dim,)), ((), ())), preferred_element_type=jnp.float32)

def reference(gen_input, noise_score, gen_steps, score_steps, base_up, base_down, gen_adapt_in, gen_adapt_out, fake_adapt_in, fake_adapt_out, modulation_scale, modulation_shift, output_gate):
    image_count = gen_steps.shape[0]
    feature_count = gen_input.shape[1]
    loss_scale = 1.0 / math.sqrt(image_count * IMG_TOK)
    embed_gen = embedding(gen_steps, feature_count)
    embed_score = embedding(score_steps, feature_count)
    blend_all = (score_steps.astype(jnp.float32) + 0.5) / 1000.0
    input_blocks = gen_input.reshape(image_count, IMG_TOK, feature_count)
    noise_blocks = noise_score.reshape(image_count, IMG_TOK, feature_count)

    def image_step(carry, packed):
        given_rows, noise_rows, gen_embed, score_embed, blend = packed
        u_gen = modulate(given_rows, gen_embed[None, :], modulation_scale, modulation_shift)
        low_gen = matmul(u_gen, gen_adapt_in).astype(jnp.bfloat16)
        pre_gen = matmul(u_gen, base_up) + matmul(low_gen, gen_adapt_out)
        act_gen = gelu_value(pre_gen).astype(jnp.bfloat16)
        out_gen = matmul(act_gen, base_down)
        latents = (given_rows.astype(jnp.float32) + output_gate * out_gen).astype(jnp.bfloat16)
        noised = ((1.0 - blend) * latents.astype(jnp.float32) + blend * noise_rows.astype(jnp.float32)).astype(jnp.bfloat16)
        u_score = modulate(noised, score_embed[None, :], modulation_scale, modulation_shift)
        low_fake = matmul(u_score, fake_adapt_in).astype(jnp.bfloat16)
        pre_real = matmul(u_score, base_up)
        pre_fake = pre_real + matmul(low_fake, fake_adapt_out)
        act_real = gelu_value(pre_real).astype(jnp.bfloat16)
        act_fake = gelu_value(pre_fake).astype(jnp.bfloat16)
        out_real = matmul(act_real, base_down)
        out_fake = matmul(act_fake, base_down)
        diff_rows = (output_gate * (out_fake - out_real)).astype(jnp.bfloat16)
        cot_gen = (output_gate * diff_rows.astype(jnp.float32) * loss_scale).astype(jnp.bfloat16)
        target = noise_rows.astype(jnp.float32) - latents.astype(jnp.float32)
        cot_fake = (output_gate * (noised.astype(jnp.float32) + output_gate * out_fake - target) * loss_scale).astype(jnp.bfloat16)
        back_gen = (contract(cot_gen, base_down, 1, 1) * gelu_slope(pre_gen)).astype(jnp.bfloat16)
        back_fake = (contract(cot_fake, base_down, 1, 1) * gelu_slope(pre_fake)).astype(jnp.bfloat16)
        out_grad_gen = contract(low_gen, back_gen, 0, 0)
        out_grad_fake = contract(low_fake, back_fake, 0, 0)
        mix_gen = contract(back_gen, gen_adapt_out, 1, 1)
        mix_fake = contract(back_fake, fake_adapt_out, 1, 1)
        in_grad_gen = lax.dot_general(u_gen.astype(jnp.float32), mix_gen, (((0,), (0,)), ((), ())), precision=lax.Precision.HIGHEST, preferred_element_type=jnp.float32)
        in_grad_fake = lax.dot_general(u_score.astype(jnp.float32), mix_fake, (((0,), (0,)), ((), ())), precision=lax.Precision.HIGHEST, preferred_element_type=jnp.float32)
        summed = (carry[0] + in_grad_gen, carry[1] + out_grad_gen, carry[2] + in_grad_fake, carry[3] + out_grad_fake)
        return (summed, diff_rows)
    adapter_rank = gen_adapt_in.shape[1]
    hidden_count = base_up.shape[1]
    start_carry = (jnp.zeros((feature_count, adapter_rank), jnp.float32), jnp.zeros((adapter_rank, hidden_count), jnp.float32), jnp.zeros((feature_count, adapter_rank), jnp.float32), jnp.zeros((adapter_rank, hidden_count), jnp.float32))
    grads, diff_blocks = lax.scan(image_step, start_carry, (input_blocks, noise_blocks, embed_gen, embed_score, blend_all))
    score_diff = diff_blocks.reshape(image_count * IMG_TOK, feature_count)
    return (score_diff, grads[0], grads[1], grads[2], grads[3])
```

```python
import math

import jax
import jax.numpy as jnp
from jax import lax
from jax.sharding import Mesh
from jax.sharding import PartitionSpec as P

IMG_TOK = 1024
AXES = ("z", "y", "xh", "xl", "core")
CHIPS = ("z", "y", "xh", "xl")

gelu_coef = 0.044715
root_two_pi = math.sqrt(2.0 / math.pi)


def gelu_value(pre):
    inner_arg = root_two_pi * (pre + gelu_coef * pre * pre * pre)
    return 0.5 * pre * (1.0 + jnp.tanh(inner_arg))


def gelu_slope(pre):
    tanh_val = jnp.tanh(root_two_pi * (pre + gelu_coef * pre * pre * pre))
    return 0.5 * (1.0 + tanh_val) + 0.5 * pre * (1.0 - tanh_val * tanh_val) * root_two_pi * (
        1.0 + 3.0 * gelu_coef * pre * pre
    )


def embedding(steps, feature_count):
    half_width = feature_count // 2
    frequency = jnp.exp(-math.log(10000.0) * jnp.arange(half_width, dtype=jnp.float32) / half_width)
    phase_angle = steps.astype(jnp.float32)[:, None] * frequency[None, :]
    return jnp.concatenate([jnp.sin(phase_angle), jnp.cos(phase_angle)], axis=1)


def modulate(rows, scale_rows, shift_rows):
    widened = rows.astype(jnp.float32)
    normed = widened * lax.rsqrt(jnp.mean(widened * widened, axis=1, keepdims=True) + 1e-06)
    return (normed * scale_rows + shift_rows).astype(jnp.bfloat16)


def matmul(left, right):
    return jnp.dot(left, right, preferred_element_type=jnp.float32)


def contract(left, right, left_dim, right_dim):
    return lax.dot_general(
        left, right, (((left_dim,), (right_dim,)), ((), ())), preferred_element_type=jnp.float32
    )


def swap_cores(value):
    return lax.ppermute(value, "core", [(0, 1), (1, 0)])


def three_terms(value):
    high = lax.reduce_precision(value, 8, 7)
    rest = value - high
    middle = lax.reduce_precision(rest, 8, 7)
    low = rest - middle
    return jnp.concatenate([high, middle, low], axis=1).astype(jnp.bfloat16)


def local(
    gen_input,
    noise_score,
    gen_steps,
    score_steps,
    base_up,
    base_down,
    gen_adapt_in,
    gen_adapt_out,
    fake_adapt_in,
    fake_adapt_out,
    modulation_scale,
    modulation_shift,
    output_gate,
):
    bf16, f32 = jnp.bfloat16, jnp.float32
    shard_rows, width = gen_input.shape
    hidden = base_up.shape[1]
    rank = gen_adapt_in.shape[1]
    image_count = gen_steps.shape[0]
    loss_scale = 1.0 / math.sqrt(image_count * IMG_TOK)
    core = lax.axis_index("core")
    xl = lax.axis_index("xl")
    first_row = lax.axis_index(AXES) * shard_rows
    first_image = first_row // IMG_TOK
    last_image = (first_row + shard_rows - 1) // IMG_TOK
    row_ids = first_row + jnp.arange(shard_rows, dtype=jnp.int32)
    in_last = (row_ids >= last_image * IMG_TOK)[:, None]

    def two_steps(steps):
        return jnp.stack([steps[first_image], steps[last_image]])

    def modulation(steps):
        embed = embedding(two_steps(steps), width)
        scale = 1.0 + modulation_scale[None, :] * embed
        shift = modulation_shift[None, :] * embed
        return (
            jnp.where(in_last, scale[1:], scale[:1]),
            jnp.where(in_last, shift[1:], shift[:1]),
        )

    def both_rows(mine):
        return jnp.concatenate([mine, swap_cores(mine)], axis=0)

    up_all = lax.all_gather(base_up, ("xl", "z", "y", "xh"), axis=0, tiled=True)
    down_all = lax.all_gather(base_down.T, ("xl", "z", "y", "xh"), axis=0, tiled=True)
    up_all = up_all.reshape(2, width, hidden)
    down_all = down_all.reshape(2, width, hidden)

    def other_quarter(mine):
        theirs = lax.ppermute(mine, "xl", [(0, 1), (1, 0)])
        return jnp.stack([jnp.where(xl == 0, mine, theirs), jnp.where(xl == 0, theirs, mine)])

    adapt_out = other_quarter(jnp.concatenate([gen_adapt_out, fake_adapt_out], axis=0))
    gen_out, fake_out = adapt_out[:, :rank], adapt_out[:, rank:]

    u_mine = modulate(gen_input, *modulation(gen_steps))
    u_gen = both_rows(u_mine)
    low_gen = matmul(u_gen, gen_adapt_in).astype(bf16)
    pre_gen = [matmul(u_gen, up_all[q]) + matmul(low_gen, gen_out[q]) for q in range(2)]
    act_gen = [gelu_value(p).astype(bf16) for p in pre_gen]

    def down(acts):
        return contract(acts[0], down_all[0], 1, 1) + contract(acts[1], down_all[1], 1, 1)

    out_gen = down(act_gen)
    out_mine = out_gen[:shard_rows] + swap_cores(out_gen[shard_rows:].astype(bf16)).astype(f32)
    latents = (gen_input.astype(f32) + output_gate * out_mine).astype(bf16)
    two_blend = (two_steps(score_steps).astype(f32) + 0.5) / 1000.0
    blend = jnp.where(in_last, two_blend[1], two_blend[0])
    noised = ((1.0 - blend) * latents.astype(f32) + blend * noise_score.astype(f32)).astype(bf16)
    u_score = both_rows(modulate(noised, *modulation(score_steps)))
    low_fake = matmul(u_score, fake_adapt_in).astype(bf16)
    pre_real = [matmul(u_score, up_all[q]) for q in range(2)]
    pre_fake = [pre_real[q] + matmul(low_fake, fake_out[q]) for q in range(2)]
    acts = [
        jnp.concatenate([gelu_value(pre_real[q]), gelu_value(pre_fake[q])], axis=0).astype(bf16)
        for q in range(2)
    ]
    outs = down(acts)
    parts = [outs[i * shard_rows : (i + 1) * shard_rows] for i in range(4)]
    got = swap_cores(jnp.concatenate([parts[1], parts[3]], axis=0).astype(bf16)).astype(f32)
    out_real = parts[0] + got[:shard_rows]
    out_fake = parts[2] + got[shard_rows:]
    score_diff = (output_gate * (out_fake - out_real)).astype(bf16)
    cot_gen = (output_gate * score_diff.astype(f32) * loss_scale).astype(bf16)
    target = noise_score.astype(f32) - latents.astype(f32)
    cot_fake = (
        output_gate * (noised.astype(f32) + output_gate * out_fake - target) * loss_scale
    ).astype(bf16)
    cots = jnp.concatenate([cot_gen, cot_fake], axis=0)
    cots_other = swap_cores(cots)
    cots = jnp.concatenate(
        [cot_gen, cots_other[:shard_rows], cot_fake, cots_other[shard_rows:]], axis=0
    )
    group = 2 * shard_rows
    backs = [matmul(cots, down_all[q]) for q in range(2)]
    back_gen = [(backs[q][:group] * gelu_slope(pre_gen[q])).astype(bf16) for q in range(2)]
    back_fake = [(backs[q][group:] * gelu_slope(pre_fake[q])).astype(bf16) for q in range(2)]

    def out_grad(low, back):
        return [contract(low, back[q], 0, 0) for q in range(2)]

    def mixed(back, adapter):
        return contract(back[0], adapter[0], 1, 1) + contract(back[1], adapter[1], 1, 1)

    mix = jnp.concatenate([mixed(back_gen, gen_out), mixed(back_fake, fake_out)], axis=1)
    mix_other = swap_cores(mix)
    mix = mix + jnp.concatenate([mix_other[shard_rows:], mix_other[:shard_rows]], axis=0)

    def in_grad(u, mix_part):
        product = contract(u, three_terms(mix_part), 0, 0)
        total = product[:, :rank] + product[:, rank : 2 * rank] + product[:, 2 * rank :]
        chips = total.reshape(-1, 2, width // 128, rank)
        return jnp.where(core == 0, chips[:, 0], chips[:, 1])

    in_grads = jnp.concatenate([in_grad(u_gen, mix[:, :rank]), in_grad(u_score, mix[:, rank:])], axis=2)
    chips, in_rows = in_grads.shape[0], in_grads.shape[1]
    groups = chips // 2
    out_grads = jnp.stack(
        [jnp.stack(out_grad(low_gen, back_gen)), jnp.stack(out_grad(low_fake, back_fake))]
    )
    out_grads = out_grads.reshape(2, 2, groups, rank // groups, hidden).transpose(2, 1, 0, 3, 4)
    out_rows = 2 * (rank // groups) * hidden // 128
    packed = jnp.concatenate(
        [in_grads.astype(bf16), out_grads.astype(bf16).reshape(chips, out_rows, 128)], axis=1
    )
    received = lax.all_to_all(packed, CHIPS, 0, 0, tiled=True)
    summed = jnp.sum(received.astype(f32), axis=0)
    gen_grad_in, fake_grad_in = summed[:in_rows, :rank], summed[:in_rows, rank:]
    grads_out = summed[in_rows:].reshape(2, rank // groups, hidden)
    return (score_diff, gen_grad_in, grads_out[0], fake_grad_in, grads_out[1])


def solution(mesh):
    fine = Mesh(mesh.devices.reshape(4, 4, 2, 2, 2), AXES)
    dp, mp = ("z", "y", "xh"), ("xl", "core")
    return jax.shard_map(
        local,
        mesh=fine,
        in_specs=(
            P(AXES, None),
            P(AXES, None),
            P(),
            P(),
            P(dp, mp),
            P(mp, dp),
            P(),
            P(None, mp),
            P(),
            P(None, mp),
            P(),
            P(),
            P(),
        ),
        out_specs=(
            P(AXES, None),
            P(AXES, None),
            P(dp, mp),
            P(AXES, None),
            P(dp, mp),
        ),
        check_vma=False,
    )
```

```python
import math

import jax
import jax.numpy as jnp
from jax import lax
from jax.experimental import pallas as pl
from jax.experimental.pallas import tpu as pltpu
from jax.sharding import Mesh
from jax.sharding import PartitionSpec as P

IMG_TOK = 1024
AXES = ("z", "y", "xh", "xl", "core")
CHIPS = ("z", "y", "xh", "xl")

gelu_coef = 0.044715
root_two_pi = math.sqrt(2.0 / math.pi)


def gelu_value(pre):
    inner_arg = root_two_pi * (pre + gelu_coef * pre * pre * pre)
    return 0.5 * pre * (1.0 + jnp.tanh(inner_arg))


def gelu_slope(pre):
    tanh_val = jnp.tanh(root_two_pi * (pre + gelu_coef * pre * pre * pre))
    return 0.5 * (1.0 + tanh_val) + 0.5 * pre * (1.0 - tanh_val * tanh_val) * root_two_pi * (
        1.0 + 3.0 * gelu_coef * pre * pre
    )


def embedding(steps, feature_count):
    half_width = feature_count // 2
    frequency = jnp.exp(-math.log(10000.0) * jnp.arange(half_width, dtype=jnp.float32) / half_width)
    phase_angle = steps.astype(jnp.float32)[:, None] * frequency[None, :]
    return jnp.concatenate([jnp.sin(phase_angle), jnp.cos(phase_angle)], axis=1)


def modulate(rows, scale_rows, shift_rows):
    widened = rows.astype(jnp.float32)
    normed = widened * lax.rsqrt(jnp.mean(widened * widened, axis=1, keepdims=True) + 1e-06)
    return (normed * scale_rows + shift_rows).astype(jnp.bfloat16)


def matmul(left, right):
    return jnp.dot(left, right, preferred_element_type=jnp.float32)


def contract(left, right, left_dim, right_dim):
    return lax.dot_general(
        left, right, (((left_dim,), (right_dim,)), ((), ())), preferred_element_type=jnp.float32
    )


def swap_cores(value):
    return lax.ppermute(value, "core", [(0, 1), (1, 0)])


RING_AXES = (("y", "z", "x"), ("z", "x", "y"), ("x", "y", "z"))
RING = 4


def chip_ring(axis):
    pairs = []
    for device in range(128):
        place = {"z": device // 32, "y": device // 8 % 4, "x": device // 2 % 4, "core": device % 2}
        step = 1 if place["core"] == 0 else -1
        place[axis] = (place[axis] + step) % RING
        target = place["z"] * 32 + place["y"] * 8 + place["x"] * 2 + place["core"]
        pairs.append((device, target))
    return pairs


def ring_slots(pieces):
    for phase in range(3):
        slots = [[piece] for piece in pieces]
        for _ in range(RING - 1):
            for i, held in enumerate(slots):
                held.append(lax.ppermute(held[-1], AXES, chip_ring(RING_AXES[i][phase])))
        if phase < 2:
            pieces = [jnp.concatenate(held, axis=0) for held in slots]
    return slots


def place_kernel(steps, whole, place_ref, *refs):
    count = 3 * len(steps)
    slots, rest = refs[:count], refs[count:]
    whole_ref = rest[0] if whole else None
    up_ref, down_ref, sems = rest[-3:]
    me = {"z": place_ref[0], "y": place_ref[1], "x": place_ref[2]}
    direction = place_ref[3]
    targets = ((up_ref, 0), (up_ref, 1), (down_ref, 0))

    def source(axis, step):
        return lax.rem(me[axis] - step * direction + RING, RING)

    def where(axis_steps):
        at = {axis: source(axis, step) for axis, step in axis_steps}
        quarter = lax.rem(at["x"], 2)
        group = (at["z"] * 4 + at["y"]) * 2 + at["x"] // 2
        return quarter, group

    if whole:
        for quarter in range(2):
            pltpu.make_async_copy(
                whole_ref.at[:, quarter], down_ref.at[quarter, :, 1], sems.at[count + quarter]
            ).start()
    for n, step in enumerate(steps):
        for i in range(3):
            first, second, third = RING_AXES[i]
            target, part = targets[i]
            slot = slots[n * 3 + i]
            for t in range(RING):
                for u in range(RING):
                    quarter, group = where(((first, u), (second, t), (third, step)))
                    pltpu.make_async_copy(
                        slot.at[t * RING + u], target.at[quarter, group, part], sems.at[n * 3 + i]
                    ).start()
    if whole:
        for quarter in range(2):
            pltpu.make_async_copy(
                whole_ref.at[:, quarter], down_ref.at[quarter, :, 1], sems.at[count + quarter]
            ).wait()
    for n in range(len(steps)):
        for i in range(3):
            target, part = targets[i]
            slot = slots[n * 3 + i]
            pltpu.make_async_copy(
                slot, target.at[0, pl.ds(0, 16), part], sems.at[n * 3 + i]
            ).wait()


def place(steps, slots, whole, placed, coords):
    flat = [slots[i][step] for step in steps for i in range(3)]
    rows, hidden = flat[0].shape[0] // 16, flat[0].shape[1]
    flat = [x.reshape(16, rows, hidden) for x in flat]
    shape = jax.ShapeDtypeStruct((2, 32, 2, rows, hidden), flat[0].dtype)
    extra = [] if whole is None else [whole.reshape(32, 2, rows, hidden)]
    kept = [] if placed is None else list(placed)
    count = 1 + len(flat) + len(extra)
    anywhere = pl.BlockSpec(memory_space=pl.ANY)

    def body(place_ref, *refs):
        inputs = refs[: len(flat) + len(extra)]
        outputs = refs[len(flat) + len(extra) + len(kept) :]
        place_kernel(steps, whole is not None, place_ref, *inputs, *outputs)

    moved = 2 * 2 * rows * hidden * (16 * len(flat) + 64 * len(extra))
    return pl.pallas_call(
        body,
        out_shape=(shape, shape),
        in_specs=[pl.BlockSpec(memory_space=pltpu.SMEM)] + [anywhere] * (count - 1 + len(kept)),
        out_specs=(anywhere, anywhere),
        scratch_shapes=[pltpu.SemaphoreType.DMA((len(flat) + 2,))],
        input_output_aliases={count: 0, count + 1: 1} if kept else {},
        cost_estimate=pl.CostEstimate(flops=0, bytes_accessed=moved, transcendentals=0),
    )(coords, *flat, *extra, *kept)


def three_terms(value):
    high = lax.reduce_precision(value, 8, 7)
    rest = value - high
    middle = lax.reduce_precision(rest, 8, 7)
    low = rest - middle
    return jnp.concatenate([high, middle, low], axis=1).astype(jnp.bfloat16)


def local(
    gen_input,
    noise_score,
    gen_steps,
    score_steps,
    base_up,
    base_down,
    gen_adapt_in,
    gen_adapt_out,
    fake_adapt_in,
    fake_adapt_out,
    modulation_scale,
    modulation_shift,
    output_gate,
):
    bf16, f32 = jnp.bfloat16, jnp.float32
    shard_rows, width = gen_input.shape
    hidden = base_up.shape[1]
    rank = gen_adapt_in.shape[1]
    image_count = gen_steps.shape[0]
    loss_scale = 1.0 / math.sqrt(image_count * IMG_TOK)
    core = lax.axis_index("core")
    xl = lax.axis_index("xl")
    first_row = lax.axis_index(AXES) * shard_rows
    first_image = first_row // IMG_TOK
    last_image = (first_row + shard_rows - 1) // IMG_TOK
    row_ids = first_row + jnp.arange(shard_rows, dtype=jnp.int32)
    in_last = (row_ids >= last_image * IMG_TOK)[:, None]

    def two_steps(steps):
        return jnp.stack([steps[first_image], steps[last_image]])

    def modulation(steps):
        embed = embedding(two_steps(steps), width)
        scale = 1.0 + modulation_scale[None, :] * embed
        shift = modulation_shift[None, :] * embed
        return (
            jnp.where(in_last, scale[1:], scale[:1]),
            jnp.where(in_last, shift[1:], shift[:1]),
        )

    def both_rows(mine):
        return jnp.concatenate([mine, swap_cores(mine)], axis=0)

    coords = jnp.stack(
        [
            lax.axis_index("z"),
            lax.axis_index("y"),
            lax.axis_index("xh") * 2 + xl,
            1 - 2 * core,
        ]
    ).astype(jnp.int32)
    down_rows = base_down.T
    half = base_up.shape[0] // 2
    last_quarter = lax.all_gather(down_rows[half:], CHIPS, axis=0, tiled=True)
    slots = ring_slots([base_up[:half], base_up[half:], down_rows[:half]])
    placed = place((0, 1, 2), slots, last_quarter, None, coords)
    up_all, down_all = place((3,), slots, None, placed, coords)
    up_all = up_all.reshape(2, width, hidden)
    down_all = down_all.reshape(2, width, hidden)

    def other_quarter(mine):
        theirs = lax.ppermute(mine, "xl", [(0, 1), (1, 0)])
        return jnp.stack([jnp.where(xl == 0, mine, theirs), jnp.where(xl == 0, theirs, mine)])

    adapt_out = other_quarter(jnp.concatenate([gen_adapt_out, fake_adapt_out], axis=0))
    gen_out, fake_out = adapt_out[:, :rank], adapt_out[:, rank:]

    u_mine = modulate(gen_input, *modulation(gen_steps))
    u_gen = both_rows(u_mine)
    low_gen = matmul(u_gen, gen_adapt_in).astype(bf16)
    pre_gen = [matmul(u_gen, up_all[q]) + matmul(low_gen, gen_out[q]) for q in range(2)]
    act_gen = [gelu_value(p).astype(bf16) for p in pre_gen]

    def down(acts):
        return contract(acts[0], down_all[0], 1, 1) + contract(acts[1], down_all[1], 1, 1)

    out_gen = down(act_gen)
    out_mine = out_gen[:shard_rows] + swap_cores(out_gen[shard_rows:].astype(bf16)).astype(f32)
    latents = (gen_input.astype(f32) + output_gate * out_mine).astype(bf16)
    two_blend = (two_steps(score_steps).astype(f32) + 0.5) / 1000.0
    blend = jnp.where(in_last, two_blend[1], two_blend[0])
    noised = ((1.0 - blend) * latents.astype(f32) + blend * noise_score.astype(f32)).astype(bf16)
    u_score = both_rows(modulate(noised, *modulation(score_steps)))
    low_fake = matmul(u_score, fake_adapt_in).astype(bf16)
    pre_real = [matmul(u_score, up_all[q]) for q in range(2)]
    pre_fake = [pre_real[q] + matmul(low_fake, fake_out[q]) for q in range(2)]
    acts = [
        jnp.concatenate([gelu_value(pre_real[q]), gelu_value(pre_fake[q])], axis=0).astype(bf16)
        for q in range(2)
    ]
    outs = down(acts)
    parts = [outs[i * shard_rows : (i + 1) * shard_rows] for i in range(4)]
    got = swap_cores(jnp.concatenate([parts[1], parts[3]], axis=0).astype(bf16)).astype(f32)
    out_real = parts[0] + got[:shard_rows]
    out_fake = parts[2] + got[shard_rows:]
    score_diff = (output_gate * (out_fake - out_real)).astype(bf16)
    cot_gen = (output_gate * score_diff.astype(f32) * loss_scale).astype(bf16)
    target = noise_score.astype(f32) - latents.astype(f32)
    cot_fake = (
        output_gate * (noised.astype(f32) + output_gate * out_fake - target) * loss_scale
    ).astype(bf16)
    cots = jnp.concatenate([cot_gen, cot_fake], axis=0)
    cots_other = swap_cores(cots)
    cots = jnp.concatenate(
        [cot_gen, cots_other[:shard_rows], cot_fake, cots_other[shard_rows:]], axis=0
    )
    group = 2 * shard_rows
    backs = [matmul(cots, down_all[q]) for q in range(2)]
    back_gen = [(backs[q][:group] * gelu_slope(pre_gen[q])).astype(bf16) for q in range(2)]
    back_fake = [(backs[q][group:] * gelu_slope(pre_fake[q])).astype(bf16) for q in range(2)]

    def out_grad(low, back):
        return [contract(low, back[q], 0, 0) for q in range(2)]

    def mixed(back, adapter):
        return contract(back[0], adapter[0], 1, 1) + contract(back[1], adapter[1], 1, 1)

    mix = jnp.concatenate([mixed(back_gen, gen_out), mixed(back_fake, fake_out)], axis=1)
    mix_other = swap_cores(mix)
    mix = mix + jnp.concatenate([mix_other[shard_rows:], mix_other[:shard_rows]], axis=0)

    def in_grad(u, mix_part):
        product = contract(u, three_terms(mix_part), 0, 0)
        total = product[:, :rank] + product[:, rank : 2 * rank] + product[:, 2 * rank :]
        chips = total.reshape(-1, 2, width // 128, rank)
        return jnp.where(core == 0, chips[:, 0], chips[:, 1])

    in_grads = jnp.concatenate([in_grad(u_gen, mix[:, :rank]), in_grad(u_score, mix[:, rank:])], axis=2)
    chips, in_rows = in_grads.shape[0], in_grads.shape[1]
    groups = chips // 2
    out_grads = jnp.stack(
        [jnp.stack(out_grad(low_gen, back_gen)), jnp.stack(out_grad(low_fake, back_fake))]
    )
    out_grads = out_grads.reshape(2, 2, groups, rank // groups, hidden).transpose(2, 1, 0, 3, 4)
    out_rows = 2 * (rank // groups) * hidden // 128
    packed = jnp.concatenate(
        [in_grads.astype(bf16), out_grads.astype(bf16).reshape(chips, out_rows, 128)], axis=1
    )
    received = lax.all_to_all(packed, CHIPS, 0, 0, tiled=True)
    summed = jnp.sum(received.astype(f32), axis=0)
    gen_grad_in, fake_grad_in = summed[:in_rows, :rank], summed[:in_rows, rank:]
    grads_out = summed[in_rows:].reshape(2, rank // groups, hidden)
    return (score_diff, gen_grad_in, grads_out[0], fake_grad_in, grads_out[1])


def solution(mesh):
    fine = Mesh(mesh.devices.reshape(4, 4, 2, 2, 2), AXES)
    dp, mp = ("z", "y", "xh"), ("xl", "core")
    return jax.shard_map(
        local,
        mesh=fine,
        in_specs=(
            P(AXES, None),
            P(AXES, None),
            P(),
            P(),
            P(dp, mp),
            P(mp, dp),
            P(),
            P(None, mp),
            P(),
            P(None, mp),
            P(),
            P(),
            P(),
        ),
        out_specs=(
            P(AXES, None),
            P(AXES, None),
            P(dp, mp),
            P(AXES, None),
            P(dp, mp),
        ),
        check_vma=False,
    )
```

```python
import math

import jax
import jax.numpy as jnp
from jax import lax
from jax.experimental import pallas as pl
from jax.experimental.pallas import tpu as pltpu
from jax.sharding import Mesh
from jax.sharding import PartitionSpec as P

IMG_TOK = 1024
AXES = ("z", "y", "xh", "xl", "core")
CHIPS = ("z", "y", "xh", "xl")

gelu_coef = 0.044715
root_two_pi = math.sqrt(2.0 / math.pi)


def gelu_value(pre):
    inner_arg = root_two_pi * (pre + gelu_coef * pre * pre * pre)
    return 0.5 * pre * (1.0 + jnp.tanh(inner_arg))


def gelu_slope(pre):
    tanh_val = jnp.tanh(root_two_pi * (pre + gelu_coef * pre * pre * pre))
    return 0.5 * (1.0 + tanh_val) + 0.5 * pre * (1.0 - tanh_val * tanh_val) * root_two_pi * (
        1.0 + 3.0 * gelu_coef * pre * pre
    )


def embedding(steps, feature_count):
    half_width = feature_count // 2
    frequency = jnp.exp(-math.log(10000.0) * jnp.arange(half_width, dtype=jnp.float32) / half_width)
    phase_angle = steps.astype(jnp.float32)[:, None] * frequency[None, :]
    return jnp.concatenate([jnp.sin(phase_angle), jnp.cos(phase_angle)], axis=1)


def modulate(rows, scale_rows, shift_rows):
    widened = rows.astype(jnp.float32)
    normed = widened * lax.rsqrt(jnp.mean(widened * widened, axis=1, keepdims=True) + 1e-06)
    return (normed * scale_rows + shift_rows).astype(jnp.bfloat16)


def matmul(left, right):
    return jnp.dot(left, right, preferred_element_type=jnp.float32)


def contract(left, right, left_dim, right_dim):
    return lax.dot_general(
        left, right, (((left_dim,), (right_dim,)), ((), ())), preferred_element_type=jnp.float32
    )


def swap_cores(value):
    return lax.ppermute(value, "core", [(0, 1), (1, 0)])


RING_AXES = (("y", "z", "x"), ("z", "x", "y"), ("x", "y", "z"))
RING = 4


def chip_ring(axis):
    pairs = []
    for device in range(128):
        place = {"z": device // 32, "y": device // 8 % 4, "x": device // 2 % 4, "core": device % 2}
        step = 1 if place["core"] == 0 else -1
        place[axis] = (place[axis] + step) % RING
        target = place["z"] * 32 + place["y"] * 8 + place["x"] * 2 + place["core"]
        pairs.append((device, target))
    return pairs


def ring_slots(pieces):
    for phase in range(3):
        slots = [[piece] for piece in pieces]
        for _ in range(RING - 1):
            for i, held in enumerate(slots):
                held.append(lax.ppermute(held[-1], AXES, chip_ring(RING_AXES[i][phase])))
        if phase < 2:
            pieces = [jnp.concatenate(held, axis=0) for held in slots]
    return slots


PIECE = 48
TILE = 256
SCOPED = 20 * 2**20
ANYWHERE = pl.BlockSpec(memory_space=pl.ANY)
IN_VMEM = pl.BlockSpec(memory_space=pltpu.VMEM)
IN_SMEM = pl.BlockSpec(memory_space=pltpu.SMEM)
NT = (((1,), (1,)), ((), ()))
TN = (((0,), (0,)), ((), ()))


def dot(left, right, dims=(((1,), (0,)), ((), ()))):
    return lax.dot_general(left, right, dims, preferred_element_type=jnp.float32)


def gelu_and_slope(pre):
    square = pre * pre
    tanh_val = jnp.tanh(root_two_pi * (pre + gelu_coef * square * pre))
    half = 0.5 * (1.0 + tanh_val)
    slope = half + 0.5 * pre * (1.0 - tanh_val * tanh_val) * root_two_pi * (
        1.0 + 3.0 * gelu_coef * square
    )
    return pre * half, slope


def start_slot(place_ref, i, step, slot, target, part, sem):
    me = {"z": place_ref[0], "y": place_ref[1], "x": place_ref[2]}
    direction = place_ref[3]
    first, second, third = RING_AXES[i]

    def source(axis, distance):
        return lax.rem(me[axis] - distance * direction + RING, RING)

    def one(k, carry):
        at = {
            first: source(first, lax.rem(k, RING)),
            second: source(second, lax.div(k, RING)),
            third: source(third, step),
        }
        quarter = lax.rem(at["x"], 2)
        group = (at["z"] * 4 + at["y"]) * 2 + lax.div(at["x"], 2)
        rows = pl.ds(pl.multiple_of(group * 2 * PIECE + part * PIECE, 16), PIECE)
        pltpu.make_async_copy(slot.at[k], target.at[quarter, rows], sem).start()
        return carry

    lax.fori_loop(0, 16, one, 0, unroll=4)


def wait_slot(slot, sem):
    pltpu.make_async_copy(slot, slot, sem).wait()


def load_body(place_ref, *refs):
    slots, (whole, up, down, sems) = refs[:9], refs[9:]
    targets = ((up, 0), (up, 1), (down, 0))
    for step in range(3):
        for i, (target, part) in enumerate(targets):
            n = step * 3 + i
            start_slot(place_ref, i, step, slots[n], target, part, sems.at[n])

    def one(group, carry):
        rows = pl.ds(pl.multiple_of(group * 2 * PIECE + PIECE, 16), PIECE)
        for quarter in range(2):
            pltpu.make_async_copy(
                whole.at[group, quarter], down.at[quarter, rows], sems.at[9]
            ).start()
        return carry

    lax.fori_loop(0, 32, one, 0, unroll=2)
    for n in range(9):
        wait_slot(slots[n], sems.at[n])
    wait_slot(whole, sems.at[9])


def weights_shape(width, hidden):
    return pltpu.VMEM((2, width, hidden), jnp.bfloat16)


def in_vmem(value):
    return pltpu.with_memory_space_constraint(value, pltpu.VMEM)


def load_weights(coords, slots, whole, width, hidden):
    flat = [slots[i][step].reshape(16, PIECE, hidden) for step in range(3) for i in range(3)]
    shape = weights_shape(width, hidden)
    return pl.pallas_call(
        load_body,
        out_shape=(shape, shape),
        in_specs=[IN_SMEM] + [ANYWHERE] * 10,
        out_specs=(IN_VMEM, IN_VMEM),
        scratch_shapes=[pltpu.SemaphoreType.DMA((10,))],
        compiler_params=pltpu.CompilerParams(vmem_limit_bytes=SCOPED),
        cost_estimate=pl.CostEstimate(
            flops=0, bytes_accessed=13 * 16 * PIECE * hidden * 4, transcendentals=0
        ),
        name="load_weights",
    )(coords, *flat, whole.reshape(32, 2, PIECE, hidden))


def gen_body(
    place_ref, u, low, adapt, slot_a, slot_b, slot_c, up_in, down_in, up, down, slope, mine, other, act, sems
):
    rows = mine.shape[0]
    start_slot(place_ref, 0, 3, slot_a, up, 0, sems.at[0])
    start_slot(place_ref, 1, 3, slot_b, up, 1, sems.at[1])
    start_slot(place_ref, 2, 3, slot_c, down, 0, sems.at[2])
    wait_slot(slot_a, sems.at[0])
    wait_slot(slot_b, sems.at[1])
    for q in range(2):

        def hidden_tile(n, carry, q=q):
            cols = pl.ds(pl.multiple_of(n * TILE, TILE), TILE)
            pre = dot(u[...], up[q, :, cols]) + dot(low[...], adapt[q, :, cols])
            value, slope[q, :, cols] = gelu_and_slope(pre)
            act[q, :, cols] = value.astype(act.dtype)
            return carry

        lax.fori_loop(0, up.shape[2] // TILE, hidden_tile, 0)
    wait_slot(slot_c, sems.at[2])

    def width_tile(n, carry):
        cols = pl.ds(pl.multiple_of(n * TILE, TILE), TILE)
        out = dot(act[0], down[0, cols, :], NT) + dot(act[1], down[1, cols, :], NT)
        mine[:, cols] = out[:rows]
        other[:, cols] = out[rows:].astype(other.dtype)
        return carry

    lax.fori_loop(0, down.shape[1] // TILE, width_tile, 0)


def gen_forward(coords, u, low, adapt, slots, up, down):
    group, width = u.shape
    hidden = up.shape[2]
    rows = group // 2
    shape = weights_shape(width, hidden)
    f32, bf16 = jnp.float32, jnp.bfloat16
    last = [slots[i][3].reshape(16, PIECE, hidden) for i in range(3)]
    return pl.pallas_call(
        gen_body,
        out_shape=(
            shape,
            shape,
            jax.ShapeDtypeStruct((2, group, hidden), f32),
            jax.ShapeDtypeStruct((rows, width), f32),
            jax.ShapeDtypeStruct((rows, width), bf16),
        ),
        in_specs=[IN_SMEM] + [IN_VMEM] * 3 + [ANYWHERE] * 3 + [IN_VMEM] * 2,
        out_specs=(IN_VMEM,) * 5,
        scratch_shapes=[pltpu.VMEM((2, group, hidden), bf16), pltpu.SemaphoreType.DMA((3,))],
        input_output_aliases={7: 0, 8: 1},
        compiler_params=pltpu.CompilerParams(vmem_limit_bytes=SCOPED),
        cost_estimate=pl.CostEstimate(
            flops=8 * group * width * hidden,
            bytes_accessed=10 * 2**20,
            transcendentals=2 * group * hidden,
        ),
        name="gen_forward",
    )(coords, u, low, adapt, *last, in_vmem(up), in_vmem(down))


def score_body(
    u_mine, u_other, adapt_in, adapt_out, up, down, slope, low_ref, real, fake, others, u, act
):
    rows = u_mine.shape[0]
    group = 2 * rows
    u[:rows] = u_mine[...]
    u[rows:] = u_other[...]
    low = dot(u[...], adapt_in[...]).astype(low_ref.dtype)
    low_ref[...] = low
    for q in range(2):

        def hidden_tile(n, carry, q=q):
            cols = pl.ds(pl.multiple_of(n * TILE, TILE), TILE)
            pre_real = dot(u[...], up[q, :, cols])
            pre_fake = pre_real + dot(low_ref[...], adapt_out[q, :, cols])
            act[q, :group, cols] = gelu_value(pre_real).astype(act.dtype)
            value, slope[q, :, cols] = gelu_and_slope(pre_fake)
            act[q, group:, cols] = value.astype(act.dtype)
            return carry

        lax.fori_loop(0, up.shape[2] // TILE, hidden_tile, 0)

    def width_tile(n, carry):
        cols = pl.ds(pl.multiple_of(n * TILE, TILE), TILE)
        out = dot(act[0], down[0, cols, :], NT) + dot(act[1], down[1, cols, :], NT)
        real[:, cols] = out[:rows]
        others[:rows, cols] = out[rows:group].astype(others.dtype)
        fake[:, cols] = out[group : group + rows]
        others[rows:, cols] = out[group + rows :].astype(others.dtype)
        return carry

    lax.fori_loop(0, down.shape[1] // TILE, width_tile, 0)


def score_forward(u_mine, u_other, adapt_in, adapt_out, up, down):
    rows, width = u_mine.shape
    hidden = up.shape[2]
    group = 2 * rows
    f32, bf16 = jnp.float32, jnp.bfloat16
    return pl.pallas_call(
        score_body,
        out_shape=(
            jax.ShapeDtypeStruct((2, group, hidden), f32),
            jax.ShapeDtypeStruct((group, adapt_in.shape[1]), bf16),
            jax.ShapeDtypeStruct((rows, width), f32),
            jax.ShapeDtypeStruct((rows, width), f32),
            jax.ShapeDtypeStruct((group, width), bf16),
        ),
        in_specs=[IN_VMEM] * 6,
        out_specs=(IN_VMEM,) * 5,
        scratch_shapes=[pltpu.VMEM((group, width), bf16), pltpu.VMEM((2, 2 * group, hidden), bf16)],
        compiler_params=pltpu.CompilerParams(vmem_limit_bytes=SCOPED),
        cost_estimate=pl.CostEstimate(
            flops=12 * group * width * hidden,
            bytes_accessed=10 * 2**20,
            transcendentals=4 * group * hidden,
        ),
        name="score_forward",
    )(u_mine, u_other, adapt_in, adapt_out, in_vmem(up), in_vmem(down))


def back_body(
    cots_mine, cots_other, slope_gen, slope_fake, low_gen, low_fake, gen_out, fake_out, down, grads, mix, cots
):
    group = cots_mine.shape[0]
    rows = group // 2
    for i in range(2):
        cots[i * group : i * group + rows] = cots_mine[i * rows : (i + 1) * rows]
        cots[i * group + rows : (i + 1) * group] = cots_other[i * rows : (i + 1) * rows]
    zero = jnp.zeros((group, low_gen.shape[1]), jnp.float32)
    mixed = (zero, zero)
    for q in range(2):

        def hidden_tile(n, carry, q=q):
            cols = pl.ds(pl.multiple_of(n * TILE, TILE), TILE)
            raw = dot(cots[...], down[q, :, cols])
            back_gen = (raw[:group] * slope_gen[q, :, cols]).astype(jnp.bfloat16)
            back_fake = (raw[group:] * slope_fake[q, :, cols]).astype(jnp.bfloat16)
            grads[0, q, :, cols] = dot(low_gen[...], back_gen, TN).astype(grads.dtype)
            grads[1, q, :, cols] = dot(low_fake[...], back_fake, TN).astype(grads.dtype)
            return (
                carry[0] + dot(back_gen, gen_out[q, :, cols], NT),
                carry[1] + dot(back_fake, fake_out[q, :, cols], NT),
            )

        mixed = lax.fori_loop(0, down.shape[2] // TILE, hidden_tile, mixed)
    mix[0] = mixed[0]
    mix[1] = mixed[1]


def backward(cots_mine, cots_other, slope_gen, slope_fake, low_gen, low_fake, gen_out, fake_out, down):
    group, width = cots_mine.shape
    hidden = down.shape[2]
    rank = low_gen.shape[1]
    f32, bf16 = jnp.float32, jnp.bfloat16
    return pl.pallas_call(
        back_body,
        out_shape=(
            jax.ShapeDtypeStruct((2, 2, rank, hidden), bf16),
            jax.ShapeDtypeStruct((2, group, rank), f32),
        ),
        in_specs=[IN_VMEM] * 9,
        out_specs=(IN_VMEM,) * 2,
        scratch_shapes=[pltpu.VMEM((2 * group, width), bf16)],
        compiler_params=pltpu.CompilerParams(vmem_limit_bytes=SCOPED),
        cost_estimate=pl.CostEstimate(
            flops=8 * group * width * hidden, bytes_accessed=10 * 2**20, transcendentals=0
        ),
        name="backward",
    )(cots_mine, cots_other, slope_gen, slope_fake, low_gen, low_fake, gen_out, fake_out, in_vmem(down))


def three_terms(value):
    high = lax.reduce_precision(value, 8, 7)
    rest = value - high
    middle = lax.reduce_precision(rest, 8, 7)
    low = rest - middle
    return jnp.concatenate([high, middle, low], axis=1).astype(jnp.bfloat16)


def local(
    gen_input,
    noise_score,
    gen_steps,
    score_steps,
    base_up,
    base_down,
    gen_adapt_in,
    gen_adapt_out,
    fake_adapt_in,
    fake_adapt_out,
    modulation_scale,
    modulation_shift,
    output_gate,
):
    bf16, f32 = jnp.bfloat16, jnp.float32
    shard_rows, width = gen_input.shape
    hidden = base_up.shape[1]
    rank = gen_adapt_in.shape[1]
    image_count = gen_steps.shape[0]
    loss_scale = 1.0 / math.sqrt(image_count * IMG_TOK)
    core = lax.axis_index("core")
    xl = lax.axis_index("xl")
    first_row = lax.axis_index(AXES) * shard_rows
    first_image = first_row // IMG_TOK
    last_image = (first_row + shard_rows - 1) // IMG_TOK
    row_ids = first_row + jnp.arange(shard_rows, dtype=jnp.int32)
    in_last = (row_ids >= last_image * IMG_TOK)[:, None]

    def two_steps(steps):
        return jnp.stack([steps[first_image], steps[last_image]])

    def modulation(steps):
        embed = embedding(two_steps(steps), width)
        scale = 1.0 + modulation_scale[None, :] * embed
        shift = modulation_shift[None, :] * embed
        return (
            jnp.where(in_last, scale[1:], scale[:1]),
            jnp.where(in_last, shift[1:], shift[:1]),
        )

    def both_rows(mine):
        return jnp.concatenate([mine, swap_cores(mine)], axis=0)

    coords = jnp.stack(
        [
            lax.axis_index("z"),
            lax.axis_index("y"),
            lax.axis_index("xh") * 2 + xl,
            1 - 2 * core,
        ]
    ).astype(jnp.int32)
    down_rows = base_down.T
    half = base_up.shape[0] // 2
    last_quarter = lax.all_gather(down_rows[half:], CHIPS, axis=0, tiled=True)
    slots = ring_slots([base_up[:half], base_up[half:], down_rows[:half]])
    up_part, down_part = load_weights(coords, slots, last_quarter, width, hidden)

    def other_quarter(mine):
        theirs = lax.ppermute(mine, "xl", [(0, 1), (1, 0)])
        return jnp.stack([jnp.where(xl == 0, mine, theirs), jnp.where(xl == 0, theirs, mine)])

    adapt_out = other_quarter(jnp.concatenate([gen_adapt_out, fake_adapt_out], axis=0))
    gen_out, fake_out = adapt_out[:, :rank], adapt_out[:, rank:]

    u_mine = modulate(gen_input, *modulation(gen_steps))
    u_gen = both_rows(u_mine)
    low_gen = matmul(u_gen, gen_adapt_in).astype(bf16)
    up_all, down_all, slope_gen, out_mine, out_other = gen_forward(
        coords, u_gen, low_gen, gen_out, slots, up_part, down_part
    )
    out_mine = out_mine + swap_cores(out_other).astype(f32)
    latents = (gen_input.astype(f32) + output_gate * out_mine).astype(bf16)
    two_blend = (two_steps(score_steps).astype(f32) + 0.5) / 1000.0
    blend = jnp.where(in_last, two_blend[1], two_blend[0])
    noised = ((1.0 - blend) * latents.astype(f32) + blend * noise_score.astype(f32)).astype(bf16)
    u_score = modulate(noised, *modulation(score_steps))
    u_score_other = swap_cores(u_score)
    slope_fake, low_fake, out_real, out_fake, outs_other = score_forward(
        u_score, u_score_other, fake_adapt_in, fake_out, up_all, down_all
    )
    got = swap_cores(outs_other).astype(f32)
    out_real = out_real + got[:shard_rows]
    out_fake = out_fake + got[shard_rows:]
    score_diff = (output_gate * (out_fake - out_real)).astype(bf16)
    cot_gen = (output_gate * score_diff.astype(f32) * loss_scale).astype(bf16)
    target = noise_score.astype(f32) - latents.astype(f32)
    cot_fake = (
        output_gate * (noised.astype(f32) + output_gate * out_fake - target) * loss_scale
    ).astype(bf16)
    cots = jnp.concatenate([cot_gen, cot_fake], axis=0)
    out_grads, mix = backward(
        cots, swap_cores(cots), slope_gen, slope_fake, low_gen, low_fake, gen_out, fake_out, down_all
    )
    mix = jnp.concatenate([mix[0], mix[1]], axis=1)
    mix_other = swap_cores(mix)
    mix = mix + jnp.concatenate([mix_other[shard_rows:], mix_other[:shard_rows]], axis=0)

    def in_grad(u, mix_part):
        product = contract(u, three_terms(mix_part), 0, 0)
        total = product[:, :rank] + product[:, rank : 2 * rank] + product[:, 2 * rank :]
        chips = total.reshape(-1, 2, width // 128, rank)
        return jnp.where(core == 0, chips[:, 0], chips[:, 1])

    u_score_group = jnp.concatenate([u_score, u_score_other], axis=0)
    in_grads = jnp.concatenate(
        [in_grad(u_gen, mix[:, :rank]), in_grad(u_score_group, mix[:, rank:])], axis=2
    )
    chips, in_rows = in_grads.shape[0], in_grads.shape[1]
    groups = chips // 2
    out_grads = out_grads.reshape(2, 2, groups, rank // groups, hidden).transpose(2, 1, 0, 3, 4)
    out_rows = 2 * (rank // groups) * hidden // 128
    packed = jnp.concatenate(
        [in_grads.astype(bf16), out_grads.reshape(chips, out_rows, 128)], axis=1
    )
    received = lax.all_to_all(packed, CHIPS, 0, 0, tiled=True)
    summed = jnp.sum(received.astype(f32), axis=0)
    gen_grad_in, fake_grad_in = summed[:in_rows, :rank], summed[:in_rows, rank:]
    grads_out = summed[in_rows:].reshape(2, rank // groups, hidden)
    return (score_diff, gen_grad_in, grads_out[0], fake_grad_in, grads_out[1])


def solution(mesh):
    fine = Mesh(mesh.devices.reshape(4, 4, 2, 2, 2), AXES)
    dp, mp = ("z", "y", "xh"), ("xl", "core")
    return jax.shard_map(
        local,
        mesh=fine,
        in_specs=(
            P(AXES, None),
            P(AXES, None),
            P(),
            P(),
            P(dp, mp),
            P(mp, dp),
            P(),
            P(None, mp),
            P(),
            P(None, mp),
            P(),
            P(),
            P(),
        ),
        out_specs=(
            P(AXES, None),
            P(AXES, None),
            P(dp, mp),
            P(AXES, None),
            P(dp, mp),
        ),
        check_vma=False,
    )
```

```python
import functools
import math

import jax
import jax.numpy as jnp
from jax import lax
from jax.experimental import pallas as pl
from jax.experimental.pallas import tpu as pltpu
from jax.sharding import Mesh
from jax.sharding import PartitionSpec as P

IMG_TOK = 1024
AXES = ("z", "y", "xh", "xl", "core")
CHIPS = ("z", "y", "xh", "xl")

gelu_coef = 0.044715
root_two_pi = math.sqrt(2.0 / math.pi)


def gelu_value(pre):
    inner_arg = root_two_pi * (pre + gelu_coef * pre * pre * pre)
    return 0.5 * pre * (1.0 + jnp.tanh(inner_arg))


def gelu_slope(pre):
    tanh_val = jnp.tanh(root_two_pi * (pre + gelu_coef * pre * pre * pre))
    return 0.5 * (1.0 + tanh_val) + 0.5 * pre * (1.0 - tanh_val * tanh_val) * root_two_pi * (
        1.0 + 3.0 * gelu_coef * pre * pre
    )


def embedding(steps, feature_count):
    half_width = feature_count // 2
    frequency = jnp.exp(-math.log(10000.0) * jnp.arange(half_width, dtype=jnp.float32) / half_width)
    phase_angle = steps.astype(jnp.float32)[:, None] * frequency[None, :]
    return jnp.concatenate([jnp.sin(phase_angle), jnp.cos(phase_angle)], axis=1)


def modulate(rows, scale_rows, shift_rows):
    widened = rows.astype(jnp.float32)
    normed = widened * lax.rsqrt(jnp.mean(widened * widened, axis=1, keepdims=True) + 1e-06)
    return (normed * scale_rows + shift_rows).astype(jnp.bfloat16)


def matmul(left, right):
    return jnp.dot(left, right, preferred_element_type=jnp.float32)


def contract(left, right, left_dim, right_dim):
    return lax.dot_general(
        left, right, (((left_dim,), (right_dim,)), ((), ())), preferred_element_type=jnp.float32
    )


def swap_cores(value):
    return lax.ppermute(value, "core", [(0, 1), (1, 0)])


RING_AXES = (("y", "z", "x"), ("z", "x", "y"), ("x", "y", "z"))
RING = 4


def chip_ring(axis):
    pairs = []
    for device in range(128):
        place = {"z": device // 32, "y": device // 8 % 4, "x": device // 2 % 4, "core": device % 2}
        step = 1 if place["core"] == 0 else -1
        place[axis] = (place[axis] + step) % RING
        target = place["z"] * 32 + place["y"] * 8 + place["x"] * 2 + place["core"]
        pairs.append((device, target))
    return pairs


def ring(pieces, phase):
    slots = [[piece] for piece in pieces]
    for _ in range(RING - 1):
        for i, held in enumerate(slots):
            held.append(lax.ppermute(held[-1], AXES, chip_ring(RING_AXES[i][phase])))
    return slots


def ring_slots(pieces, early, middle):
    slots = ring([jnp.concatenate(held, axis=0) for held in ring(pieces, 0)], 1)
    halves = [[jnp.concatenate(held[2 * h : 2 * h + 2], axis=0) for held in slots] for h in range(2)]
    halves[0], early = lax.optimization_barrier((halves[0], early))
    found = [[[piece] for piece in half] for half in halves]
    for step in range(1, RING):
        for h in range(2):
            for i in range(3):
                found[h][i].append(lax.ppermute(found[h][i][-1], AXES, chip_ring(RING_AXES[i][2])))
        if step == RING - 2:
            held = [found[0][i][-1] for i in range(3)]
            held, middle = lax.optimization_barrier((held, middle))
            for i in range(3):
                found[0][i][-1] = held[i]
    return found, early, middle


PIECE = 48
TILE = 256
MIB = 2**20
ANYWHERE = pl.BlockSpec(memory_space=pl.ANY)
IN_VMEM = pl.BlockSpec(memory_space=pltpu.VMEM)
IN_SMEM = pl.BlockSpec(memory_space=pltpu.SMEM)
NT = (((1,), (1,)), ((), ()))
TN = (((0,), (0,)), ((), ()))


def dot(left, right, dims=(((1,), (0,)), ((), ()))):
    return lax.dot_general(left, right, dims, preferred_element_type=jnp.float32)


def gelu_and_slope(pre):
    square = pre * pre
    tanh_val = jnp.tanh(root_two_pi * (pre + gelu_coef * square * pre))
    half = 0.5 * (1.0 + tanh_val)
    slope = half + 0.5 * pre * (1.0 - tanh_val * tanh_val) * root_two_pi * (
        1.0 + 3.0 * gelu_coef * square
    )
    return pre * half, slope


def start_slot(place_ref, half, i, step, slot, target, part, sem):
    me = {"z": place_ref[0], "y": place_ref[1], "x": place_ref[2]}
    direction = place_ref[3]
    first, second, third = RING_AXES[i]

    def source(axis, distance):
        return lax.rem(me[axis] - distance * direction + RING, RING)

    def one(k, carry):
        at = {
            first: source(first, lax.rem(k, RING)),
            second: source(second, 2 * half + lax.div(k, RING)),
            third: source(third, step),
        }
        quarter = lax.rem(at["x"], 2)
        group = (at["z"] * 4 + at["y"]) * 2 + lax.div(at["x"], 2)
        rows = pl.ds(pl.multiple_of(group * 2 * PIECE + part * PIECE, 16), PIECE)
        pltpu.make_async_copy(slot.at[k], target.at[quarter, rows], sem).start()
        return carry

    lax.fori_loop(0, 2 * RING, one, 0, unroll=4)


def wait_slot(slot, sem):
    pltpu.make_async_copy(slot, slot, sem).wait()


def load_body(place_ref, *refs):
    slots, (whole, up, down, sems) = refs[:18], refs[18:]
    targets = ((up, 0), (up, 1), (down, 0))
    for n, slot in enumerate(slots):
        step, half, i = n // 6, n // 3 % 2, n % 3
        target, part = targets[i]
        start_slot(place_ref, half, i, step, slot, target, part, sems.at[n])

    def one(group, carry):
        rows = pl.ds(pl.multiple_of(group * 2 * PIECE + PIECE, 16), PIECE)
        for quarter in range(2):
            pltpu.make_async_copy(
                whole.at[group, quarter], down.at[quarter, rows], sems.at[18]
            ).start()
        return carry

    lax.fori_loop(0, 32, one, 0, unroll=2)
    for n, slot in enumerate(slots):
        wait_slot(slot, sems.at[n])
    wait_slot(whole, sems.at[18])


def weights_shape(width, hidden):
    return pltpu.VMEM((2, width, hidden), jnp.bfloat16)


def in_vmem(value):
    return pltpu.with_memory_space_constraint(value, pltpu.VMEM)


def load_weights(coords, slots, whole, width, hidden):
    flat = [
        slots[half][i][step].reshape(2 * RING, PIECE, hidden)
        for step in range(3)
        for half in range(2)
        for i in range(3)
    ]
    shape = weights_shape(width, hidden)
    return pl.pallas_call(
        load_body,
        out_shape=(shape, shape),
        in_specs=[IN_SMEM] + [ANYWHERE] * 19,
        out_specs=(IN_VMEM, IN_VMEM),
        scratch_shapes=[pltpu.SemaphoreType.DMA((19,))],
        compiler_params=pltpu.CompilerParams(vmem_limit_bytes=4 * MIB),
        cost_estimate=pl.CostEstimate(
            flops=0, bytes_accessed=13 * 16 * PIECE * hidden * 4, transcendentals=0
        ),
        name="load_weights",
    )(coords, *flat, whole.reshape(32, 2, PIECE, hidden))


def gen_body(place_ref, u, low, adapt, *refs):
    slots, (_, _, up, down, slope, mine, other, act, sems) = refs[:6], refs[6:]
    rows = mine.shape[0]
    targets = ((up, 0), (up, 1), (down, 0))
    for i, (target, part) in enumerate(targets):
        for half in range(2):
            n = 2 * i + half
            start_slot(place_ref, half, i, 3, slots[n], target, part, sems.at[n])
    for n in range(4):
        wait_slot(slots[n], sems.at[n])
    for q in range(2):

        def hidden_tile(n, carry, q=q):
            cols = pl.ds(pl.multiple_of(n * TILE, TILE), TILE)
            pre = dot(u[...], up[q, :, cols]) + dot(low[...], adapt[q, :, cols])
            value, slope[q, :, cols] = gelu_and_slope(pre)
            act[q, :, cols] = value.astype(act.dtype)
            return carry

        lax.fori_loop(0, up.shape[2] // TILE, hidden_tile, 0)
    for n in range(4, 6):
        wait_slot(slots[n], sems.at[n])

    def width_tile(n, carry):
        cols = pl.ds(pl.multiple_of(n * TILE, TILE), TILE)
        out = dot(act[0], down[0, cols, :], NT) + dot(act[1], down[1, cols, :], NT)
        mine[:, cols] = out[:rows]
        other[:, cols] = out[rows:].astype(other.dtype)
        return carry

    lax.fori_loop(0, down.shape[1] // TILE, width_tile, 0)


def gen_forward(coords, u, low, adapt, slots, up, down):
    group, width = u.shape
    hidden = up.shape[2]
    rows = group // 2
    shape = weights_shape(width, hidden)
    f32, bf16 = jnp.float32, jnp.bfloat16
    last = [
        slots[half][i][3].reshape(2 * RING, PIECE, hidden) for i in range(3) for half in range(2)
    ]
    return pl.pallas_call(
        gen_body,
        out_shape=(
            shape,
            shape,
            jax.ShapeDtypeStruct((2, group, hidden), f32),
            jax.ShapeDtypeStruct((rows, width), f32),
            jax.ShapeDtypeStruct((rows, width), bf16),
        ),
        in_specs=[IN_SMEM] + [IN_VMEM] * 3 + [ANYWHERE] * 6 + [IN_VMEM] * 2,
        out_specs=(IN_VMEM,) * 5,
        scratch_shapes=[pltpu.VMEM((2, group, hidden), bf16), pltpu.SemaphoreType.DMA((6,))],
        input_output_aliases={10: 0, 11: 1},
        compiler_params=pltpu.CompilerParams(vmem_limit_bytes=12 * MIB),
        cost_estimate=pl.CostEstimate(
            flops=8 * group * width * hidden,
            bytes_accessed=10 * 2**20,
            transcendentals=2 * group * hidden,
        ),
        name="gen_forward",
    )(coords, u, low, adapt, *last, in_vmem(up), in_vmem(down))


def score_body(
    u_mine, u_other, adapt_in, adapt_out, up, down, slope, low_ref, real, fake, others, u, act
):
    rows = u_mine.shape[0]
    group = 2 * rows
    u[:rows] = u_mine[...]
    u[rows:] = u_other[...]
    low_ref[...] = dot(u[...], adapt_in[...], NT).astype(low_ref.dtype)
    for q in range(2):

        def hidden_tile(n, carry, q=q):
            cols = pl.ds(pl.multiple_of(n * TILE, TILE), TILE)
            pre_real = dot(u[...], up[q, :, cols])
            pre_fake = pre_real + dot(low_ref[...], adapt_out[q, :, cols])
            act[q, :group, cols] = gelu_value(pre_real).astype(act.dtype)
            value, slope[q, :, cols] = gelu_and_slope(pre_fake)
            act[q, group:, cols] = value.astype(act.dtype)
            return carry

        lax.fori_loop(0, up.shape[2] // TILE, hidden_tile, 0)

    def width_tile(n, carry):
        cols = pl.ds(pl.multiple_of(n * TILE, TILE), TILE)
        out = dot(act[0], down[0, cols, :], NT) + dot(act[1], down[1, cols, :], NT)
        real[:, cols] = out[:rows]
        others[:rows, cols] = out[rows:group].astype(others.dtype)
        fake[:, cols] = out[group : group + rows]
        others[rows:, cols] = out[group + rows :].astype(others.dtype)
        return carry

    lax.fori_loop(0, down.shape[1] // TILE, width_tile, 0)


def score_forward(u_mine, u_other, adapt_in, adapt_out, up, down):
    rows, width = u_mine.shape
    hidden = up.shape[2]
    group = 2 * rows
    f32, bf16 = jnp.float32, jnp.bfloat16
    return pl.pallas_call(
        score_body,
        out_shape=(
            jax.ShapeDtypeStruct((2, group, hidden), f32),
            jax.ShapeDtypeStruct((group, adapt_in.shape[0]), bf16),
            jax.ShapeDtypeStruct((rows, width), f32),
            jax.ShapeDtypeStruct((rows, width), f32),
            jax.ShapeDtypeStruct((group, width), bf16),
        ),
        in_specs=[IN_VMEM] * 6,
        out_specs=(IN_VMEM,) * 5,
        scratch_shapes=[pltpu.VMEM((group, width), bf16), pltpu.VMEM((2, 2 * group, hidden), bf16)],
        compiler_params=pltpu.CompilerParams(vmem_limit_bytes=16 * MIB),
        cost_estimate=pl.CostEstimate(
            flops=12 * group * width * hidden,
            bytes_accessed=10 * 2**20,
            transcendentals=4 * group * hidden,
        ),
        name="score_forward",
    )(u_mine, u_other, adapt_in, adapt_out, in_vmem(up), in_vmem(down))


def back_body(
    cots_mine, cots_other, slope_gen, slope_fake, low_gen, low_fake, gen_out, fake_out, down, grads, mix, cots
):
    group = cots_mine.shape[0]
    rows = group // 2
    for i in range(2):
        cots[i * group : i * group + rows] = cots_mine[i * rows : (i + 1) * rows]
        cots[i * group + rows : (i + 1) * group] = cots_other[i * rows : (i + 1) * rows]
    zero = jnp.zeros((group, low_gen.shape[1]), jnp.float32)
    mixed = (zero, zero)
    for q in range(2):

        def hidden_tile(n, carry, q=q):
            cols = pl.ds(pl.multiple_of(n * TILE, TILE), TILE)
            raw = dot(cots[...], down[q, :, cols])
            back_gen = (raw[:group] * slope_gen[q, :, cols]).astype(jnp.bfloat16)
            back_fake = (raw[group:] * slope_fake[q, :, cols]).astype(jnp.bfloat16)
            grads[0, q, :, cols] = dot(low_gen[...], back_gen, TN).astype(grads.dtype)
            grads[1, q, :, cols] = dot(low_fake[...], back_fake, TN).astype(grads.dtype)
            return (
                carry[0] + dot(back_gen, gen_out[q, :, cols], NT),
                carry[1] + dot(back_fake, fake_out[q, :, cols], NT),
            )

        mixed = lax.fori_loop(0, down.shape[2] // TILE, hidden_tile, mixed)
    mix[0] = mixed[0]
    mix[1] = mixed[1]


def backward(cots_mine, cots_other, slope_gen, slope_fake, low_gen, low_fake, gen_out, fake_out, down):
    group, width = cots_mine.shape
    hidden = down.shape[2]
    rank = low_gen.shape[1]
    f32, bf16 = jnp.float32, jnp.bfloat16
    return pl.pallas_call(
        back_body,
        out_shape=(
            jax.ShapeDtypeStruct((2, 2, rank, hidden), bf16),
            jax.ShapeDtypeStruct((2, group, rank), f32),
        ),
        in_specs=[IN_VMEM] * 9,
        out_specs=(IN_VMEM,) * 2,
        scratch_shapes=[pltpu.VMEM((2 * group, width), bf16)],
        compiler_params=pltpu.CompilerParams(vmem_limit_bytes=16 * MIB),
        cost_estimate=pl.CostEstimate(
            flops=8 * group * width * hidden, bytes_accessed=10 * 2**20, transcendentals=0
        ),
        name="backward",
    )(cots_mine, cots_other, slope_gen, slope_fake, low_gen, low_fake, gen_out, fake_out, in_vmem(down))


STRIP = 16


def noise_body(ends, blends, given, noise, mine, other, mods, gate, latents_ref, noised_ref, u_ref):
    f32 = jnp.float32

    def strip(n, carry):
        rows = pl.ds(pl.multiple_of(n * STRIP, STRIP), STRIP)
        in_last = n * STRIP + lax.broadcasted_iota(jnp.int32, (STRIP, 1), 0) >= ends[0]
        out = mine[rows] + other[rows].astype(f32)
        latents = (given[rows].astype(f32) + gate[...] * out).astype(latents_ref.dtype)
        latents_ref[rows] = latents
        blend = jnp.where(in_last, blends[1], blends[0])
        noised = (
            (1.0 - blend) * latents.astype(f32) + blend * noise[rows].astype(f32)
        ).astype(noised_ref.dtype)
        noised_ref[rows] = noised
        scale = jnp.where(in_last, mods[1:2], mods[0:1])
        shift = jnp.where(in_last, mods[3:4], mods[2:3])
        u_ref[rows] = modulate(noised, scale, shift)
        return carry

    lax.fori_loop(0, given.shape[0] // STRIP, strip, 0)


def add_noise(ends, blends, given, noise, mine, other, mods, gate):
    shape = jax.ShapeDtypeStruct(given.shape, given.dtype)
    return pl.pallas_call(
        noise_body,
        out_shape=(shape,) * 3,
        in_specs=[IN_SMEM] * 2 + [IN_VMEM] * 6,
        out_specs=(IN_VMEM,) * 3,
        compiler_params=pltpu.CompilerParams(vmem_limit_bytes=10 * MIB),
        cost_estimate=pl.CostEstimate(flops=0, bytes_accessed=6 * MIB, transcendentals=0),
        name="add_noise",
    )(ends, blends, given, noise, mine, other, mods, gate)


def cotangent_body(scale, real, fake, others, gate_ref, noise, latents, noised, diff_ref, cots):
    f32 = jnp.float32
    count = real.shape[0]

    def strip(n, carry):
        start = pl.multiple_of(n * STRIP, STRIP)
        rows, second = pl.ds(start, STRIP), pl.ds(count + start, STRIP)
        gate = gate_ref[...]
        out_real = real[rows] + others[rows].astype(f32)
        out_fake = fake[rows] + others[second].astype(f32)
        diff = (gate * (out_fake - out_real)).astype(diff_ref.dtype)
        diff_ref[rows] = diff
        cots[rows] = (gate * diff.astype(f32) * scale).astype(cots.dtype)
        target = noise[rows].astype(f32) - latents[rows].astype(f32)
        cots[second] = (
            gate * (noised[rows].astype(f32) + gate * out_fake - target) * scale
        ).astype(cots.dtype)
        return carry

    lax.fori_loop(0, count // STRIP, strip, 0)


def cotangents(scale, real, fake, others, gate, noise, latents, noised):
    rows, width = real.shape
    return pl.pallas_call(
        functools.partial(cotangent_body, scale),
        out_shape=(
            jax.ShapeDtypeStruct((rows, width), noise.dtype),
            jax.ShapeDtypeStruct((2 * rows, width), noise.dtype),
        ),
        in_specs=[IN_VMEM] * 7,
        out_specs=(IN_VMEM,) * 2,
        compiler_params=pltpu.CompilerParams(vmem_limit_bytes=12 * MIB),
        cost_estimate=pl.CostEstimate(flops=0, bytes_accessed=8 * MIB, transcendentals=0),
        name="cotangents",
    )(real, fake, others, gate, noise, latents, noised)


def three_terms(value):
    high = lax.reduce_precision(value, 8, 7)
    rest = value - high
    middle = lax.reduce_precision(rest, 8, 7)
    low = rest - middle
    return jnp.concatenate([high, middle, low], axis=1).astype(jnp.bfloat16)


def local(
    gen_input,
    noise_score,
    gen_steps,
    score_steps,
    base_up,
    base_down,
    gen_adapt_in,
    gen_adapt_out,
    fake_adapt_in,
    fake_adapt_out,
    modulation_scale,
    modulation_shift,
    output_gate,
):
    bf16, f32 = jnp.bfloat16, jnp.float32
    shard_rows, width = gen_input.shape
    hidden = base_up.shape[1]
    rank = gen_adapt_in.shape[1]
    image_count = gen_steps.shape[0]
    loss_scale = 1.0 / math.sqrt(image_count * IMG_TOK)
    core = lax.axis_index("core")
    xl = lax.axis_index("xl")
    first_row = lax.axis_index(AXES) * shard_rows
    first_image = first_row // IMG_TOK
    last_image = (first_row + shard_rows - 1) // IMG_TOK
    row_ids = first_row + jnp.arange(shard_rows, dtype=jnp.int32)
    in_last = (row_ids >= last_image * IMG_TOK)[:, None]

    def two_steps(steps):
        return jnp.stack([steps[first_image], steps[last_image]])

    def modulation(steps):
        embed = embedding(two_steps(steps), width)
        return 1.0 + modulation_scale[None, :] * embed, modulation_shift[None, :] * embed

    def both_rows(mine):
        return jnp.concatenate([mine, swap_cores(mine)], axis=0)

    coords = jnp.stack(
        [
            lax.axis_index("z"),
            lax.axis_index("y"),
            lax.axis_index("xh") * 2 + xl,
            1 - 2 * core,
        ]
    ).astype(jnp.int32)
    down_rows = base_down.T
    half = base_up.shape[0] // 2
    last_quarter = lax.all_gather(down_rows[half:], CHIPS, axis=0, tiled=True)
    def other_quarter(mine):
        theirs = lax.ppermute(mine, "xl", [(0, 1), (1, 0)])
        return jnp.stack([jnp.where(xl == 0, mine, theirs), jnp.where(xl == 0, theirs, mine)])

    adapt_out = other_quarter(jnp.concatenate([gen_adapt_out, fake_adapt_out], axis=0))
    gen_scale, gen_shift = modulation(gen_steps)
    u_mine = modulate(
        gen_input,
        jnp.where(in_last, gen_scale[1:], gen_scale[:1]),
        jnp.where(in_last, gen_shift[1:], gen_shift[:1]),
    )
    u_gen = both_rows(u_mine)
    low_gen = matmul(u_gen, gen_adapt_in).astype(bf16)
    mods = jnp.concatenate(modulation(score_steps), axis=0)
    blends = (two_steps(score_steps).astype(f32) + 0.5) / 1000.0
    ends = (last_image * IMG_TOK - first_row).astype(jnp.int32).reshape(1)
    slots, adapt_out, prepared = ring_slots(
        [base_up[:half], base_up[half:], down_rows[:half]],
        adapt_out,
        (u_gen, low_gen, mods, blends, ends, coords),
    )
    u_gen, low_gen, mods, blends, ends, coords = prepared
    gen_out, fake_out = adapt_out[:, :rank], adapt_out[:, rank:]
    up_part, down_part = load_weights(coords, slots, last_quarter, width, hidden)

    up_all, down_all, slope_gen, out_mine, out_other = gen_forward(
        coords, u_gen, low_gen, gen_out, slots, up_part, down_part
    )
    gate = output_gate.reshape(1, width)
    latents, noised, u_score = add_noise(
        ends, blends, gen_input, noise_score, out_mine, swap_cores(out_other), mods, gate
    )
    u_score_other = swap_cores(u_score)
    slope_fake, low_fake, out_real, out_fake, outs_other = score_forward(
        u_score, u_score_other, fake_adapt_in.T, fake_out, up_all, down_all
    )
    score_diff, cots = cotangents(
        loss_scale, out_real, out_fake, swap_cores(outs_other), gate, noise_score, latents, noised
    )
    out_grads, mix = backward(
        cots, swap_cores(cots), slope_gen, slope_fake, low_gen, low_fake, gen_out, fake_out, down_all
    )
    mix = jnp.concatenate([mix[0], mix[1]], axis=1)
    mix_other = swap_cores(mix)
    mix = mix + jnp.concatenate([mix_other[shard_rows:], mix_other[:shard_rows]], axis=0)

    def in_grad(u, mix_part):
        product = contract(u, three_terms(mix_part), 0, 0)
        total = product[:, :rank] + product[:, rank : 2 * rank] + product[:, 2 * rank :]
        chips = total.reshape(-1, 2, width // 128, rank)
        return jnp.where(core == 0, chips[:, 0], chips[:, 1])

    u_score_group = jnp.concatenate([u_score, u_score_other], axis=0)
    in_grads = jnp.concatenate(
        [in_grad(u_gen, mix[:, :rank]), in_grad(u_score_group, mix[:, rank:])], axis=2
    )
    chips, in_rows = in_grads.shape[0], in_grads.shape[1]
    groups = chips // 2
    out_grads = out_grads.reshape(2, 2, groups, rank // groups, hidden).transpose(2, 1, 0, 3, 4)
    out_rows = 2 * (rank // groups) * hidden // 128
    packed = jnp.concatenate(
        [in_grads.astype(bf16), out_grads.reshape(chips, out_rows, 128)], axis=1
    )
    received = lax.all_to_all(packed, CHIPS, 0, 0, tiled=True)
    summed = jnp.sum(received.astype(f32), axis=0)
    gen_grad_in, fake_grad_in = summed[:in_rows, :rank], summed[:in_rows, rank:]
    grads_out = summed[in_rows:].reshape(2, rank // groups, hidden)
    return (score_diff, gen_grad_in, grads_out[0], fake_grad_in, grads_out[1])


def solution(mesh):
    fine = Mesh(mesh.devices.reshape(4, 4, 2, 2, 2), AXES)
    dp, mp = ("z", "y", "xh"), ("xl", "core")
    return jax.shard_map(
        local,
        mesh=fine,
        in_specs=(
            P(AXES, None),
            P(AXES, None),
            P(),
            P(),
            P(dp, mp),
            P(mp, dp),
            P(),
            P(None, mp),
            P(),
            P(None, mp),
            P(),
            P(),
            P(),
        ),
        out_specs=(
            P(AXES, None),
            P(AXES, None),
            P(dp, mp),
            P(AXES, None),
            P(dp, mp),
        ),
        check_vma=False,
    )
```

```python
import functools
import math

import jax
import jax.numpy as jnp
from jax import lax
from jax.experimental import pallas as pl
from jax.experimental.pallas import tpu as pltpu
from jax.sharding import Mesh
from jax.sharding import PartitionSpec as P

IMG_TOK = 1024
AXES = ("z", "y", "xh", "xl", "core")
CHIPS = ("z", "y", "xh", "xl")

gelu_coef = 0.044715
root_two_pi = math.sqrt(2.0 / math.pi)


def gelu_value(pre):
    inner_arg = root_two_pi * (pre + gelu_coef * pre * pre * pre)
    return 0.5 * pre * (1.0 + jnp.tanh(inner_arg))


def gelu_slope(pre):
    tanh_val = jnp.tanh(root_two_pi * (pre + gelu_coef * pre * pre * pre))
    return 0.5 * (1.0 + tanh_val) + 0.5 * pre * (1.0 - tanh_val * tanh_val) * root_two_pi * (
        1.0 + 3.0 * gelu_coef * pre * pre
    )


def embedding(steps, feature_count):
    half_width = feature_count // 2
    frequency = jnp.exp(-math.log(10000.0) * jnp.arange(half_width, dtype=jnp.float32) / half_width)
    phase_angle = steps.astype(jnp.float32)[:, None] * frequency[None, :]
    return jnp.concatenate([jnp.sin(phase_angle), jnp.cos(phase_angle)], axis=1)


def modulate(rows, scale_rows, shift_rows):
    widened = rows.astype(jnp.float32)
    normed = widened * lax.rsqrt(jnp.mean(widened * widened, axis=1, keepdims=True) + 1e-06)
    return (normed * scale_rows + shift_rows).astype(jnp.bfloat16)


def matmul(left, right):
    return jnp.dot(left, right, preferred_element_type=jnp.float32)


def contract(left, right, left_dim, right_dim):
    return lax.dot_general(
        left, right, (((left_dim,), (right_dim,)), ((), ())), preferred_element_type=jnp.float32
    )


def swap_cores(value):
    return lax.ppermute(value, "core", [(0, 1), (1, 0)])


RING_AXES = (("y", "z", "x"), ("z", "x", "y"), ("x", "y", "z"))
RING = 4


def chip_ring(axis):
    pairs = []
    for device in range(128):
        place = {"z": device // 32, "y": device // 8 % 4, "x": device // 2 % 4, "core": device % 2}
        step = 1 if place["core"] == 0 else -1
        place[axis] = (place[axis] + step) % RING
        target = place["z"] * 32 + place["y"] * 8 + place["x"] * 2 + place["core"]
        pairs.append((device, target))
    return pairs


def ring(pieces, phase):
    slots = [[piece] for piece in pieces]
    for _ in range(RING - 1):
        for i, held in enumerate(slots):
            held.append(lax.ppermute(held[-1], AXES, chip_ring(RING_AXES[i][phase])))
    return slots


def ring_slots(pieces, early, middle):
    for phase in range(2):
        pieces = [jnp.concatenate(held, axis=0) for held in ring(pieces, phase)]
    pieces, early = lax.optimization_barrier((pieces, early))
    slots = [[piece] for piece in pieces]
    for step in range(1, RING):
        if step == RING - 1:
            held = [slots[i][-1] for i in range(3)]
            held, middle = lax.optimization_barrier((held, middle))
            slots = [slots[i][:-1] + [held[i]] for i in range(3)]
        for i in range(3):
            slots[i].append(lax.ppermute(slots[i][-1], AXES, chip_ring(RING_AXES[i][2])))
    return slots, early, middle


PIECE = 48
TILE = 256
MIB = 2**20
ANYWHERE = pl.BlockSpec(memory_space=pl.ANY)
IN_VMEM = pl.BlockSpec(memory_space=pltpu.VMEM)
IN_SMEM = pl.BlockSpec(memory_space=pltpu.SMEM)
NT = (((1,), (1,)), ((), ()))
TN = (((0,), (0,)), ((), ()))


def dot(left, right, dims=(((1,), (0,)), ((), ()))):
    return lax.dot_general(left, right, dims, preferred_element_type=jnp.float32)


def gelu_and_slope(pre):
    square = pre * pre
    tanh_val = jnp.tanh(root_two_pi * (pre + gelu_coef * square * pre))
    half = 0.5 * (1.0 + tanh_val)
    slope = half + 0.5 * pre * (1.0 - tanh_val * tanh_val) * root_two_pi * (
        1.0 + 3.0 * gelu_coef * square
    )
    return pre * half, slope


IN_HBM = pl.BlockSpec(memory_space=pltpu.HBM)
CHUNK = 512


def piece_place(place_ref, i, step, k):
    me = {"z": place_ref[0], "y": place_ref[1], "x": place_ref[2]}
    direction = place_ref[3]
    first, second, third = RING_AXES[i]

    def source(axis, distance):
        return lax.rem(me[axis] - distance * direction + RING, RING)

    at = {
        first: source(first, lax.rem(k, RING)),
        second: source(second, lax.div(k, RING)),
        third: source(third, step),
    }
    group = (at["z"] * 4 + at["y"]) * 2 + lax.div(at["x"], 2)
    row = group * 2 * PIECE + (PIECE if i == 1 else 0)
    return lax.rem(at["x"], 2), pl.multiple_of(row, 16)


def each_piece(one):
    def step(k, carry):
        one(k)
        return carry

    lax.fori_loop(0, RING * RING, step, 0, unroll=4)


def wait_all(ref, sem):
    pltpu.make_async_copy(ref, ref, sem).wait()


def load_body(place_ref, *refs):
    slots, (whole, up_out, down_out, up, down, sems) = refs[:9], refs[9:]
    targets = (up, up, down)
    for n, slot in enumerate(slots):
        step, i = n // 3, n % 3

        def one(k, slot=slot, step=step, i=i, n=n):
            quarter, row = piece_place(place_ref, i, step, k)
            pltpu.make_async_copy(
                slot.at[k], targets[i].at[quarter, pl.ds(row, PIECE)], sems.at[n]
            ).start()

        each_piece(one)

    def one_group(group, carry):
        rows = pl.ds(pl.multiple_of(group * 2 * PIECE + PIECE, 16), PIECE)
        for quarter in range(2):
            pltpu.make_async_copy(whole.at[group, quarter], down.at[quarter, rows], sems.at[9]).start()
        return carry

    lax.fori_loop(0, whole.shape[0], one_group, 0, unroll=2)
    for i in (0, 1):
        for step in range(3):
            wait_all(slots[3 * step + i], sems.at[3 * step + i])
    up_copy = pltpu.make_async_copy(up, up_out, sems.at[10])
    up_copy.start()
    for step in range(3):
        wait_all(slots[3 * step + 2], sems.at[3 * step + 2])
    wait_all(whole, sems.at[9])
    down_copy = pltpu.make_async_copy(down, down_out, sems.at[11])
    down_copy.start()
    up_copy.wait()
    down_copy.wait()


def load_weights(coords, slots, whole, width, hidden):
    flat = [slots[i][step].reshape(RING * RING, PIECE, hidden) for step in range(3) for i in range(3)]
    shape = jax.ShapeDtypeStruct((2, width, hidden), jnp.bfloat16)
    return pl.pallas_call(
        load_body,
        out_shape=(shape, shape),
        in_specs=[IN_SMEM] + [ANYWHERE] * 10,
        out_specs=(IN_HBM, IN_HBM),
        scratch_shapes=[
            pltpu.VMEM(shape.shape, shape.dtype),
            pltpu.VMEM(shape.shape, shape.dtype),
            pltpu.SemaphoreType.DMA((12,)),
        ],
        compiler_params=pltpu.CompilerParams(vmem_limit_bytes=40 * MIB),
        cost_estimate=pl.CostEstimate(
            flops=0, bytes_accessed=8 * width * hidden * 4, transcendentals=0
        ),
        name="load_weights",
    )(coords, *flat, whole.reshape(32, 2, PIECE, hidden))


def start_by_columns(source, target, sems):
    per_quarter = target.shape[2] // CHUNK
    copies = []
    for n in range(2 * per_quarter):
        at = (n // per_quarter, slice(None), pl.ds(n % per_quarter * CHUNK, CHUNK))
        copies.append(pltpu.make_async_copy(source.at[at], target.at[at], sems.at[n]))
        copies[-1].start()
    return copies


def start_by_rows(source, target, sems):
    copies = []
    for n in range(target.shape[1] // CHUNK):
        at = (slice(None), pl.ds(n * CHUNK, CHUNK))
        copies.append(pltpu.make_async_copy(source.at[at], target.at[at], sems.at[n]))
        copies[-1].start()
    return copies


def for_tiles(copies, per_quarter, one):
    for n, copy in enumerate(copies):
        if copy is not None:
            copy.wait()
        for t in range(CHUNK // TILE):
            one(n // per_quarter, pl.ds(n % per_quarter * CHUNK + t * TILE, TILE))


def gen_body(place_ref, u, low, adapt, slot_a, slot_b, slot_c, up_in, down_in, *refs):
    up_out, down_out, slope, mine, other, up, down, last, act, sems, up_sems, down_sems = refs
    rows = mine.shape[0]
    slots = (slot_a, slot_b, slot_c)
    held = (up, up, down)
    stored = (up_out, up_out, down_out)
    fetches = [pltpu.make_async_copy(slots[i], last.at[i], sems.at[i]) for i in range(3)]
    for i in range(2):
        fetches[i].start()
    up_copies = [
        pltpu.make_async_copy(up_in.at[q], up.at[q], up_sems.at[q]) for q in range(2)
    ]
    for copy in up_copies:
        copy.start()
    fetches[2].start()
    down_copy = pltpu.make_async_copy(down_in, down, down_sems.at[0])
    down_copy.start()

    def place(i):
        def one(k):
            quarter, row = piece_place(place_ref, i, 3, k)
            held[i][quarter, pl.ds(row, PIECE)] = last[i, k]

        each_piece(one)

    def store(i):
        def one(k):
            quarter, row = piece_place(place_ref, i, 3, k)
            pltpu.make_async_copy(
                last.at[i, k], stored[i].at[quarter, pl.ds(row, PIECE)], sems.at[3 + i]
            ).start()

        each_piece(one)

    for copy in fetches[:2] + up_copies:
        copy.wait()
    place(0)
    place(1)

    def hidden_tile(q, cols):
        pre = dot(u[...], up[q, :, cols]) + dot(low[...], adapt[q, :, cols])
        value, slope[q, :, cols] = gelu_and_slope(pre)
        act[q, :, cols] = value.astype(act.dtype)

    for_tiles([None] * (2 * up.shape[2] // CHUNK), up.shape[2] // CHUNK, hidden_tile)
    fetches[2].wait()
    down_copy.wait()
    place(2)
    for i in range(3):
        store(i)

    def width_tile(q, cols):
        out = dot(act[0], down[0, cols, :], NT) + dot(act[1], down[1, cols, :], NT)
        mine[:, cols] = out[:rows]
        other[:, cols] = out[rows:].astype(other.dtype)

    for_tiles([None] * (down.shape[1] // CHUNK), down.shape[1] // CHUNK, width_tile)
    for i in range(3):
        wait_all(last.at[i], sems.at[3 + i])


def gen_forward(coords, u, low, adapt, slots, up, down):
    group, width = u.shape
    hidden = up.shape[2]
    rows = group // 2
    f32, bf16 = jnp.float32, jnp.bfloat16
    shape = jax.ShapeDtypeStruct((2, width, hidden), bf16)
    last = [slots[i][3].reshape(RING * RING, PIECE, hidden) for i in range(3)]
    return pl.pallas_call(
        gen_body,
        out_shape=(
            shape,
            shape,
            jax.ShapeDtypeStruct((2, group, hidden), f32),
            jax.ShapeDtypeStruct((rows, width), f32),
            jax.ShapeDtypeStruct((rows, width), bf16),
        ),
        in_specs=[IN_SMEM] + [IN_VMEM] * 3 + [ANYWHERE] * 3 + [IN_HBM] * 2,
        out_specs=(IN_HBM, IN_HBM) + (IN_VMEM,) * 3,
        scratch_shapes=[
            pltpu.VMEM(shape.shape, bf16),
            pltpu.VMEM(shape.shape, bf16),
            pltpu.VMEM((3, RING * RING, PIECE, hidden), bf16),
            pltpu.VMEM((2, group, hidden), bf16),
            pltpu.SemaphoreType.DMA((6,)),
            pltpu.SemaphoreType.DMA((2,)),
            pltpu.SemaphoreType.DMA((1,)),
        ],
        input_output_aliases={7: 0, 8: 1},
        compiler_params=pltpu.CompilerParams(vmem_limit_bytes=56 * MIB),
        cost_estimate=pl.CostEstimate(
            flops=8 * group * width * hidden,
            bytes_accessed=50 * MIB,
            transcendentals=2 * group * hidden,
        ),
        name="gen_forward",
    )(coords, u, low, adapt, *last, up, down)


def score_body(
    u_mine, u_other, adapt_in, adapt_out, up_in, down_in, slope, low, real, fake, others, *scratch
):
    u, act, up, down, up_sems, down_sems = scratch
    up_copies = start_by_columns(up_in, up, up_sems)
    down_copies = start_by_rows(down_in, down, down_sems)
    rows = u_mine.shape[0]
    group = 2 * rows
    u[:rows] = u_mine[...]
    u[rows:] = u_other[...]
    low[...] = dot(u[...], adapt_in[...], NT).astype(low.dtype)

    def hidden_tile(q, cols):
        pre_real = dot(u[...], up[q, :, cols])
        pre_fake = pre_real + dot(low[...], adapt_out[q, :, cols])
        act[q, :group, cols] = gelu_value(pre_real).astype(act.dtype)
        value, slope[q, :, cols] = gelu_and_slope(pre_fake)
        act[q, group:, cols] = value.astype(act.dtype)

    for_tiles(up_copies, up.shape[2] // CHUNK, hidden_tile)

    def width_tile(q, cols):
        out = dot(act[0], down[0, cols, :], NT) + dot(act[1], down[1, cols, :], NT)
        real[:, cols] = out[:rows]
        others[:rows, cols] = out[rows:group].astype(others.dtype)
        fake[:, cols] = out[group : group + rows]
        others[rows:, cols] = out[group + rows :].astype(others.dtype)

    for_tiles(down_copies, down.shape[1] // CHUNK, width_tile)


def score_forward(u_mine, u_other, adapt_in, adapt_out, up, down):
    rows, width = u_mine.shape
    hidden = up.shape[2]
    group = 2 * rows
    f32, bf16 = jnp.float32, jnp.bfloat16
    return pl.pallas_call(
        score_body,
        out_shape=(
            jax.ShapeDtypeStruct((2, group, hidden), f32),
            jax.ShapeDtypeStruct((group, adapt_in.shape[0]), bf16),
            jax.ShapeDtypeStruct((rows, width), f32),
            jax.ShapeDtypeStruct((rows, width), f32),
            jax.ShapeDtypeStruct((group, width), bf16),
        ),
        in_specs=[IN_VMEM] * 4 + [IN_HBM] * 2,
        out_specs=(IN_VMEM,) * 5,
        scratch_shapes=[
            pltpu.VMEM((group, width), bf16),
            pltpu.VMEM((2, 2 * group, hidden), bf16),
            pltpu.VMEM(up.shape, bf16),
            pltpu.VMEM(down.shape, bf16),
            pltpu.SemaphoreType.DMA((2 * hidden // CHUNK,)),
            pltpu.SemaphoreType.DMA((width // CHUNK,)),
        ],
        compiler_params=pltpu.CompilerParams(vmem_limit_bytes=56 * MIB),
        cost_estimate=pl.CostEstimate(
            flops=12 * group * width * hidden,
            bytes_accessed=10 * 2**20,
            transcendentals=4 * group * hidden,
        ),
        name="score_forward",
    )(u_mine, u_other, adapt_in, adapt_out, up, down)


def back_body(
    cots_mine, cots_other, slope_gen, slope_fake, low_gen, low_fake, gen_out, fake_out, down_in, grads, mix, *scratch
):
    cots, down, sems = scratch
    copies = start_by_columns(down_in, down, sems)
    group = cots_mine.shape[0]
    rows = group // 2
    for i in range(2):
        cots[i * group : i * group + rows] = cots_mine[i * rows : (i + 1) * rows]
        cots[i * group + rows : (i + 1) * group] = cots_other[i * rows : (i + 1) * rows]
    mix[...] = jnp.zeros_like(mix)

    def hidden_tile(q, cols):
        raw = dot(cots[...], down[q, :, cols])
        back_gen = (raw[:group] * slope_gen[q, :, cols]).astype(jnp.bfloat16)
        back_fake = (raw[group:] * slope_fake[q, :, cols]).astype(jnp.bfloat16)
        grads[0, q, :, cols] = dot(low_gen[...], back_gen, TN).astype(grads.dtype)
        grads[1, q, :, cols] = dot(low_fake[...], back_fake, TN).astype(grads.dtype)
        mix[0] += dot(back_gen, gen_out[q, :, cols], NT)
        mix[1] += dot(back_fake, fake_out[q, :, cols], NT)

    for_tiles(copies, down.shape[2] // CHUNK, hidden_tile)


def backward(cots_mine, cots_other, slope_gen, slope_fake, low_gen, low_fake, gen_out, fake_out, down):
    group, width = cots_mine.shape
    hidden = down.shape[2]
    rank = low_gen.shape[1]
    f32, bf16 = jnp.float32, jnp.bfloat16
    return pl.pallas_call(
        back_body,
        out_shape=(
            jax.ShapeDtypeStruct((2, 2, rank, hidden), bf16),
            jax.ShapeDtypeStruct((2, group, rank), f32),
        ),
        in_specs=[IN_VMEM] * 8 + [IN_HBM],
        out_specs=(IN_VMEM,) * 2,
        scratch_shapes=[
            pltpu.VMEM((2 * group, width), bf16),
            pltpu.VMEM(down.shape, bf16),
            pltpu.SemaphoreType.DMA((2 * hidden // CHUNK,)),
        ],
        compiler_params=pltpu.CompilerParams(vmem_limit_bytes=40 * MIB),
        cost_estimate=pl.CostEstimate(
            flops=8 * group * width * hidden, bytes_accessed=10 * 2**20, transcendentals=0
        ),
        name="backward",
    )(cots_mine, cots_other, slope_gen, slope_fake, low_gen, low_fake, gen_out, fake_out, down)


STRIP = 16


def noise_body(ends, blends, given, noise, mine, other, mods, gate, latents_ref, noised_ref, u_ref):
    f32 = jnp.float32

    def strip(n, carry):
        rows = pl.ds(pl.multiple_of(n * STRIP, STRIP), STRIP)
        in_last = n * STRIP + lax.broadcasted_iota(jnp.int32, (STRIP, 1), 0) >= ends[0]
        out = mine[rows] + other[rows].astype(f32)
        latents = (given[rows].astype(f32) + gate[...] * out).astype(latents_ref.dtype)
        latents_ref[rows] = latents
        blend = jnp.where(in_last, blends[1], blends[0])
        noised = (
            (1.0 - blend) * latents.astype(f32) + blend * noise[rows].astype(f32)
        ).astype(noised_ref.dtype)
        noised_ref[rows] = noised
        scale = jnp.where(in_last, mods[1:2], mods[0:1])
        shift = jnp.where(in_last, mods[3:4], mods[2:3])
        u_ref[rows] = modulate(noised, scale, shift)
        return carry

    lax.fori_loop(0, given.shape[0] // STRIP, strip, 0)


def add_noise(ends, blends, given, noise, mine, other, mods, gate):
    shape = jax.ShapeDtypeStruct(given.shape, given.dtype)
    return pl.pallas_call(
        noise_body,
        out_shape=(shape,) * 3,
        in_specs=[IN_SMEM] * 2 + [IN_VMEM] * 6,
        out_specs=(IN_VMEM,) * 3,
        compiler_params=pltpu.CompilerParams(vmem_limit_bytes=10 * MIB),
        cost_estimate=pl.CostEstimate(flops=0, bytes_accessed=6 * MIB, transcendentals=0),
        name="add_noise",
    )(ends, blends, given, noise, mine, other, mods, gate)


def cotangent_body(scale, real, fake, others, gate_ref, noise, latents, noised, diff_ref, cots):
    f32 = jnp.float32
    count = real.shape[0]

    def strip(n, carry):
        start = pl.multiple_of(n * STRIP, STRIP)
        rows, second = pl.ds(start, STRIP), pl.ds(count + start, STRIP)
        gate = gate_ref[...]
        out_real = real[rows] + others[rows].astype(f32)
        out_fake = fake[rows] + others[second].astype(f32)
        diff = (gate * (out_fake - out_real)).astype(diff_ref.dtype)
        diff_ref[rows] = diff
        cots[rows] = (gate * diff.astype(f32) * scale).astype(cots.dtype)
        target = noise[rows].astype(f32) - latents[rows].astype(f32)
        cots[second] = (
            gate * (noised[rows].astype(f32) + gate * out_fake - target) * scale
        ).astype(cots.dtype)
        return carry

    lax.fori_loop(0, count // STRIP, strip, 0)


def cotangents(scale, real, fake, others, gate, noise, latents, noised):
    rows, width = real.shape
    return pl.pallas_call(
        functools.partial(cotangent_body, scale),
        out_shape=(
            jax.ShapeDtypeStruct((rows, width), noise.dtype),
            jax.ShapeDtypeStruct((2 * rows, width), noise.dtype),
        ),
        in_specs=[IN_VMEM] * 7,
        out_specs=(IN_VMEM,) * 2,
        compiler_params=pltpu.CompilerParams(vmem_limit_bytes=12 * MIB),
        cost_estimate=pl.CostEstimate(flops=0, bytes_accessed=8 * MIB, transcendentals=0),
        name="cotangents",
    )(real, fake, others, gate, noise, latents, noised)


def three_terms(value):
    high = lax.reduce_precision(value, 8, 7)
    rest = value - high
    middle = lax.reduce_precision(rest, 8, 7)
    low = rest - middle
    return jnp.concatenate([high, middle, low], axis=1).astype(jnp.bfloat16)


def local(
    gen_input,
    noise_score,
    gen_steps,
    score_steps,
    base_up,
    base_down,
    gen_adapt_in,
    gen_adapt_out,
    fake_adapt_in,
    fake_adapt_out,
    modulation_scale,
    modulation_shift,
    output_gate,
):
    bf16, f32 = jnp.bfloat16, jnp.float32
    shard_rows, width = gen_input.shape
    hidden = base_up.shape[1]
    rank = gen_adapt_in.shape[1]
    image_count = gen_steps.shape[0]
    loss_scale = 1.0 / math.sqrt(image_count * IMG_TOK)
    core = lax.axis_index("core")
    xl = lax.axis_index("xl")
    first_row = lax.axis_index(AXES) * shard_rows
    first_image = first_row // IMG_TOK
    last_image = (first_row + shard_rows - 1) // IMG_TOK
    row_ids = first_row + jnp.arange(shard_rows, dtype=jnp.int32)
    in_last = (row_ids >= last_image * IMG_TOK)[:, None]

    def two_steps(steps):
        return jnp.stack([steps[first_image], steps[last_image]])

    def modulation(steps):
        embed = embedding(two_steps(steps), width)
        return 1.0 + modulation_scale[None, :] * embed, modulation_shift[None, :] * embed

    def both_rows(mine):
        return jnp.concatenate([mine, swap_cores(mine)], axis=0)

    coords = jnp.stack(
        [
            lax.axis_index("z"),
            lax.axis_index("y"),
            lax.axis_index("xh") * 2 + xl,
            1 - 2 * core,
        ]
    ).astype(jnp.int32)
    down_rows = base_down.T
    half = base_up.shape[0] // 2
    last_quarter = lax.all_gather(down_rows[half:], CHIPS, axis=0, tiled=True)
    def other_quarter(mine):
        theirs = lax.ppermute(mine, "xl", [(0, 1), (1, 0)])
        return jnp.stack([jnp.where(xl == 0, mine, theirs), jnp.where(xl == 0, theirs, mine)])

    adapt_out = other_quarter(jnp.concatenate([gen_adapt_out, fake_adapt_out], axis=0))
    gen_scale, gen_shift = modulation(gen_steps)
    u_mine = modulate(
        gen_input,
        jnp.where(in_last, gen_scale[1:], gen_scale[:1]),
        jnp.where(in_last, gen_shift[1:], gen_shift[:1]),
    )
    u_gen = both_rows(u_mine)
    low_gen = matmul(u_gen, gen_adapt_in).astype(bf16)
    mods = jnp.concatenate(modulation(score_steps), axis=0)
    blends = (two_steps(score_steps).astype(f32) + 0.5) / 1000.0
    ends = (last_image * IMG_TOK - first_row).astype(jnp.int32).reshape(1)
    slots, adapt_out, prepared = ring_slots(
        [base_up[:half], base_up[half:], down_rows[:half]],
        adapt_out,
        (u_gen, low_gen, mods, blends, ends, coords),
    )
    u_gen, low_gen, mods, blends, ends, coords = prepared
    gen_out, fake_out = adapt_out[:, :rank], adapt_out[:, rank:]
    up_part, down_part = load_weights(coords, slots, last_quarter, width, hidden)

    up_all, down_all, slope_gen, out_mine, out_other = gen_forward(
        coords, u_gen, low_gen, gen_out, slots, up_part, down_part
    )
    gate = output_gate.reshape(1, width)
    latents, noised, u_score = add_noise(
        ends, blends, gen_input, noise_score, out_mine, swap_cores(out_other), mods, gate
    )
    u_score_other = swap_cores(u_score)
    slope_fake, low_fake, out_real, out_fake, outs_other = score_forward(
        u_score, u_score_other, fake_adapt_in.T, fake_out, up_all, down_all
    )
    score_diff, cots = cotangents(
        loss_scale, out_real, out_fake, swap_cores(outs_other), gate, noise_score, latents, noised
    )
    out_grads, mix = backward(
        cots, swap_cores(cots), slope_gen, slope_fake, low_gen, low_fake, gen_out, fake_out, down_all
    )
    mix = jnp.concatenate([mix[0], mix[1]], axis=1)
    mix_other = swap_cores(mix)
    mix = mix + jnp.concatenate([mix_other[shard_rows:], mix_other[:shard_rows]], axis=0)

    def in_grad(u, mix_part):
        product = contract(u, three_terms(mix_part), 0, 0)
        total = product[:, :rank] + product[:, rank : 2 * rank] + product[:, 2 * rank :]
        chips = total.reshape(-1, 2, width // 128, rank)
        return jnp.where(core == 0, chips[:, 0], chips[:, 1])

    u_score_group = jnp.concatenate([u_score, u_score_other], axis=0)
    in_grads = jnp.concatenate(
        [in_grad(u_gen, mix[:, :rank]), in_grad(u_score_group, mix[:, rank:])], axis=2
    )
    chips, in_rows = in_grads.shape[0], in_grads.shape[1]
    groups = chips // 2
    out_grads = out_grads.reshape(2, 2, groups, rank // groups, hidden).transpose(2, 1, 0, 3, 4)
    out_rows = 2 * (rank // groups) * hidden // 128
    packed = jnp.concatenate(
        [in_grads.astype(bf16), out_grads.reshape(chips, out_rows, 128)], axis=1
    )
    received = lax.all_to_all(packed, CHIPS, 0, 0, tiled=True)
    summed = jnp.sum(received.astype(f32), axis=0)
    gen_grad_in, fake_grad_in = summed[:in_rows, :rank], summed[:in_rows, rank:]
    grads_out = summed[in_rows:].reshape(2, rank // groups, hidden)
    return (score_diff, gen_grad_in, grads_out[0], fake_grad_in, grads_out[1])


def solution(mesh):
    fine = Mesh(mesh.devices.reshape(4, 4, 2, 2, 2), AXES)
    dp, mp = ("z", "y", "xh"), ("xl", "core")
    return jax.shard_map(
        local,
        mesh=fine,
        in_specs=(
            P(AXES, None),
            P(AXES, None),
            P(),
            P(),
            P(dp, mp),
            P(mp, dp),
            P(),
            P(None, mp),
            P(),
            P(None, mp),
            P(),
            P(),
            P(),
        ),
        out_specs=(
            P(AXES, None),
            P(AXES, None),
            P(dp, mp),
            P(AXES, None),
            P(dp, mp),
        ),
        check_vma=False,
    )
```

```python
import functools
import math

import jax
import jax.numpy as jnp
from jax import lax
from jax.experimental import pallas as pl
from jax.experimental.pallas import tpu as pltpu
from jax.sharding import Mesh
from jax.sharding import PartitionSpec as P

IMG_TOK = 1024
AXES = ("z", "y", "xh", "xl", "core")
CHIPS = ("z", "y", "xh", "xl")

gelu_coef = 0.044715
root_two_pi = math.sqrt(2.0 / math.pi)


def gelu_value(pre):
    inner_arg = root_two_pi * (pre + gelu_coef * pre * pre * pre)
    return 0.5 * pre * (1.0 + jnp.tanh(inner_arg))


def gelu_slope(pre):
    tanh_val = jnp.tanh(root_two_pi * (pre + gelu_coef * pre * pre * pre))
    return 0.5 * (1.0 + tanh_val) + 0.5 * pre * (1.0 - tanh_val * tanh_val) * root_two_pi * (
        1.0 + 3.0 * gelu_coef * pre * pre
    )


def embedding(steps, feature_count):
    half_width = feature_count // 2
    frequency = jnp.exp(-math.log(10000.0) * jnp.arange(half_width, dtype=jnp.float32) / half_width)
    phase_angle = steps.astype(jnp.float32)[:, None] * frequency[None, :]
    return jnp.concatenate([jnp.sin(phase_angle), jnp.cos(phase_angle)], axis=1)


def modulate(rows, scale_rows, shift_rows):
    widened = rows.astype(jnp.float32)
    normed = widened * lax.rsqrt(jnp.mean(widened * widened, axis=1, keepdims=True) + 1e-06)
    return (normed * scale_rows + shift_rows).astype(jnp.bfloat16)


def matmul(left, right):
    return jnp.dot(left, right, preferred_element_type=jnp.float32)


def contract(left, right, left_dim, right_dim):
    return lax.dot_general(
        left, right, (((left_dim,), (right_dim,)), ((), ())), preferred_element_type=jnp.float32
    )


def swap_cores(value):
    return lax.ppermute(value, "core", [(0, 1), (1, 0)])


RING_AXES = (("y", "z", "x"), ("z", "x", "y"), ("x", "y", "z"))
RING = 4


def chip_ring(axis):
    pairs = []
    for device in range(128):
        place = {"z": device // 32, "y": device // 8 % 4, "x": device // 2 % 4, "core": device % 2}
        step = 1 if place["core"] == 0 else -1
        place[axis] = (place[axis] + step) % RING
        target = place["z"] * 32 + place["y"] * 8 + place["x"] * 2 + place["core"]
        pairs.append((device, target))
    return pairs


def ring(pieces, phase):
    slots = [[piece] for piece in pieces]
    for _ in range(RING - 1):
        for i, held in enumerate(slots):
            held.append(lax.ppermute(held[-1], AXES, chip_ring(RING_AXES[i][phase])))
    return slots


def ring_slots(pieces, early, middle):
    for phase in range(2):
        pieces = [jnp.concatenate(held, axis=0) for held in ring(pieces, phase)]
    pieces, early = lax.optimization_barrier((pieces, early))
    count = pieces[0].shape[0] // 2
    slots = [[[piece[h * count : (h + 1) * count]] for piece in pieces] for h in range(2)]
    for step in range(1, RING):
        if step == RING - 1:
            held = [slots[0][i][-1] for i in range(3)]
            held, middle = lax.optimization_barrier((held, middle))
            for i in range(3):
                slots[0][i][-1] = held[i]
        for h in range(2):
            for i in range(3):
                slots[h][i].append(lax.ppermute(slots[h][i][-1], AXES, chip_ring(RING_AXES[i][2])))
    return slots, early, middle


SHARD = 96
PIECE = 64
REST = SHARD - PIECE
TILE = 512
MIB = 2**20
ANYWHERE = pl.BlockSpec(memory_space=pl.ANY)
IN_VMEM = pl.BlockSpec(memory_space=pltpu.VMEM)
IN_SMEM = pl.BlockSpec(memory_space=pltpu.SMEM)
NT = (((1,), (1,)), ((), ()))
TN = (((0,), (0,)), ((), ()))


def dot(left, right, dims=(((1,), (0,)), ((), ()))):
    return lax.dot_general(left, right, dims, preferred_element_type=jnp.float32)


def gelu_and_slope(pre):
    square = pre * pre
    tanh_val = jnp.tanh(root_two_pi * (pre + gelu_coef * square * pre))
    half = 0.5 * (1.0 + tanh_val)
    slope = half + 0.5 * pre * (1.0 - tanh_val * tanh_val) * root_two_pi * (
        1.0 + 3.0 * gelu_coef * square
    )
    return pre * half, slope


IN_HBM = pl.BlockSpec(memory_space=pltpu.HBM)


def piece_place(place_ref, i, step, k):
    me = {"z": place_ref[0], "y": place_ref[1], "x": place_ref[2]}
    direction = place_ref[3]
    first, second, third = RING_AXES[i]

    def source(axis, distance):
        return lax.rem(me[axis] - distance * direction + RING, RING)

    at = {
        first: source(first, lax.rem(k, RING)),
        second: source(second, lax.div(k, RING)),
        third: source(third, step),
    }
    group = (at["z"] * 4 + at["y"]) * 2 + lax.div(at["x"], 2)
    return lax.rem(at["x"], 2), pl.multiple_of(group * SHARD, 32)


def each(count, one, unroll=4):
    def step(k, carry):
        one(k)
        return carry

    lax.fori_loop(0, count, step, 0, unroll=unroll)


def wait_all(ref, sem):
    pltpu.make_async_copy(ref, ref, sem).wait()


def start_piece(i, source, quarter, row, up, down, sem):
    hidden = source.shape[1]
    cols = pl.ds(pl.multiple_of(quarter * hidden, 128), hidden)
    if i < 2:
        target = (up, down)[i].at[pl.ds(row, PIECE), cols]
        pltpu.make_async_copy(source, target, sem).start()
    else:
        for n, matrix in enumerate((up, down)):
            rows = pl.ds(pl.multiple_of(row + PIECE, 32), REST)
            pltpu.make_async_copy(source.at[pl.ds(n * REST, REST)], matrix.at[rows, cols], sem).start()


def load_body(place_ref, *refs):
    slots, (up_out, down_out, up, down, sems) = refs[:18], refs[18:]
    for n, slot in enumerate(slots):
        step, half, i = n // 6, n // 3 % 2, n % 3

        def one(k, slot=slot, step=step, half=half, i=i, n=n):
            quarter, row = piece_place(place_ref, i, step, 2 * RING * half + k)
            start_piece(i, slot.at[k], quarter, row, up, down, sems.at[n])

        each(2 * RING, one)
    for n, slot in enumerate(slots):
        if n % 3 != 1:
            wait_all(slot, sems.at[n])
    up_copy = pltpu.make_async_copy(up, up_out, sems.at[18])
    up_copy.start()
    for n, slot in enumerate(slots):
        if n % 3 == 1:
            wait_all(slot, sems.at[n])
    down_copy = pltpu.make_async_copy(down, down_out, sems.at[19])
    down_copy.start()
    up_copy.wait()
    down_copy.wait()


def load_weights(coords, slots, width, hidden):
    flat = [
        slots[half][i][step].reshape(2 * RING, PIECE, hidden)
        for step in range(3)
        for half in range(2)
        for i in range(3)
    ]
    shape = jax.ShapeDtypeStruct((width, 2 * hidden), jnp.bfloat16)
    return pl.pallas_call(
        load_body,
        out_shape=(shape, shape),
        in_specs=[IN_SMEM] + [ANYWHERE] * 18,
        out_specs=(IN_HBM, IN_HBM),
        scratch_shapes=[
            pltpu.VMEM(shape.shape, shape.dtype),
            pltpu.VMEM(shape.shape, shape.dtype),
            pltpu.SemaphoreType.DMA((20,)),
        ],
        compiler_params=pltpu.CompilerParams(vmem_limit_bytes=40 * MIB),
        cost_estimate=pl.CostEstimate(
            flops=0, bytes_accessed=8 * width * hidden * 4, transcendentals=0
        ),
        name="load_weights",
    )(coords, *flat)


def column_copy(source, target, sems, n):
    cols = pl.ds(pl.multiple_of(n * TILE, TILE), TILE)
    return pltpu.make_async_copy(source.at[:, cols], target.at[:, cols], sems.at[n])


def row_copy(source, target, sems, n):
    rows = pl.ds(pl.multiple_of(n * TILE, TILE), TILE)
    return pltpu.make_async_copy(source.at[rows], target.at[rows], sems.at[n])


def tile_at(n):
    return pl.ds(pl.multiple_of(n * TILE, TILE), TILE)


def gen_body(place_ref, u, low, adapt, *refs):
    slots, (up_in, down_in, up_out, down_out, slope, mine, other) = refs[:6], refs[6:13]
    up, down, last, act, sems, up_sems, down_sems = refs[13:]
    rows = mine.shape[0]
    tiles = up.shape[1] // TILE
    per_quarter = tiles // 2
    pieces = RING * RING
    fetches = {}
    for i in (0, 2, 1):
        for half in range(2):
            n = 2 * i + half
            target = last.at[i, pl.ds(half * 2 * RING, 2 * RING)]
            fetches[n] = pltpu.make_async_copy(slots[n], target, sems.at[n])
    for n in (0, 1, 4, 5):
        fetches[n].start()
    each(tiles, lambda n: column_copy(up_in, up, up_sems, n).start(), 1)
    for n in (2, 3):
        fetches[n].start()
    whole_down = pltpu.make_async_copy(down_in, down, down_sems.at[0])
    whole_down.start()
    for n in (0, 1, 4, 5):
        fetches[n].wait()

    def hidden_tile(n):
        column_copy(up_in, up, up_sems, n).wait()
        cols = tile_at(n)
        part = pl.ds(pl.multiple_of(lax.rem(n, per_quarter) * TILE, TILE), TILE)

        def place(k):
            for i in (0, 2):
                quarter, row = piece_place(place_ref, i, 3, k)

                @pl.when(quarter == lax.div(n, per_quarter))
                def _(i=i, row=row):
                    if i == 0:
                        up[pl.ds(row, PIECE), cols] = last[0, k, :, part]
                    else:
                        up[pl.ds(pl.multiple_of(row + PIECE, 32), REST), cols] = last[2, k, :REST, part]

        each(pieces, place, 1)
        pre = dot(u[...], up[:, cols]) + dot(low[...], adapt[:, cols])
        value, slope[:, cols] = gelu_and_slope(pre)
        act[:, cols] = value.astype(act.dtype)

    each(tiles, hidden_tile, 1)
    for n in (2, 3):
        fetches[n].wait()
    whole_down.wait()
    hidden = last.shape[3]

    def place_down(k):
        for i in (1, 2):
            quarter, row = piece_place(place_ref, i, 3, k)
            cols = pl.ds(pl.multiple_of(quarter * hidden, 128), hidden)
            if i == 1:
                down[pl.ds(row, PIECE), cols] = last[1, k]
            else:
                down[pl.ds(pl.multiple_of(row + PIECE, 32), REST), cols] = last[2, k, REST:]

    each(pieces, place_down, 1)
    for i in range(3):

        def store(k, i=i):
            quarter, row = piece_place(place_ref, i, 3, k)
            start_piece(i, last.at[i, k], quarter, row, up_out, down_out, sems.at[6 + i])

        each(pieces, store)

    def width_tile(n):
        cols = tile_at(n)
        out = dot(act[...], down[cols, :], NT)
        mine[:, cols] = out[:rows]
        other[:, cols] = out[rows:].astype(other.dtype)

    each(down.shape[0] // TILE, width_tile, 1)
    for i in range(3):
        wait_all(last.at[i], sems.at[6 + i])


def gen_forward(coords, u, low, adapt, slots, up, down):
    group, width = u.shape
    hidden = up.shape[1]
    rows = group // 2
    f32, bf16 = jnp.float32, jnp.bfloat16
    shape = jax.ShapeDtypeStruct((width, hidden), bf16)
    last = [
        slots[half][i][3].reshape(2 * RING, PIECE, hidden // 2) for i in range(3) for half in range(2)
    ]
    return pl.pallas_call(
        gen_body,
        out_shape=(
            shape,
            shape,
            jax.ShapeDtypeStruct((group, hidden), f32),
            jax.ShapeDtypeStruct((rows, width), f32),
            jax.ShapeDtypeStruct((rows, width), bf16),
        ),
        in_specs=[IN_SMEM] + [IN_VMEM] * 3 + [ANYWHERE] * 6 + [IN_HBM] * 2,
        out_specs=(IN_HBM, IN_HBM) + (IN_VMEM,) * 3,
        scratch_shapes=[
            pltpu.VMEM(shape.shape, bf16),
            pltpu.VMEM(shape.shape, bf16),
            pltpu.VMEM((3, RING * RING, PIECE, hidden // 2), bf16),
            pltpu.VMEM((group, hidden), bf16),
            pltpu.SemaphoreType.DMA((9,)),
            pltpu.SemaphoreType.DMA((hidden // TILE,)),
            pltpu.SemaphoreType.DMA((1,)),
        ],
        input_output_aliases={10: 0, 11: 1},
        compiler_params=pltpu.CompilerParams(vmem_limit_bytes=56 * MIB),
        cost_estimate=pl.CostEstimate(
            flops=4 * group * width * hidden,
            bytes_accessed=50 * MIB,
            transcendentals=group * hidden,
        ),
        name="gen_forward",
    )(coords, u, low, adapt, *last, up, down)


def score_body(
    u_mine, u_other, adapt_in, adapt_out, up_in, down_in, slope, low, real, fake, others, *scratch
):
    u, act, up, down, up_sems, down_sems = scratch
    hidden_tiles, width_tiles = up.shape[1] // TILE, down.shape[0] // TILE
    each(hidden_tiles, lambda n: column_copy(up_in, up, up_sems, n).start(), 1)
    each(width_tiles, lambda n: row_copy(down_in, down, down_sems, n).start(), 1)
    rows = u_mine.shape[0]
    group = 2 * rows
    u[:rows] = u_mine[...]
    u[rows:] = u_other[...]
    low[...] = dot(u[...], adapt_in[...], NT).astype(low.dtype)

    def hidden_tile(n):
        column_copy(up_in, up, up_sems, n).wait()
        cols = tile_at(n)
        pre_real = dot(u[...], up[:, cols])
        pre_fake = pre_real + dot(low[...], adapt_out[:, cols])
        act[:group, cols] = gelu_value(pre_real).astype(act.dtype)
        value, slope[:, cols] = gelu_and_slope(pre_fake)
        act[group:, cols] = value.astype(act.dtype)

    each(hidden_tiles, hidden_tile, 1)

    def width_tile(n):
        row_copy(down_in, down, down_sems, n).wait()
        cols = tile_at(n)
        out = dot(act[...], down[cols, :], NT)
        real[:, cols] = out[:rows]
        others[:rows, cols] = out[rows:group].astype(others.dtype)
        fake[:, cols] = out[group : group + rows]
        others[rows:, cols] = out[group + rows :].astype(others.dtype)

    each(width_tiles, width_tile, 1)


def score_forward(u_mine, u_other, adapt_in, adapt_out, up, down):
    rows, width = u_mine.shape
    hidden = up.shape[1]
    group = 2 * rows
    f32, bf16 = jnp.float32, jnp.bfloat16
    return pl.pallas_call(
        score_body,
        out_shape=(
            jax.ShapeDtypeStruct((group, hidden), f32),
            jax.ShapeDtypeStruct((group, adapt_in.shape[0]), bf16),
            jax.ShapeDtypeStruct((rows, width), f32),
            jax.ShapeDtypeStruct((rows, width), f32),
            jax.ShapeDtypeStruct((group, width), bf16),
        ),
        in_specs=[IN_VMEM] * 4 + [IN_HBM] * 2,
        out_specs=(IN_VMEM,) * 5,
        scratch_shapes=[
            pltpu.VMEM((group, width), bf16),
            pltpu.VMEM((2 * group, hidden), bf16),
            pltpu.VMEM(up.shape, bf16),
            pltpu.VMEM(down.shape, bf16),
            pltpu.SemaphoreType.DMA((hidden // TILE,)),
            pltpu.SemaphoreType.DMA((width // TILE,)),
        ],
        compiler_params=pltpu.CompilerParams(vmem_limit_bytes=56 * MIB),
        cost_estimate=pl.CostEstimate(
            flops=6 * group * width * hidden,
            bytes_accessed=50 * MIB,
            transcendentals=2 * group * hidden,
        ),
        name="score_forward",
    )(u_mine, u_other, adapt_in, adapt_out, up, down)


def back_body(
    cots_mine, cots_other, slope_gen, slope_fake, low_gen, low_fake, gen_out, fake_out, down_in, grads, mix, *scratch
):
    cots, down, sems = scratch
    tiles = down.shape[1] // TILE
    each(tiles, lambda n: column_copy(down_in, down, sems, n).start(), 1)
    group = cots_mine.shape[0]
    rows = group // 2
    for i in range(2):
        cots[i * group : i * group + rows] = cots_mine[i * rows : (i + 1) * rows]
        cots[i * group + rows : (i + 1) * group] = cots_other[i * rows : (i + 1) * rows]
    mix[...] = jnp.zeros_like(mix)

    def hidden_tile(n):
        column_copy(down_in, down, sems, n).wait()
        cols = tile_at(n)
        raw = dot(cots[...], down[:, cols])
        back_gen = (raw[:group] * slope_gen[:, cols]).astype(jnp.bfloat16)
        back_fake = (raw[group:] * slope_fake[:, cols]).astype(jnp.bfloat16)
        grads[0, :, cols] = dot(low_gen[...], back_gen, TN).astype(grads.dtype)
        grads[1, :, cols] = dot(low_fake[...], back_fake, TN).astype(grads.dtype)
        mix[0] += dot(back_gen, gen_out[:, cols], NT)
        mix[1] += dot(back_fake, fake_out[:, cols], NT)

    each(tiles, hidden_tile, 1)


def backward(cots_mine, cots_other, slope_gen, slope_fake, low_gen, low_fake, gen_out, fake_out, down):
    group, width = cots_mine.shape
    hidden = down.shape[1]
    rank = low_gen.shape[1]
    f32, bf16 = jnp.float32, jnp.bfloat16
    return pl.pallas_call(
        back_body,
        out_shape=(
            jax.ShapeDtypeStruct((2, rank, hidden), bf16),
            jax.ShapeDtypeStruct((2, group, rank), f32),
        ),
        in_specs=[IN_VMEM] * 8 + [IN_HBM],
        out_specs=(IN_VMEM,) * 2,
        scratch_shapes=[
            pltpu.VMEM((2 * group, width), bf16),
            pltpu.VMEM(down.shape, bf16),
            pltpu.SemaphoreType.DMA((hidden // TILE,)),
        ],
        compiler_params=pltpu.CompilerParams(vmem_limit_bytes=40 * MIB),
        cost_estimate=pl.CostEstimate(
            flops=4 * group * width * hidden, bytes_accessed=30 * MIB, transcendentals=0
        ),
        name="backward",
    )(cots_mine, cots_other, slope_gen, slope_fake, low_gen, low_fake, gen_out, fake_out, down)


STRIP = 16


def noise_body(ends, blends, given, noise, mine, other, mods, gate, latents_ref, noised_ref, u_ref):
    f32 = jnp.float32

    def strip(n, carry):
        rows = pl.ds(pl.multiple_of(n * STRIP, STRIP), STRIP)
        in_last = n * STRIP + lax.broadcasted_iota(jnp.int32, (STRIP, 1), 0) >= ends[0]
        out = mine[rows] + other[rows].astype(f32)
        latents = (given[rows].astype(f32) + gate[...] * out).astype(latents_ref.dtype)
        latents_ref[rows] = latents
        blend = jnp.where(in_last, blends[1], blends[0])
        noised = (
            (1.0 - blend) * latents.astype(f32) + blend * noise[rows].astype(f32)
        ).astype(noised_ref.dtype)
        noised_ref[rows] = noised
        scale = jnp.where(in_last, mods[1:2], mods[0:1])
        shift = jnp.where(in_last, mods[3:4], mods[2:3])
        u_ref[rows] = modulate(noised, scale, shift)
        return carry

    lax.fori_loop(0, given.shape[0] // STRIP, strip, 0)


def add_noise(ends, blends, given, noise, mine, other, mods, gate):
    shape = jax.ShapeDtypeStruct(given.shape, given.dtype)
    return pl.pallas_call(
        noise_body,
        out_shape=(shape,) * 3,
        in_specs=[IN_SMEM] * 2 + [IN_VMEM] * 6,
        out_specs=(IN_VMEM,) * 3,
        compiler_params=pltpu.CompilerParams(vmem_limit_bytes=10 * MIB),
        cost_estimate=pl.CostEstimate(flops=0, bytes_accessed=6 * MIB, transcendentals=0),
        name="add_noise",
    )(ends, blends, given, noise, mine, other, mods, gate)


def cotangent_body(scale, real, fake, others, gate_ref, noise, latents, noised, diff_ref, cots):
    f32 = jnp.float32
    count = real.shape[0]

    def strip(n, carry):
        start = pl.multiple_of(n * STRIP, STRIP)
        rows, second = pl.ds(start, STRIP), pl.ds(count + start, STRIP)
        gate = gate_ref[...]
        out_real = real[rows] + others[rows].astype(f32)
        out_fake = fake[rows] + others[second].astype(f32)
        diff = (gate * (out_fake - out_real)).astype(diff_ref.dtype)
        diff_ref[rows] = diff
        cots[rows] = (gate * diff.astype(f32) * scale).astype(cots.dtype)
        target = noise[rows].astype(f32) - latents[rows].astype(f32)
        cots[second] = (
            gate * (noised[rows].astype(f32) + gate * out_fake - target) * scale
        ).astype(cots.dtype)
        return carry

    lax.fori_loop(0, count // STRIP, strip, 0)


def cotangents(scale, real, fake, others, gate, noise, latents, noised):
    rows, width = real.shape
    return pl.pallas_call(
        functools.partial(cotangent_body, scale),
        out_shape=(
            jax.ShapeDtypeStruct((rows, width), noise.dtype),
            jax.ShapeDtypeStruct((2 * rows, width), noise.dtype),
        ),
        in_specs=[IN_VMEM] * 7,
        out_specs=(IN_VMEM,) * 2,
        compiler_params=pltpu.CompilerParams(vmem_limit_bytes=12 * MIB),
        cost_estimate=pl.CostEstimate(flops=0, bytes_accessed=8 * MIB, transcendentals=0),
        name="cotangents",
    )(real, fake, others, gate, noise, latents, noised)


def three_terms(value):
    high = lax.reduce_precision(value, 8, 7)
    rest = value - high
    middle = lax.reduce_precision(rest, 8, 7)
    low = rest - middle
    return jnp.concatenate([high, middle, low], axis=1).astype(jnp.bfloat16)


def local(
    gen_input,
    noise_score,
    gen_steps,
    score_steps,
    base_up,
    base_down,
    gen_adapt_in,
    gen_adapt_out,
    fake_adapt_in,
    fake_adapt_out,
    modulation_scale,
    modulation_shift,
    output_gate,
):
    bf16, f32 = jnp.bfloat16, jnp.float32
    shard_rows, width = gen_input.shape
    hidden = base_up.shape[1]
    rank = gen_adapt_in.shape[1]
    image_count = gen_steps.shape[0]
    loss_scale = 1.0 / math.sqrt(image_count * IMG_TOK)
    core = lax.axis_index("core")
    xl = lax.axis_index("xl")
    first_row = lax.axis_index(AXES) * shard_rows
    first_image = first_row // IMG_TOK
    last_image = (first_row + shard_rows - 1) // IMG_TOK
    row_ids = first_row + jnp.arange(shard_rows, dtype=jnp.int32)
    in_last = (row_ids >= last_image * IMG_TOK)[:, None]

    def two_steps(steps):
        return jnp.stack([steps[first_image], steps[last_image]])

    def modulation(steps):
        embed = embedding(two_steps(steps), width)
        return 1.0 + modulation_scale[None, :] * embed, modulation_shift[None, :] * embed

    def both_rows(mine):
        return jnp.concatenate([mine, swap_cores(mine)], axis=0)

    coords = jnp.stack(
        [
            lax.axis_index("z"),
            lax.axis_index("y"),
            lax.axis_index("xh") * 2 + xl,
            1 - 2 * core,
        ]
    ).astype(jnp.int32)
    down_rows = base_down.T

    def both_quarters(mine):
        theirs = lax.ppermute(mine, "xl", [(0, 1), (1, 0)])
        quarters = [jnp.where(xl == 0, mine, theirs), jnp.where(xl == 0, theirs, mine)]
        return jnp.concatenate(quarters, axis=1)

    adapt_out = both_quarters(jnp.concatenate([gen_adapt_out, fake_adapt_out], axis=0))
    gen_scale, gen_shift = modulation(gen_steps)
    u_mine = modulate(
        gen_input,
        jnp.where(in_last, gen_scale[1:], gen_scale[:1]),
        jnp.where(in_last, gen_shift[1:], gen_shift[:1]),
    )
    u_gen = both_rows(u_mine)
    low_gen = matmul(u_gen, gen_adapt_in).astype(bf16)
    mods = jnp.concatenate(modulation(score_steps), axis=0)
    blends = (two_steps(score_steps).astype(f32) + 0.5) / 1000.0
    ends = (last_image * IMG_TOK - first_row).astype(jnp.int32).reshape(1)
    slots, adapt_out, prepared = ring_slots(
        [
            base_up[:PIECE],
            down_rows[:PIECE],
            jnp.concatenate([base_up[PIECE:], down_rows[PIECE:]], axis=0),
        ],
        adapt_out,
        (u_gen, low_gen, mods, blends, ends, coords),
    )
    u_gen, low_gen, mods, blends, ends, coords = prepared
    gen_out, fake_out = adapt_out[:rank], adapt_out[rank:]
    up_part, down_part = load_weights(coords, slots, width, hidden)

    up_all, down_all, slope_gen, out_mine, out_other = gen_forward(
        coords, u_gen, low_gen, gen_out, slots, up_part, down_part
    )
    gate = output_gate.reshape(1, width)
    latents, noised, u_score = add_noise(
        ends, blends, gen_input, noise_score, out_mine, swap_cores(out_other), mods, gate
    )
    u_score_other = swap_cores(u_score)
    slope_fake, low_fake, out_real, out_fake, outs_other = score_forward(
        u_score, u_score_other, fake_adapt_in.T, fake_out, up_all, down_all
    )
    score_diff, cots = cotangents(
        loss_scale, out_real, out_fake, swap_cores(outs_other), gate, noise_score, latents, noised
    )
    out_grads, mix = backward(
        cots, swap_cores(cots), slope_gen, slope_fake, low_gen, low_fake, gen_out, fake_out, down_all
    )
    mix = jnp.concatenate([mix[0], mix[1]], axis=1)
    mix_other = swap_cores(mix)
    mix = mix + jnp.concatenate([mix_other[shard_rows:], mix_other[:shard_rows]], axis=0)

    def in_grad(u, mix_part):
        product = contract(u, three_terms(mix_part), 0, 0)
        total = product[:, :rank] + product[:, rank : 2 * rank] + product[:, 2 * rank :]
        chips = total.reshape(-1, 2, width // 128, rank)
        return jnp.where(core == 0, chips[:, 0], chips[:, 1])

    u_score_group = jnp.concatenate([u_score, u_score_other], axis=0)
    in_grads = jnp.concatenate(
        [in_grad(u_gen, mix[:, :rank]), in_grad(u_score_group, mix[:, rank:])], axis=2
    )
    chips, in_rows = in_grads.shape[0], in_grads.shape[1]
    groups = chips // 2
    out_grads = out_grads.reshape(2, groups, rank // groups, 2, hidden).transpose(1, 3, 0, 2, 4)
    out_rows = 2 * (rank // groups) * hidden // 128
    packed = jnp.concatenate(
        [in_grads.astype(bf16), out_grads.reshape(chips, out_rows, 128)], axis=1
    )
    received = lax.all_to_all(packed, CHIPS, 0, 0, tiled=True)
    summed = jnp.sum(received.astype(f32), axis=0)
    gen_grad_in, fake_grad_in = summed[:in_rows, :rank], summed[:in_rows, rank:]
    grads_out = summed[in_rows:].reshape(2, rank // groups, hidden)
    return (score_diff, gen_grad_in, grads_out[0], fake_grad_in, grads_out[1])


def solution(mesh):
    fine = Mesh(mesh.devices.reshape(4, 4, 2, 2, 2), AXES)
    dp, mp = ("z", "y", "xh"), ("xl", "core")
    return jax.shard_map(
        local,
        mesh=fine,
        in_specs=(
            P(AXES, None),
            P(AXES, None),
            P(),
            P(),
            P(dp, mp),
            P(mp, dp),
            P(),
            P(None, mp),
            P(),
            P(None, mp),
            P(),
            P(),
            P(),
        ),
        out_specs=(
            P(AXES, None),
            P(AXES, None),
            P(dp, mp),
            P(AXES, None),
            P(dp, mp),
        ),
        check_vma=False,
    )
```

```python
import functools
import math

import jax
import jax.numpy as jnp
from jax import lax
from jax.experimental import pallas as pl
from jax.experimental.pallas import tpu as pltpu
from jax.sharding import Mesh
from jax.sharding import PartitionSpec as P

IMG_TOK = 1024
AXES = ("z", "y", "xh", "xl", "core")
CHIPS = ("z", "y", "xh", "xl")

gelu_coef = 0.044715
root_two_pi = math.sqrt(2.0 / math.pi)


def gelu_value(pre):
    inner_arg = root_two_pi * (pre + gelu_coef * pre * pre * pre)
    return 0.5 * pre * (1.0 + jnp.tanh(inner_arg))


def gelu_slope(pre):
    tanh_val = jnp.tanh(root_two_pi * (pre + gelu_coef * pre * pre * pre))
    return 0.5 * (1.0 + tanh_val) + 0.5 * pre * (1.0 - tanh_val * tanh_val) * root_two_pi * (
        1.0 + 3.0 * gelu_coef * pre * pre
    )


def embedding(steps, feature_count):
    half_width = feature_count // 2
    frequency = jnp.exp(-math.log(10000.0) * jnp.arange(half_width, dtype=jnp.float32) / half_width)
    phase_angle = steps.astype(jnp.float32)[:, None] * frequency[None, :]
    return jnp.concatenate([jnp.sin(phase_angle), jnp.cos(phase_angle)], axis=1)


def modulate(rows, scale_rows, shift_rows):
    widened = rows.astype(jnp.float32)
    normed = widened * lax.rsqrt(jnp.mean(widened * widened, axis=1, keepdims=True) + 1e-06)
    return (normed * scale_rows + shift_rows).astype(jnp.bfloat16)


def matmul(left, right):
    return jnp.dot(left, right, preferred_element_type=jnp.float32)


def contract(left, right, left_dim, right_dim):
    return lax.dot_general(
        left, right, (((left_dim,), (right_dim,)), ((), ())), preferred_element_type=jnp.float32
    )


def swap_cores(value):
    return lax.ppermute(value, "core", [(0, 1), (1, 0)])


RING_AXES = (("y", "z", "x"), ("z", "x", "y"), ("x", "y", "z"))
RING = 4


def chip_ring(axis):
    pairs = []
    for device in range(128):
        place = {"z": device // 32, "y": device // 8 % 4, "x": device // 2 % 4, "core": device % 2}
        step = 1 if place["core"] == 0 else -1
        place[axis] = (place[axis] + step) % RING
        target = place["z"] * 32 + place["y"] * 8 + place["x"] * 2 + place["core"]
        pairs.append((device, target))
    return pairs


def ring(pieces, phase):
    slots = [[piece] for piece in pieces]
    for _ in range(RING - 1):
        for i, held in enumerate(slots):
            held.append(lax.ppermute(held[-1], AXES, chip_ring(RING_AXES[i][phase])))
    return slots


def ring_slots(pieces, adapters, exchange, inputs, prepare):
    pieces = [jnp.concatenate(held, axis=0) for held in ring(pieces, 0)]
    pieces, adapters = lax.optimization_barrier((pieces, adapters))
    exchanged = exchange(adapters)
    pieces = [jnp.concatenate(held, axis=0) for held in ring(pieces, 1)]
    pieces, exchanged = lax.optimization_barrier((pieces, exchanged))
    count = pieces[0].shape[0] // 2
    slots = [[[piece[h * count : (h + 1) * count]] for piece in pieces] for h in range(2)]
    for step in range(1, RING):
        if step == RING - 1:
            held = [slots[0][i][-1] for i in range(3)]
            held, prepared = lax.optimization_barrier((held, prepared))
            for i in range(3):
                slots[0][i][-1] = held[i]
        for h in range(2):
            for i in range(3):
                slots[h][i].append(lax.ppermute(slots[h][i][-1], AXES, chip_ring(RING_AXES[i][2])))
        if step == 1:
            slots[0][0][1], inputs = lax.optimization_barrier((slots[0][0][1], inputs))
            prepared = prepare(*inputs)
    return slots, exchanged, prepared


SHARD = 96
PIECE = 64
REST = SHARD - PIECE
TILE = 512
MIB = 2**20
ANYWHERE = pl.BlockSpec(memory_space=pl.ANY)
IN_VMEM = pl.BlockSpec(memory_space=pltpu.VMEM)
IN_SMEM = pl.BlockSpec(memory_space=pltpu.SMEM)
NT = (((1,), (1,)), ((), ()))
TN = (((0,), (0,)), ((), ()))


def dot(left, right, dims=(((1,), (0,)), ((), ()))):
    return lax.dot_general(left, right, dims, preferred_element_type=jnp.float32)


def gelu_and_slope(pre):
    square = pre * pre
    tanh_val = jnp.tanh(root_two_pi * (pre + gelu_coef * square * pre))
    half = 0.5 * (1.0 + tanh_val)
    slope = half + 0.5 * pre * (1.0 - tanh_val * tanh_val) * root_two_pi * (
        1.0 + 3.0 * gelu_coef * square
    )
    return pre * half, slope


IN_HBM = pl.BlockSpec(memory_space=pltpu.HBM)


def piece_place(place_ref, i, step, k):
    me = {"z": place_ref[0], "y": place_ref[1], "x": place_ref[2]}
    direction = place_ref[3]
    first, second, third = RING_AXES[i]

    def source(axis, distance):
        return lax.rem(me[axis] - distance * direction + RING, RING)

    at = {
        first: source(first, lax.rem(k, RING)),
        second: source(second, lax.div(k, RING)),
        third: source(third, step),
    }
    group = (at["z"] * 4 + at["y"]) * 2 + lax.div(at["x"], 2)
    return lax.rem(at["x"], 2), pl.multiple_of(group * SHARD, 32)


def each(count, one, unroll=4):
    def step(k, carry):
        one(k)
        return carry

    lax.fori_loop(0, count, step, 0, unroll=unroll)


def wait_all(ref, sem):
    pltpu.make_async_copy(ref, ref, sem).wait()


def start_piece(i, source, quarter, row, up, down, sem):
    hidden = source.shape[1]
    cols = pl.ds(pl.multiple_of(quarter * hidden, 128), hidden)
    if i < 2:
        target = (up, down)[i].at[pl.ds(row, PIECE), cols]
        pltpu.make_async_copy(source, target, sem).start()
    else:
        for n, matrix in enumerate((up, down)):
            rows = pl.ds(pl.multiple_of(row + PIECE, 32), REST)
            pltpu.make_async_copy(source.at[pl.ds(n * REST, REST)], matrix.at[rows, cols], sem).start()


def load_body(place_ref, *refs):
    slots, (up_out, down_out, up, down, sems) = refs[:18], refs[18:]
    for n, slot in enumerate(slots):
        step, half, i = n // 6, n // 3 % 2, n % 3

        def one(k, slot=slot, step=step, half=half, i=i, n=n):
            quarter, row = piece_place(place_ref, i, step, 2 * RING * half + k)
            start_piece(i, slot.at[k], quarter, row, up, down, sems.at[n])

        each(2 * RING, one)
    for n, slot in enumerate(slots):
        if n % 3 != 1:
            wait_all(slot, sems.at[n])
    up_copy = pltpu.make_async_copy(up, up_out, sems.at[18])
    up_copy.start()
    for n, slot in enumerate(slots):
        if n % 3 == 1:
            wait_all(slot, sems.at[n])
    down_copy = pltpu.make_async_copy(down, down_out, sems.at[19])
    down_copy.start()
    up_copy.wait()
    down_copy.wait()


def load_weights(coords, slots, width, hidden):
    flat = [
        slots[half][i][step].reshape(2 * RING, PIECE, hidden)
        for step in range(3)
        for half in range(2)
        for i in range(3)
    ]
    shape = jax.ShapeDtypeStruct((width, 2 * hidden), jnp.bfloat16)
    return pl.pallas_call(
        load_body,
        out_shape=(shape, shape),
        in_specs=[IN_SMEM] + [IN_HBM] * 18,
        out_specs=(IN_HBM, IN_HBM),
        scratch_shapes=[
            pltpu.VMEM(shape.shape, shape.dtype),
            pltpu.VMEM(shape.shape, shape.dtype),
            pltpu.SemaphoreType.DMA((20,)),
        ],
        compiler_params=pltpu.CompilerParams(vmem_limit_bytes=40 * MIB),
        cost_estimate=pl.CostEstimate(
            flops=0, bytes_accessed=8 * width * hidden * 4, transcendentals=0
        ),
        name="load_weights",
    )(coords, *flat)


def column_copy(source, target, sems, n):
    cols = pl.ds(pl.multiple_of(n * TILE, TILE), TILE)
    return pltpu.make_async_copy(source.at[:, cols], target.at[:, cols], sems.at[n])


def row_copy(source, target, sems, n):
    rows = pl.ds(pl.multiple_of(n * TILE, TILE), TILE)
    return pltpu.make_async_copy(source.at[rows], target.at[rows], sems.at[n])


def tile_at(n):
    return pl.ds(pl.multiple_of(n * TILE, TILE), TILE)


def gen_body(place_ref, u, low, adapt, *refs):
    slots, (up_in, down_in, up_out, down_out, slope, mine, other) = refs[:6], refs[6:13]
    up, down, last, act, sems, up_sems, down_sems = refs[13:]
    rows = mine.shape[0]
    tiles = up.shape[1] // TILE
    per_quarter = tiles // 2
    pieces = RING * RING
    fetches = {}
    for i in (0, 2, 1):
        for half in range(2):
            n = 2 * i + half
            target = last.at[i, pl.ds(half * 2 * RING, 2 * RING)]
            fetches[n] = pltpu.make_async_copy(slots[n], target, sems.at[n])
    for n in (0, 1, 4, 5):
        fetches[n].start()
    each(tiles, lambda n: column_copy(up_in, up, up_sems, n).start(), 1)
    for n in (2, 3):
        fetches[n].start()
    whole_down = pltpu.make_async_copy(down_in, down, down_sems.at[0])
    whole_down.start()
    for n in (0, 1, 4, 5):
        fetches[n].wait()

    hidden = last.shape[3]

    def hidden_tile(n):
        cols = tile_at(n)
        pre = dot(u[...], up[:, cols]) + dot(low[...], adapt[:, cols])
        value, slope[:, cols] = gelu_and_slope(pre)
        act[:, cols] = value.astype(act.dtype)

    for q in range(2):
        quarter_cols = pl.ds(q * hidden, hidden)
        for n in range(q * per_quarter, (q + 1) * per_quarter):
            column_copy(up_in, up, up_sems, n).wait()

        def place(k, q=q, quarter_cols=quarter_cols):
            for i in (0, 2):
                quarter, row = piece_place(place_ref, i, 3, k)

                @pl.when(quarter == q)
                def _(i=i, row=row):
                    if i == 0:
                        up[pl.ds(row, PIECE), quarter_cols] = last[0, k]
                    else:
                        rest = pl.ds(pl.multiple_of(row + PIECE, 32), REST)
                        up[rest, quarter_cols] = last[2, k, :REST]

        each(pieces, place, 1)
        each(per_quarter, lambda n, q=q: hidden_tile(q * per_quarter + n), 1)
    for n in (2, 3):
        fetches[n].wait()
    whole_down.wait()

    def place_down(k):
        for i in (1, 2):
            quarter, row = piece_place(place_ref, i, 3, k)
            cols = pl.ds(pl.multiple_of(quarter * hidden, 128), hidden)
            if i == 1:
                down[pl.ds(row, PIECE), cols] = last[1, k]
            else:
                down[pl.ds(pl.multiple_of(row + PIECE, 32), REST), cols] = last[2, k, REST:]

    each(pieces, place_down, 1)
    for i in range(3):

        def store(k, i=i):
            quarter, row = piece_place(place_ref, i, 3, k)
            start_piece(i, last.at[i, k], quarter, row, up_out, down_out, sems.at[6 + i])

        each(pieces, store)

    def width_tile(n):
        cols = tile_at(n)
        out = dot(act[...], down[cols, :], NT)
        mine[:, cols] = out[:rows]
        other[:, cols] = out[rows:].astype(other.dtype)

    each(down.shape[0] // TILE, width_tile, 1)
    for i in range(3):
        wait_all(last.at[i], sems.at[6 + i])


def gen_forward(coords, u, low, adapt, slots, up, down):
    group, width = u.shape
    hidden = up.shape[1]
    rows = group // 2
    f32, bf16 = jnp.float32, jnp.bfloat16
    shape = jax.ShapeDtypeStruct((width, hidden), bf16)
    last = [
        slots[half][i][3].reshape(2 * RING, PIECE, hidden // 2) for i in range(3) for half in range(2)
    ]
    return pl.pallas_call(
        gen_body,
        out_shape=(
            shape,
            shape,
            jax.ShapeDtypeStruct((group, hidden), f32),
            jax.ShapeDtypeStruct((rows, width), f32),
            jax.ShapeDtypeStruct((rows, width), bf16),
        ),
        in_specs=[IN_SMEM] + [IN_VMEM] * 3 + [IN_HBM] * 8,
        out_specs=(IN_HBM, IN_HBM) + (IN_VMEM,) * 3,
        scratch_shapes=[
            pltpu.VMEM(shape.shape, bf16),
            pltpu.VMEM(shape.shape, bf16),
            pltpu.VMEM((3, RING * RING, PIECE, hidden // 2), bf16),
            pltpu.VMEM((group, hidden), bf16),
            pltpu.SemaphoreType.DMA((9,)),
            pltpu.SemaphoreType.DMA((hidden // TILE,)),
            pltpu.SemaphoreType.DMA((1,)),
        ],
        input_output_aliases={10: 0, 11: 1},
        compiler_params=pltpu.CompilerParams(vmem_limit_bytes=56 * MIB),
        cost_estimate=pl.CostEstimate(
            flops=4 * group * width * hidden,
            bytes_accessed=50 * MIB,
            transcendentals=group * hidden,
        ),
        name="gen_forward",
    )(coords, u, low, adapt, *last, up, down)


def score_body(
    u_mine, u_other, adapt_in, adapt_out, up_in, down_in, slope, low, real, fake, others, *scratch
):
    u, act, up, down, up_sems, down_sems = scratch
    hidden_tiles, width_tiles = up.shape[1] // TILE, down.shape[0] // TILE
    each(hidden_tiles, lambda n: column_copy(up_in, up, up_sems, n).start(), 1)
    each(width_tiles, lambda n: row_copy(down_in, down, down_sems, n).start(), 1)
    rows = u_mine.shape[0]
    group = 2 * rows
    u[:rows] = u_mine[...]
    u[rows:] = u_other[...]
    low[...] = dot(u[...], adapt_in[...], NT).astype(low.dtype)

    def hidden_tile(n):
        column_copy(up_in, up, up_sems, n).wait()
        cols = tile_at(n)
        pre_real = dot(u[...], up[:, cols])
        pre_fake = pre_real + dot(low[...], adapt_out[:, cols])
        act[:group, cols] = gelu_value(pre_real).astype(act.dtype)
        value, slope[:, cols] = gelu_and_slope(pre_fake)
        act[group:, cols] = value.astype(act.dtype)

    each(hidden_tiles, hidden_tile, 1)

    def width_tile(n):
        row_copy(down_in, down, down_sems, n).wait()
        cols = tile_at(n)
        out = dot(act[...], down[cols, :], NT)
        real[:, cols] = out[:rows]
        others[:rows, cols] = out[rows:group].astype(others.dtype)
        fake[:, cols] = out[group : group + rows]
        others[rows:, cols] = out[group + rows :].astype(others.dtype)

    each(width_tiles, width_tile, 1)


def score_forward(u_mine, u_other, adapt_in, adapt_out, up, down):
    rows, width = u_mine.shape
    hidden = up.shape[1]
    group = 2 * rows
    f32, bf16 = jnp.float32, jnp.bfloat16
    return pl.pallas_call(
        score_body,
        out_shape=(
            jax.ShapeDtypeStruct((group, hidden), f32),
            jax.ShapeDtypeStruct((group, adapt_in.shape[0]), bf16),
            jax.ShapeDtypeStruct((rows, width), f32),
            jax.ShapeDtypeStruct((rows, width), f32),
            jax.ShapeDtypeStruct((group, width), bf16),
        ),
        in_specs=[IN_VMEM] * 4 + [IN_HBM] * 2,
        out_specs=(IN_VMEM,) * 5,
        scratch_shapes=[
            pltpu.VMEM((group, width), bf16),
            pltpu.VMEM((2 * group, hidden), bf16),
            pltpu.VMEM(up.shape, bf16),
            pltpu.VMEM(down.shape, bf16),
            pltpu.SemaphoreType.DMA((hidden // TILE,)),
            pltpu.SemaphoreType.DMA((width // TILE,)),
        ],
        compiler_params=pltpu.CompilerParams(vmem_limit_bytes=56 * MIB),
        cost_estimate=pl.CostEstimate(
            flops=6 * group * width * hidden,
            bytes_accessed=50 * MIB,
            transcendentals=2 * group * hidden,
        ),
        name="score_forward",
    )(u_mine, u_other, adapt_in, adapt_out, up, down)


def back_body(
    cots_mine, cots_other, slope_gen, slope_fake, low_gen, low_fake, gen_out, fake_out, down_in, grads, mix, *scratch
):
    cots, down, sems = scratch
    tiles = down.shape[1] // TILE
    each(tiles, lambda n: column_copy(down_in, down, sems, n).start(), 1)
    group = cots_mine.shape[0]
    rows = group // 2
    for i in range(2):
        cots[i * group : i * group + rows] = cots_mine[i * rows : (i + 1) * rows]
        cots[i * group + rows : (i + 1) * group] = cots_other[i * rows : (i + 1) * rows]
    mix[...] = jnp.zeros_like(mix)

    def hidden_tile(n):
        column_copy(down_in, down, sems, n).wait()
        cols = tile_at(n)
        raw = dot(cots[...], down[:, cols])
        back_gen = (raw[:group] * slope_gen[:, cols]).astype(jnp.bfloat16)
        back_fake = (raw[group:] * slope_fake[:, cols]).astype(jnp.bfloat16)
        grads[0, :, cols] = dot(low_gen[...], back_gen, TN).astype(grads.dtype)
        grads[1, :, cols] = dot(low_fake[...], back_fake, TN).astype(grads.dtype)
        mix[0] += dot(back_gen, gen_out[:, cols], NT)
        mix[1] += dot(back_fake, fake_out[:, cols], NT)

    each(tiles, hidden_tile, 1)


def backward(cots_mine, cots_other, slope_gen, slope_fake, low_gen, low_fake, gen_out, fake_out, down):
    group, width = cots_mine.shape
    hidden = down.shape[1]
    rank = low_gen.shape[1]
    f32, bf16 = jnp.float32, jnp.bfloat16
    return pl.pallas_call(
        back_body,
        out_shape=(
            jax.ShapeDtypeStruct((2, rank, hidden), bf16),
            jax.ShapeDtypeStruct((2, group, rank), f32),
        ),
        in_specs=[IN_VMEM] * 8 + [IN_HBM],
        out_specs=(IN_VMEM,) * 2,
        scratch_shapes=[
            pltpu.VMEM((2 * group, width), bf16),
            pltpu.VMEM(down.shape, bf16),
            pltpu.SemaphoreType.DMA((hidden // TILE,)),
        ],
        compiler_params=pltpu.CompilerParams(vmem_limit_bytes=40 * MIB),
        cost_estimate=pl.CostEstimate(
            flops=4 * group * width * hidden, bytes_accessed=30 * MIB, transcendentals=0
        ),
        name="backward",
    )(cots_mine, cots_other, slope_gen, slope_fake, low_gen, low_fake, gen_out, fake_out, down)


STRIP = 16


def noise_body(ends, blends, given, noise, mine, other, mods, gate, latents_ref, noised_ref, u_ref):
    f32 = jnp.float32

    def strip(n, carry):
        rows = pl.ds(pl.multiple_of(n * STRIP, STRIP), STRIP)
        in_last = n * STRIP + lax.broadcasted_iota(jnp.int32, (STRIP, 1), 0) >= ends[0]
        out = mine[rows] + other[rows].astype(f32)
        latents = (given[rows].astype(f32) + gate[...] * out).astype(latents_ref.dtype)
        latents_ref[rows] = latents
        blend = jnp.where(in_last, blends[1], blends[0])
        noised = (
            (1.0 - blend) * latents.astype(f32) + blend * noise[rows].astype(f32)
        ).astype(noised_ref.dtype)
        noised_ref[rows] = noised
        scale = jnp.where(in_last, mods[1:2], mods[0:1])
        shift = jnp.where(in_last, mods[3:4], mods[2:3])
        u_ref[rows] = modulate(noised, scale, shift)
        return carry

    lax.fori_loop(0, given.shape[0] // STRIP, strip, 0)


def add_noise(ends, blends, given, noise, mine, other, mods, gate):
    shape = jax.ShapeDtypeStruct(given.shape, given.dtype)
    return pl.pallas_call(
        noise_body,
        out_shape=(shape,) * 3,
        in_specs=[IN_SMEM] * 2 + [IN_VMEM] * 6,
        out_specs=(IN_VMEM,) * 3,
        compiler_params=pltpu.CompilerParams(vmem_limit_bytes=10 * MIB),
        cost_estimate=pl.CostEstimate(flops=0, bytes_accessed=6 * MIB, transcendentals=0),
        name="add_noise",
    )(ends, blends, given, noise, mine, other, mods, gate)


def cotangent_body(scale, real, fake, others, gate_ref, noise, latents, noised, diff_ref, cots):
    f32 = jnp.float32
    count = real.shape[0]

    def strip(n, carry):
        start = pl.multiple_of(n * STRIP, STRIP)
        rows, second = pl.ds(start, STRIP), pl.ds(count + start, STRIP)
        gate = gate_ref[...]
        out_real = real[rows] + others[rows].astype(f32)
        out_fake = fake[rows] + others[second].astype(f32)
        diff = (gate * (out_fake - out_real)).astype(diff_ref.dtype)
        diff_ref[rows] = diff
        cots[rows] = (gate * diff.astype(f32) * scale).astype(cots.dtype)
        target = noise[rows].astype(f32) - latents[rows].astype(f32)
        cots[second] = (
            gate * (noised[rows].astype(f32) + gate * out_fake - target) * scale
        ).astype(cots.dtype)
        return carry

    lax.fori_loop(0, count // STRIP, strip, 0)


def cotangents(scale, real, fake, others, gate, noise, latents, noised):
    rows, width = real.shape
    return pl.pallas_call(
        functools.partial(cotangent_body, scale),
        out_shape=(
            jax.ShapeDtypeStruct((rows, width), noise.dtype),
            jax.ShapeDtypeStruct((2 * rows, width), noise.dtype),
        ),
        in_specs=[IN_VMEM] * 7,
        out_specs=(IN_VMEM,) * 2,
        compiler_params=pltpu.CompilerParams(vmem_limit_bytes=12 * MIB),
        cost_estimate=pl.CostEstimate(flops=0, bytes_accessed=8 * MIB, transcendentals=0),
        name="cotangents",
    )(real, fake, others, gate, noise, latents, noised)


def three_terms(value):
    high = lax.reduce_precision(value, 8, 7)
    rest = value - high
    middle = lax.reduce_precision(rest, 8, 7)
    low = rest - middle
    return jnp.concatenate([high, middle, low], axis=1).astype(jnp.bfloat16)


def local(
    gen_input,
    noise_score,
    gen_steps,
    score_steps,
    base_up,
    base_down,
    gen_adapt_in,
    gen_adapt_out,
    fake_adapt_in,
    fake_adapt_out,
    modulation_scale,
    modulation_shift,
    output_gate,
):
    bf16, f32 = jnp.bfloat16, jnp.float32
    shard_rows, width = gen_input.shape
    hidden = base_up.shape[1]
    rank = gen_adapt_in.shape[1]
    image_count = gen_steps.shape[0]
    loss_scale = 1.0 / math.sqrt(image_count * IMG_TOK)
    core = lax.axis_index("core")
    xl = lax.axis_index("xl")
    first_row = lax.axis_index(AXES) * shard_rows
    first_image = first_row // IMG_TOK
    last_image = (first_row + shard_rows - 1) // IMG_TOK
    row_ids = first_row + jnp.arange(shard_rows, dtype=jnp.int32)
    in_last = (row_ids >= last_image * IMG_TOK)[:, None]

    def two_steps(steps):
        return jnp.stack([steps[first_image], steps[last_image]])

    def modulation(steps):
        embed = embedding(two_steps(steps), width)
        return 1.0 + modulation_scale[None, :] * embed, modulation_shift[None, :] * embed

    def both_rows(mine):
        return jnp.concatenate([mine, swap_cores(mine)], axis=0)

    def both_quarters(mine):
        theirs = lax.ppermute(mine, "xl", [(0, 1), (1, 0)])
        quarters = [jnp.where(xl == 0, mine, theirs), jnp.where(xl == 0, theirs, mine)]
        return jnp.concatenate(quarters, axis=1)

    def prepare(given, gen_steps, score_steps):
        gen_scale, gen_shift = modulation(gen_steps)
        u_mine = modulate(
            given,
            jnp.where(in_last, gen_scale[1:], gen_scale[:1]),
            jnp.where(in_last, gen_shift[1:], gen_shift[:1]),
        )
        u_gen = both_rows(u_mine)
        low_gen = matmul(u_gen, gen_adapt_in).astype(bf16)
        mods = jnp.concatenate(modulation(score_steps), axis=0)
        blends = (two_steps(score_steps).astype(f32) + 0.5) / 1000.0
        ends = (last_image * IMG_TOK - first_row).astype(jnp.int32).reshape(1)
        place = [lax.axis_index("z"), lax.axis_index("y"), lax.axis_index("xh") * 2 + xl, 1 - 2 * core]
        return u_gen, low_gen, mods, blends, ends, jnp.stack(place).astype(jnp.int32)

    down_rows = base_down.T
    slots, adapt_out, prepared = ring_slots(
        [
            base_up[:PIECE],
            down_rows[:PIECE],
            jnp.concatenate([base_up[PIECE:], down_rows[PIECE:]], axis=0),
        ],
        jnp.concatenate([gen_adapt_out, fake_adapt_out], axis=0),
        both_quarters,
        (gen_input, gen_steps, score_steps),
        prepare,
    )
    u_gen, low_gen, mods, blends, ends, coords = prepared
    gen_out, fake_out = adapt_out[:rank], adapt_out[rank:]
    up_part, down_part = load_weights(coords, slots, width, hidden)

    up_all, down_all, slope_gen, out_mine, out_other = gen_forward(
        coords, u_gen, low_gen, gen_out, slots, up_part, down_part
    )
    gate = output_gate.reshape(1, width)
    latents, noised, u_score = add_noise(
        ends, blends, gen_input, noise_score, out_mine, swap_cores(out_other), mods, gate
    )
    u_score_other = swap_cores(u_score)
    slope_fake, low_fake, out_real, out_fake, outs_other = score_forward(
        u_score, u_score_other, fake_adapt_in.T, fake_out, up_all, down_all
    )
    score_diff, cots = cotangents(
        loss_scale, out_real, out_fake, swap_cores(outs_other), gate, noise_score, latents, noised
    )
    out_grads, mix = backward(
        cots, swap_cores(cots), slope_gen, slope_fake, low_gen, low_fake, gen_out, fake_out, down_all
    )
    mix = jnp.concatenate([mix[0], mix[1]], axis=1)
    mix_other = swap_cores(mix)
    mix = mix + jnp.concatenate([mix_other[shard_rows:], mix_other[:shard_rows]], axis=0)

    def in_grad(u, mix_part):
        product = contract(u, three_terms(mix_part), 0, 0)
        total = product[:, :rank] + product[:, rank : 2 * rank] + product[:, 2 * rank :]
        chips = total.reshape(-1, 2, width // 128, rank)
        return jnp.where(core == 0, chips[:, 0], chips[:, 1])

    u_score_group = jnp.concatenate([u_score, u_score_other], axis=0)
    in_grads = jnp.concatenate(
        [in_grad(u_gen, mix[:, :rank]), in_grad(u_score_group, mix[:, rank:])], axis=2
    )
    chips, in_rows = in_grads.shape[0], in_grads.shape[1]
    groups = chips // 2
    out_grads = out_grads.reshape(2, groups, rank // groups, 2, hidden).transpose(1, 3, 0, 2, 4)
    out_rows = 2 * (rank // groups) * hidden // 128
    packed = jnp.concatenate(
        [in_grads.astype(bf16), out_grads.reshape(chips, out_rows, 128)], axis=1
    )
    received = lax.all_to_all(packed, CHIPS, 0, 0, tiled=True)
    summed = jnp.sum(received.astype(f32), axis=0)
    gen_grad_in, fake_grad_in = summed[:in_rows, :rank], summed[:in_rows, rank:]
    grads_out = summed[in_rows:].reshape(2, rank // groups, hidden)
    return (score_diff, gen_grad_in, grads_out[0], fake_grad_in, grads_out[1])


def solution(mesh):
    fine = Mesh(mesh.devices.reshape(4, 4, 2, 2, 2), AXES)
    dp, mp = ("z", "y", "xh"), ("xl", "core")
    return jax.shard_map(
        local,
        mesh=fine,
        in_specs=(
            P(AXES, None),
            P(AXES, None),
            P(),
            P(),
            P(dp, mp),
            P(mp, dp),
            P(),
            P(None, mp),
            P(),
            P(None, mp),
            P(),
            P(),
            P(),
        ),
        out_specs=(
            P(AXES, None),
            P(AXES, None),
            P(dp, mp),
            P(AXES, None),
            P(dp, mp),
        ),
        check_vma=False,
    )
```

```python
import functools
import math

import jax
import jax.numpy as jnp
from jax import lax
from jax.experimental import pallas as pl
from jax.experimental.pallas import tpu as pltpu
from jax.sharding import Mesh
from jax.sharding import PartitionSpec as P

IMG_TOK = 1024
AXES = ("z", "y", "xh", "xl", "core")
CHIPS = ("z", "y", "xh", "xl")

gelu_coef = 0.044715
root_two_pi = math.sqrt(2.0 / math.pi)


def gelu_value(pre):
    inner_arg = root_two_pi * (pre + gelu_coef * pre * pre * pre)
    return 0.5 * pre * (1.0 + jnp.tanh(inner_arg))


def gelu_slope(pre):
    tanh_val = jnp.tanh(root_two_pi * (pre + gelu_coef * pre * pre * pre))
    return 0.5 * (1.0 + tanh_val) + 0.5 * pre * (1.0 - tanh_val * tanh_val) * root_two_pi * (
        1.0 + 3.0 * gelu_coef * pre * pre
    )


def modulate(rows, scale_rows, shift_rows):
    widened = rows.astype(jnp.float32)
    normed = widened * lax.rsqrt(jnp.mean(widened * widened, axis=1, keepdims=True) + 1e-06)
    return (normed * scale_rows + shift_rows).astype(jnp.bfloat16)


def matmul(left, right):
    return jnp.dot(left, right, preferred_element_type=jnp.float32)


def contract(left, right, left_dim, right_dim):
    return lax.dot_general(
        left, right, (((left_dim,), (right_dim,)), ((), ())), preferred_element_type=jnp.float32
    )


def swap_cores(value):
    return lax.ppermute(value, "core", [(0, 1), (1, 0)])


RING_AXES = (("y", "z", "x"), ("z", "x", "y"), ("x", "y", "z"))
RING = 4


def chip_ring(axis):
    pairs = []
    for device in range(128):
        place = {"z": device // 32, "y": device // 8 % 4, "x": device // 2 % 4, "core": device % 2}
        step = 1 if place["core"] == 0 else -1
        place[axis] = (place[axis] + step) % RING
        target = place["z"] * 32 + place["y"] * 8 + place["x"] * 2 + place["core"]
        pairs.append((device, target))
    return pairs


def send(piece, i, phase):
    return lax.ppermute(piece, AXES, chip_ring(RING_AXES[i][phase]))


def gathered(pieces, phase):
    rows = pieces[0].shape[0]
    whole = [jnp.zeros((RING * rows, piece.shape[1]), piece.dtype) for piece in pieces]
    for step in range(RING):
        if step:
            pieces = [send(piece, i, phase) for i, piece in enumerate(pieces)]
        whole = [
            lax.dynamic_update_slice(buffer, piece, (step * rows, 0))
            for buffer, piece in zip(whole, pieces)
        ]
    return whole


def ring_slots(pieces, adapters, exchange, inputs, prepare):
    pieces = gathered(pieces, 0)
    pieces[2], adapters = lax.optimization_barrier((pieces[2], adapters))
    exchanged = exchange(adapters)
    pieces = gathered(pieces, 1)
    pieces[2], exchanged = lax.optimization_barrier((pieces[2], exchanged))
    slots = [[piece] for piece in pieces]
    for step in range(1, RING):
        if step == RING - 1:
            slots[2][-1], prepared = lax.optimization_barrier((slots[2][-1], prepared))
        for i in range(3):
            slots[i].append(send(slots[i][-1], i, 2))
        if step == 1:
            arrived = [slots[i][1] for i in range(3)]
            _, inputs = lax.optimization_barrier((arrived, inputs))
            prepared = prepare(*inputs)
    return slots, exchanged, prepared


SHARD = 96
PIECE = 64
REST = SHARD - PIECE
TILE = 512
MIB = 2**20
ANYWHERE = pl.BlockSpec(memory_space=pl.ANY)
IN_VMEM = pl.BlockSpec(memory_space=pltpu.VMEM)
IN_SMEM = pl.BlockSpec(memory_space=pltpu.SMEM)
NT = (((1,), (1,)), ((), ()))
TN = (((0,), (0,)), ((), ()))


def dot(left, right, dims=(((1,), (0,)), ((), ()))):
    return lax.dot_general(left, right, dims, preferred_element_type=jnp.float32)


def gelu_and_slope(pre):
    square = pre * pre
    tanh_val = jnp.tanh(root_two_pi * (pre + gelu_coef * square * pre))
    half = 0.5 * (1.0 + tanh_val)
    slope = half + 0.5 * pre * (1.0 - tanh_val * tanh_val) * root_two_pi * (
        1.0 + 3.0 * gelu_coef * square
    )
    return pre * half, slope


IN_HBM = pl.BlockSpec(memory_space=pltpu.HBM)


def piece_place(place_ref, i, step, k):
    me = {"z": place_ref[0], "y": place_ref[1], "x": place_ref[2]}
    direction = place_ref[3]
    first, second, third = RING_AXES[i]

    def source(axis, distance):
        return (me[axis] - distance * direction + RING) & (RING - 1)

    zero = k - k
    at = {
        first: source(first, k & (RING - 1)),
        second: source(second, k >> 2),
        third: source(third, step + zero),
    }
    group = (at["z"] * 4 + at["y"]) * 2 + (at["x"] >> 1)
    return at["x"] & 1, group * SHARD


def each(count, one, unroll=4):
    def step(k, carry):
        one(k)
        return carry

    lax.fori_loop(0, count, step, 0, unroll=unroll)


def wait_all(ref, sem):
    pltpu.make_async_copy(ref, ref, sem).wait()


def start_piece(i, source, quarter, row, up, down, sem):
    hidden = source.shape[1]
    cols = pl.ds(pl.multiple_of(quarter * hidden, 128), hidden)
    if i < 2:
        target = (up, down)[i].at[pl.ds(row, PIECE), cols]
        pltpu.make_async_copy(source, target, sem).start()
    else:
        for n, matrix in enumerate((up, down)):
            rows = pl.ds(pl.multiple_of(row + PIECE, 32), REST)
            pltpu.make_async_copy(source.at[pl.ds(n * REST, REST)], matrix.at[rows, cols], sem).start()


def load_body(place_ref, *refs):
    slots, (up_out, down_out, up, down, sems) = refs[:9], refs[9:]
    for n, slot in enumerate(slots):
        step, i = n // 3, n % 3

        def one(k, slot=slot, step=step, i=i, n=n):
            quarter, row = piece_place(place_ref, i, step, k)
            start_piece(i, slot.at[k], quarter, pl.multiple_of(row, 32), up, down, sems.at[n])

        each(RING * RING, one)
    for n, slot in enumerate(slots):
        if n % 3 != 1:
            wait_all(slot, sems.at[n])
    up_copy = pltpu.make_async_copy(up, up_out, sems.at[9])
    up_copy.start()
    for n, slot in enumerate(slots):
        if n % 3 == 1:
            wait_all(slot, sems.at[n])
    down_copy = pltpu.make_async_copy(down, down_out, sems.at[10])
    down_copy.start()
    up_copy.wait()
    down_copy.wait()


def load_weights(coords, slots, width, hidden):
    flat = [
        slots[i][step].reshape(RING * RING, PIECE, hidden) for step in range(3) for i in range(3)
    ]
    shape = jax.ShapeDtypeStruct((width, 2 * hidden), jnp.bfloat16)
    return pl.pallas_call(
        load_body,
        out_shape=(shape, shape),
        in_specs=[IN_SMEM] + [IN_HBM] * 9,
        out_specs=(IN_HBM, IN_HBM),
        scratch_shapes=[
            pltpu.VMEM(shape.shape, shape.dtype),
            pltpu.VMEM(shape.shape, shape.dtype),
            pltpu.SemaphoreType.DMA((11,)),
        ],
        compiler_params=pltpu.CompilerParams(vmem_limit_bytes=40 * MIB),
        cost_estimate=pl.CostEstimate(
            flops=0, bytes_accessed=8 * width * hidden * 4, transcendentals=0
        ),
        name="load_weights",
    )(coords, *flat)


def column_copy(source, target, sems, n):
    cols = pl.ds(pl.multiple_of(n * TILE, TILE), TILE)
    return pltpu.make_async_copy(source.at[:, cols], target.at[:, cols], sems.at[n])


def row_copy(source, target, sems, n):
    rows = pl.ds(pl.multiple_of(n * TILE, TILE), TILE)
    return pltpu.make_async_copy(source.at[rows], target.at[rows], sems.at[n])


def tile_at(n):
    return pl.ds(pl.multiple_of(n * TILE, TILE), TILE)


def gen_body(table, u_mine, u_other, adapt_in, adapt, *refs):
    slots, (up_in, down_in, up_out, down_out, slope, low, mine, other) = refs[:3], refs[3:11]
    up, down, last, u, act, sems, up_sems, down_sems = refs[11:]
    rows = mine.shape[0]
    tiles = up.shape[1] // TILE
    per_quarter = tiles // 2
    pieces = RING * RING
    fetches = [pltpu.make_async_copy(slots[i], last.at[i], sems.at[i]) for i in range(3)]
    fetches[0].start()
    fetches[2].start()
    each(tiles, lambda n: column_copy(up_in, up, up_sems, n).start(), 1)
    fetches[1].start()
    whole_down = pltpu.make_async_copy(down_in, down, down_sems.at[0])
    whole_down.start()
    u[:rows] = u_mine[...]
    u[rows:] = u_other[...]
    low[...] = dot(u[...], adapt_in[...], NT).astype(low.dtype)
    fetches[0].wait()
    fetches[2].wait()

    def spot(i, k):
        return table[0, i * pieces + k], pl.multiple_of(table[1, i * pieces + k], 32)

    hidden = last.shape[3]

    def hidden_tile(n):
        cols = tile_at(n)
        pre = dot(u[...], up[:, cols]) + dot(low[...], adapt[:, cols])
        value, slope[:, cols] = gelu_and_slope(pre)
        act[:, cols] = value.astype(act.dtype)

    for q in range(2):
        quarter_cols = pl.ds(q * hidden, hidden)
        for n in range(q * per_quarter, (q + 1) * per_quarter):
            column_copy(up_in, up, up_sems, n).wait()

        def place(k, q=q, quarter_cols=quarter_cols):
            for i in (0, 2):
                quarter, row = spot(i, k)

                @pl.when(quarter == q)
                def _(i=i, row=row):
                    if i == 0:
                        up[pl.ds(row, PIECE), quarter_cols] = last[0, k]
                    else:
                        rest = pl.ds(pl.multiple_of(row + PIECE, 32), REST)
                        up[rest, quarter_cols] = last[2, k, :REST]

        each(pieces, place, 2)
        each(per_quarter, lambda n, q=q: hidden_tile(q * per_quarter + n), 1)
    fetches[1].wait()
    whole_down.wait()

    def place_down(k):
        for i in (1, 2):
            quarter, row = spot(i, k)
            cols = pl.ds(pl.multiple_of(quarter * hidden, 128), hidden)
            if i == 1:
                down[pl.ds(row, PIECE), cols] = last[1, k]
            else:
                down[pl.ds(pl.multiple_of(row + PIECE, 32), REST), cols] = last[2, k, REST:]

    each(pieces, place_down, 4)
    for i in range(3):

        def store(k, i=i):
            quarter, row = spot(i, k)
            start_piece(i, last.at[i, k], quarter, row, up_out, down_out, sems.at[3 + i])

        each(pieces, store)

    def width_tile(n):
        cols = tile_at(n)
        out = dot(act[...], down[cols, :], NT)
        mine[:, cols] = out[:rows]
        other[:, cols] = out[rows:].astype(other.dtype)

    each(down.shape[0] // TILE, width_tile, 1)
    for i in range(3):
        wait_all(last.at[i], sems.at[3 + i])


def gen_forward(table, u_mine, u_other, adapt_in, adapt, slots, up, down):
    rows, width = u_mine.shape
    hidden = up.shape[1]
    group = 2 * rows
    f32, bf16 = jnp.float32, jnp.bfloat16
    shape = jax.ShapeDtypeStruct((width, hidden), bf16)
    last = [slots[i][3].reshape(RING * RING, PIECE, hidden // 2) for i in range(3)]
    return pl.pallas_call(
        gen_body,
        out_shape=(
            shape,
            shape,
            jax.ShapeDtypeStruct((group, hidden), f32),
            jax.ShapeDtypeStruct((group, adapt_in.shape[0]), bf16),
            jax.ShapeDtypeStruct((rows, width), f32),
            jax.ShapeDtypeStruct((rows, width), bf16),
        ),
        in_specs=[IN_SMEM] + [IN_VMEM] * 4 + [IN_HBM] * 5,
        out_specs=(IN_HBM, IN_HBM) + (IN_VMEM,) * 4,
        scratch_shapes=[
            pltpu.VMEM(shape.shape, bf16),
            pltpu.VMEM(shape.shape, bf16),
            pltpu.VMEM((3, RING * RING, PIECE, hidden // 2), bf16),
            pltpu.VMEM((group, width), bf16),
            pltpu.VMEM((group, hidden), bf16),
            pltpu.SemaphoreType.DMA((6,)),
            pltpu.SemaphoreType.DMA((hidden // TILE,)),
            pltpu.SemaphoreType.DMA((1,)),
        ],
        input_output_aliases={8: 0, 9: 1},
        compiler_params=pltpu.CompilerParams(vmem_limit_bytes=57 * MIB),
        cost_estimate=pl.CostEstimate(
            flops=4 * group * width * hidden,
            bytes_accessed=50 * MIB,
            transcendentals=group * hidden,
        ),
        name="gen_forward",
    )(table, u_mine, u_other, adapt_in, adapt, *last, up, down)


def score_body(
    u_mine, u_other, adapt_in, adapt_out, up_in, down_in, slope, low, real, fake, others, *scratch
):
    u, act, up, down, up_sems, down_sems = scratch
    hidden_tiles, width_tiles = up.shape[1] // TILE, down.shape[0] // TILE
    each(hidden_tiles, lambda n: column_copy(up_in, up, up_sems, n).start(), 1)
    each(width_tiles, lambda n: row_copy(down_in, down, down_sems, n).start(), 1)
    rows = u_mine.shape[0]
    group = 2 * rows
    u[:rows] = u_mine[...]
    u[rows:] = u_other[...]
    low[...] = dot(u[...], adapt_in[...], NT).astype(low.dtype)

    def hidden_tile(n):
        column_copy(up_in, up, up_sems, n).wait()
        cols = tile_at(n)
        pre_real = dot(u[...], up[:, cols])
        pre_fake = pre_real + dot(low[...], adapt_out[:, cols])
        act[:group, cols] = gelu_value(pre_real).astype(act.dtype)
        value, slope[:, cols] = gelu_and_slope(pre_fake)
        act[group:, cols] = value.astype(act.dtype)

    each(hidden_tiles, hidden_tile, 1)

    def width_tile(n):
        row_copy(down_in, down, down_sems, n).wait()
        cols = tile_at(n)
        out = dot(act[...], down[cols, :], NT)
        real[:, cols] = out[:rows]
        others[:rows, cols] = out[rows:group].astype(others.dtype)
        fake[:, cols] = out[group : group + rows]
        others[rows:, cols] = out[group + rows :].astype(others.dtype)

    each(width_tiles, width_tile, 1)


def score_forward(u_mine, u_other, adapt_in, adapt_out, up, down):
    rows, width = u_mine.shape
    hidden = up.shape[1]
    group = 2 * rows
    f32, bf16 = jnp.float32, jnp.bfloat16
    return pl.pallas_call(
        score_body,
        out_shape=(
            jax.ShapeDtypeStruct((group, hidden), f32),
            jax.ShapeDtypeStruct((group, adapt_in.shape[0]), bf16),
            jax.ShapeDtypeStruct((rows, width), f32),
            jax.ShapeDtypeStruct((rows, width), f32),
            jax.ShapeDtypeStruct((group, width), bf16),
        ),
        in_specs=[IN_VMEM] * 4 + [IN_HBM] * 2,
        out_specs=(IN_VMEM,) * 5,
        scratch_shapes=[
            pltpu.VMEM((group, width), bf16),
            pltpu.VMEM((2 * group, hidden), bf16),
            pltpu.VMEM(up.shape, bf16),
            pltpu.VMEM(down.shape, bf16),
            pltpu.SemaphoreType.DMA((hidden // TILE,)),
            pltpu.SemaphoreType.DMA((width // TILE,)),
        ],
        compiler_params=pltpu.CompilerParams(vmem_limit_bytes=56 * MIB),
        cost_estimate=pl.CostEstimate(
            flops=6 * group * width * hidden,
            bytes_accessed=50 * MIB,
            transcendentals=2 * group * hidden,
        ),
        name="score_forward",
    )(u_mine, u_other, adapt_in, adapt_out, up, down)


def back_body(
    cots_mine, cots_other, slope_gen, slope_fake, low_gen, low_fake, gen_out, fake_out, down_in, grads, mix, *scratch
):
    cots, down, sems = scratch
    tiles = down.shape[1] // TILE
    each(tiles, lambda n: column_copy(down_in, down, sems, n).start(), 1)
    group = cots_mine.shape[0]
    rows = group // 2
    for i in range(2):
        cots[i * group : i * group + rows] = cots_mine[i * rows : (i + 1) * rows]
        cots[i * group + rows : (i + 1) * group] = cots_other[i * rows : (i + 1) * rows]
    mix[...] = jnp.zeros_like(mix)

    def hidden_tile(n):
        column_copy(down_in, down, sems, n).wait()
        cols = tile_at(n)
        raw = dot(cots[...], down[:, cols])
        back_gen = (raw[:group] * slope_gen[:, cols]).astype(jnp.bfloat16)
        back_fake = (raw[group:] * slope_fake[:, cols]).astype(jnp.bfloat16)
        grads[0, :, cols] = dot(low_gen[...], back_gen, TN).astype(grads.dtype)
        grads[1, :, cols] = dot(low_fake[...], back_fake, TN).astype(grads.dtype)
        mix[0] += dot(back_gen, gen_out[:, cols], NT)
        mix[1] += dot(back_fake, fake_out[:, cols], NT)

    each(tiles, hidden_tile, 1)


def backward(cots_mine, cots_other, slope_gen, slope_fake, low_gen, low_fake, gen_out, fake_out, down):
    group, width = cots_mine.shape
    hidden = down.shape[1]
    rank = low_gen.shape[1]
    f32, bf16 = jnp.float32, jnp.bfloat16
    return pl.pallas_call(
        back_body,
        out_shape=(
            jax.ShapeDtypeStruct((2, rank, hidden), bf16),
            jax.ShapeDtypeStruct((2, group, rank), f32),
        ),
        in_specs=[IN_VMEM] * 8 + [IN_HBM],
        out_specs=(IN_VMEM,) * 2,
        scratch_shapes=[
            pltpu.VMEM((2 * group, width), bf16),
            pltpu.VMEM(down.shape, bf16),
            pltpu.SemaphoreType.DMA((hidden // TILE,)),
        ],
        compiler_params=pltpu.CompilerParams(vmem_limit_bytes=40 * MIB),
        cost_estimate=pl.CostEstimate(
            flops=4 * group * width * hidden, bytes_accessed=30 * MIB, transcendentals=0
        ),
        name="backward",
    )(cots_mine, cots_other, slope_gen, slope_fake, low_gen, low_fake, gen_out, fake_out, down)


STRIP = 16


def embed_body(ends, steps, given, scale_ref, shift_ref, u_ref, mods_ref):
    half = given.shape[1] // 2
    place = lax.broadcasted_iota(jnp.int32, (1, half), 1).astype(jnp.float32)
    frequency = jnp.exp(-math.log(10000.0) * place / half)
    row = lax.broadcasted_iota(jnp.int32, (4, 1), 0)
    column = jnp.where(
        row < 2, jnp.where(row == 0, steps[0], steps[1]), jnp.where(row == 2, steps[2], steps[3])
    )
    phase = column * frequency
    embed = jnp.concatenate([jnp.sin(phase), jnp.cos(phase)], axis=1)
    scale = 1.0 + scale_ref[...] * embed
    shift = shift_ref[...] * embed
    mods_ref[0:2] = scale[2:4]
    mods_ref[2:4] = shift[2:4]

    def strip(n, carry):
        rows = pl.ds(pl.multiple_of(n * STRIP, STRIP), STRIP)
        in_last = n * STRIP + lax.broadcasted_iota(jnp.int32, (STRIP, 1), 0) >= ends[0]
        u_ref[rows] = modulate(
            given[rows],
            jnp.where(in_last, scale[1:2], scale[0:1]),
            jnp.where(in_last, shift[1:2], shift[0:1]),
        )
        return carry

    lax.fori_loop(0, given.shape[0] // STRIP, strip, 0)


def first_modulation(ends, steps, given, scale, shift):
    width = given.shape[1]
    return pl.pallas_call(
        embed_body,
        out_shape=(
            jax.ShapeDtypeStruct(given.shape, given.dtype),
            jax.ShapeDtypeStruct((4, width), jnp.float32),
        ),
        in_specs=[IN_SMEM] * 2 + [IN_VMEM] * 3,
        out_specs=(IN_VMEM,) * 2,
        compiler_params=pltpu.CompilerParams(vmem_limit_bytes=8 * MIB),
        cost_estimate=pl.CostEstimate(flops=0, bytes_accessed=2 * MIB, transcendentals=0),
        name="first_modulation",
    )(ends, steps, given, scale.reshape(1, width), shift.reshape(1, width))


def noise_body(ends, blends, given, noise, mine, other, mods, gate, latents_ref, noised_ref, u_ref):
    f32 = jnp.float32

    def strip(n, carry):
        rows = pl.ds(pl.multiple_of(n * STRIP, STRIP), STRIP)
        in_last = n * STRIP + lax.broadcasted_iota(jnp.int32, (STRIP, 1), 0) >= ends[0]
        out = mine[rows] + other[rows].astype(f32)
        latents = (given[rows].astype(f32) + gate[...] * out).astype(latents_ref.dtype)
        latents_ref[rows] = latents
        blend = jnp.where(in_last, blends[1], blends[0])
        noised = (
            (1.0 - blend) * latents.astype(f32) + blend * noise[rows].astype(f32)
        ).astype(noised_ref.dtype)
        noised_ref[rows] = noised
        scale = jnp.where(in_last, mods[1:2], mods[0:1])
        shift = jnp.where(in_last, mods[3:4], mods[2:3])
        u_ref[rows] = modulate(noised, scale, shift)
        return carry

    lax.fori_loop(0, given.shape[0] // STRIP, strip, 0)


def add_noise(ends, blends, given, noise, mine, other, mods, gate):
    shape = jax.ShapeDtypeStruct(given.shape, given.dtype)
    return pl.pallas_call(
        noise_body,
        out_shape=(shape,) * 3,
        in_specs=[IN_SMEM] * 2 + [IN_VMEM] * 6,
        out_specs=(IN_VMEM,) * 3,
        compiler_params=pltpu.CompilerParams(vmem_limit_bytes=10 * MIB),
        cost_estimate=pl.CostEstimate(flops=0, bytes_accessed=6 * MIB, transcendentals=0),
        name="add_noise",
    )(ends, blends, given, noise, mine, other, mods, gate)


def cotangent_body(scale, real, fake, others, gate_ref, noise, latents, noised, diff_ref, cots):
    f32 = jnp.float32
    count = real.shape[0]

    def strip(n, carry):
        start = pl.multiple_of(n * STRIP, STRIP)
        rows, second = pl.ds(start, STRIP), pl.ds(count + start, STRIP)
        gate = gate_ref[...]
        out_real = real[rows] + others[rows].astype(f32)
        out_fake = fake[rows] + others[second].astype(f32)
        diff = (gate * (out_fake - out_real)).astype(diff_ref.dtype)
        diff_ref[rows] = diff
        cots[rows] = (gate * diff.astype(f32) * scale).astype(cots.dtype)
        target = noise[rows].astype(f32) - latents[rows].astype(f32)
        cots[second] = (
            gate * (noised[rows].astype(f32) + gate * out_fake - target) * scale
        ).astype(cots.dtype)
        return carry

    lax.fori_loop(0, count // STRIP, strip, 0)


def cotangents(scale, real, fake, others, gate, noise, latents, noised):
    rows, width = real.shape
    return pl.pallas_call(
        functools.partial(cotangent_body, scale),
        out_shape=(
            jax.ShapeDtypeStruct((rows, width), noise.dtype),
            jax.ShapeDtypeStruct((2 * rows, width), noise.dtype),
        ),
        in_specs=[IN_VMEM] * 7,
        out_specs=(IN_VMEM,) * 2,
        compiler_params=pltpu.CompilerParams(vmem_limit_bytes=12 * MIB),
        cost_estimate=pl.CostEstimate(flops=0, bytes_accessed=8 * MIB, transcendentals=0),
        name="cotangents",
    )(real, fake, others, gate, noise, latents, noised)


def three_terms(value):
    high = lax.reduce_precision(value, 8, 7)
    rest = value - high
    middle = lax.reduce_precision(rest, 8, 7)
    low = rest - middle
    return jnp.concatenate([high, middle, low], axis=1).astype(jnp.bfloat16)


def local(
    gen_input,
    noise_score,
    gen_steps,
    score_steps,
    base_up,
    base_down,
    gen_adapt_in,
    gen_adapt_out,
    fake_adapt_in,
    fake_adapt_out,
    modulation_scale,
    modulation_shift,
    output_gate,
):
    bf16, f32 = jnp.bfloat16, jnp.float32
    shard_rows, width = gen_input.shape
    hidden = base_up.shape[1]
    rank = gen_adapt_in.shape[1]
    image_count = gen_steps.shape[0]
    loss_scale = 1.0 / math.sqrt(image_count * IMG_TOK)
    core = lax.axis_index("core")
    xl = lax.axis_index("xl")
    first_row = lax.axis_index(AXES) * shard_rows
    first_image = first_row // IMG_TOK
    last_image = (first_row + shard_rows - 1) // IMG_TOK
    def two_steps(steps):
        return jnp.stack([steps[first_image], steps[last_image]])

    def both_quarters(mine):
        theirs = lax.ppermute(mine, "xl", [(0, 1), (1, 0)])
        quarters = [jnp.where(xl == 0, mine, theirs), jnp.where(xl == 0, theirs, mine)]
        return jnp.concatenate(quarters, axis=1)

    blends = (two_steps(score_steps).astype(f32) + 0.5) / 1000.0
    ends = (last_image * IMG_TOK - first_row).astype(jnp.int32).reshape(1)
    steps = jnp.concatenate([two_steps(gen_steps), two_steps(score_steps)]).astype(f32)
    place = [lax.axis_index("z"), lax.axis_index("y"), lax.axis_index("xh") * 2 + xl, 1 - 2 * core]
    coords = jnp.stack(place).astype(jnp.int32)
    spots = [piece_place(coords, i, 3, jnp.arange(RING * RING, dtype=jnp.int32)) for i in range(3)]
    table = jnp.stack([jnp.concatenate([spot[n] for spot in spots]) for n in range(2)])

    def prepare(given):
        u_mine, mods = first_modulation(ends, steps, given, modulation_scale, modulation_shift)
        return u_mine, swap_cores(u_mine), mods

    down_rows = base_down.T
    slots, adapt_out, prepared = ring_slots(
        [
            base_up[:PIECE],
            down_rows[:PIECE],
            jnp.concatenate([base_up[PIECE:], down_rows[PIECE:]], axis=0),
        ],
        jnp.concatenate([gen_adapt_out, fake_adapt_out], axis=0),
        both_quarters,
        (gen_input,),
        prepare,
    )
    u_gen, u_gen_other, mods = prepared
    gen_out, fake_out = adapt_out[:rank], adapt_out[rank:]
    up_part, down_part = load_weights(coords, slots, width, hidden)

    up_all, down_all, slope_gen, low_gen, out_mine, out_other = gen_forward(
        table, u_gen, u_gen_other, gen_adapt_in.T, gen_out, slots, up_part, down_part
    )
    gate = output_gate.reshape(1, width)
    latents, noised, u_score = add_noise(
        ends, blends, gen_input, noise_score, out_mine, swap_cores(out_other), mods, gate
    )
    u_score_other = swap_cores(u_score)
    slope_fake, low_fake, out_real, out_fake, outs_other = score_forward(
        u_score, u_score_other, fake_adapt_in.T, fake_out, up_all, down_all
    )
    score_diff, cots = cotangents(
        loss_scale, out_real, out_fake, swap_cores(outs_other), gate, noise_score, latents, noised
    )
    out_grads, mix = backward(
        cots, swap_cores(cots), slope_gen, slope_fake, low_gen, low_fake, gen_out, fake_out, down_all
    )
    mix = jnp.concatenate([mix[0], mix[1]], axis=1)
    mix_other = swap_cores(mix)
    mix = mix + jnp.concatenate([mix_other[shard_rows:], mix_other[:shard_rows]], axis=0)

    def in_grad(u, mix_part):
        product = contract(u, three_terms(mix_part), 0, 0)
        total = product[:, :rank] + product[:, rank : 2 * rank] + product[:, 2 * rank :]
        chips = total.reshape(-1, 2, width // 128, rank)
        return jnp.where(core == 0, chips[:, 0], chips[:, 1])

    u_gen_group = jnp.concatenate([u_gen, u_gen_other], axis=0)
    u_score_group = jnp.concatenate([u_score, u_score_other], axis=0)
    in_grads = jnp.concatenate(
        [in_grad(u_gen_group, mix[:, :rank]), in_grad(u_score_group, mix[:, rank:])], axis=2
    )
    chips, in_rows = in_grads.shape[0], in_grads.shape[1]
    groups = chips // 2
    out_grads = out_grads.reshape(2, groups, rank // groups, 2, hidden).transpose(1, 3, 0, 2, 4)
    out_rows = 2 * (rank // groups) * hidden // 128
    packed = jnp.concatenate(
        [in_grads.astype(bf16), out_grads.reshape(chips, out_rows, 128)], axis=1
    )
    received = lax.all_to_all(packed, CHIPS, 0, 0, tiled=True)
    summed = jnp.sum(received.astype(f32), axis=0)
    gen_grad_in, fake_grad_in = summed[:in_rows, :rank], summed[:in_rows, rank:]
    grads_out = summed[in_rows:].reshape(2, rank // groups, hidden)
    return (score_diff, gen_grad_in, grads_out[0], fake_grad_in, grads_out[1])


def solution(mesh):
    fine = Mesh(mesh.devices.reshape(4, 4, 2, 2, 2), AXES)
    dp, mp = ("z", "y", "xh"), ("xl", "core")
    return jax.shard_map(
        local,
        mesh=fine,
        in_specs=(
            P(AXES, None),
            P(AXES, None),
            P(),
            P(),
            P(dp, mp),
            P(mp, dp),
            P(),
            P(None, mp),
            P(),
            P(None, mp),
            P(),
            P(),
            P(),
        ),
        out_specs=(
            P(AXES, None),
            P(AXES, None),
            P(dp, mp),
            P(AXES, None),
            P(dp, mp),
        ),
        check_vma=False,
    )
```

```python
import functools
import math

import jax
import jax.numpy as jnp
from jax import lax
from jax.experimental import pallas as pl
from jax.experimental.pallas import tpu as pltpu
from jax.sharding import Mesh
from jax.sharding import PartitionSpec as P

IMG_TOK = 1024
AXES = ("z", "y", "xh", "xl", "core")
CHIPS = ("z", "y", "xh", "xl")

gelu_coef = 0.044715
root_two_pi = math.sqrt(2.0 / math.pi)


def gelu_value(pre):
    inner_arg = root_two_pi * (pre + gelu_coef * pre * pre * pre)
    return 0.5 * pre * (1.0 + jnp.tanh(inner_arg))


def gelu_slope(pre):
    tanh_val = jnp.tanh(root_two_pi * (pre + gelu_coef * pre * pre * pre))
    return 0.5 * (1.0 + tanh_val) + 0.5 * pre * (1.0 - tanh_val * tanh_val) * root_two_pi * (
        1.0 + 3.0 * gelu_coef * pre * pre
    )


def modulate(rows, scale_rows, shift_rows):
    widened = rows.astype(jnp.float32)
    normed = widened * lax.rsqrt(jnp.mean(widened * widened, axis=1, keepdims=True) + 1e-06)
    return (normed * scale_rows + shift_rows).astype(jnp.bfloat16)


def matmul(left, right):
    return jnp.dot(left, right, preferred_element_type=jnp.float32)


def contract(left, right, left_dim, right_dim):
    return lax.dot_general(
        left, right, (((left_dim,), (right_dim,)), ((), ())), preferred_element_type=jnp.float32
    )


def swap_cores(value):
    return lax.ppermute(value, "core", [(0, 1), (1, 0)])


RING_AXES = (("y", "z", "x"), ("z", "x", "y"), ("x", "y", "z"))
RING = 4


def chip_ring(axis):
    pairs = []
    for device in range(128):
        place = {"z": device // 32, "y": device // 8 % 4, "x": device // 2 % 4, "core": device % 2}
        step = 1 if place["core"] == 0 else -1
        place[axis] = (place[axis] + step) % RING
        target = place["z"] * 32 + place["y"] * 8 + place["x"] * 2 + place["core"]
        pairs.append((device, target))
    return pairs


def send(piece, i, phase):
    return lax.ppermute(piece, AXES, chip_ring(RING_AXES[i][phase]))


def gathered(pieces, phase):
    rows = pieces[0].shape[0]
    whole = [jnp.zeros((RING * rows, piece.shape[1]), piece.dtype) for piece in pieces]
    for step in range(RING):
        if step:
            pieces = [send(piece, i, phase) for i, piece in enumerate(pieces)]
        whole = [
            lax.dynamic_update_slice(buffer, piece, (step * rows, 0))
            for buffer, piece in zip(whole, pieces)
        ]
    return whole


def ring_slots(pieces, adapters, exchange, inputs, prepare):
    pieces = gathered(pieces, 0)
    pieces[2], adapters = lax.optimization_barrier((pieces[2], adapters))
    exchanged = exchange(adapters)
    pieces = gathered(pieces, 1)
    pieces[2], exchanged = lax.optimization_barrier((pieces[2], exchanged))
    slots = [[piece] for piece in pieces]
    for step in range(1, RING):
        if step == RING - 1:
            slots[2][-1], prepared = lax.optimization_barrier((slots[2][-1], prepared))
        for i in range(3):
            slots[i].append(send(slots[i][-1], i, 2))
        if step == 1:
            arrived = [slots[i][1] for i in range(3)]
            _, inputs = lax.optimization_barrier((arrived, inputs))
            prepared = prepare(*inputs)
    return slots, exchanged, prepared


SHARD = 96
PIECE = 64
REST = SHARD - PIECE
TILE = 512
WINDOW = 3
BLOCK = 8 * SHARD
MIB = 2**20
ANYWHERE = pl.BlockSpec(memory_space=pl.ANY)
IN_VMEM = pl.BlockSpec(memory_space=pltpu.VMEM)
IN_SMEM = pl.BlockSpec(memory_space=pltpu.SMEM)
NT = (((1,), (1,)), ((), ()))
TN = (((0,), (0,)), ((), ()))


def dot(left, right, dims=(((1,), (0,)), ((), ()))):
    return lax.dot_general(left, right, dims, preferred_element_type=jnp.float32)


def gelu_and_slope(pre):
    square = pre * pre
    tanh_val = jnp.tanh(root_two_pi * (pre + gelu_coef * square * pre))
    half = 0.5 * (1.0 + tanh_val)
    slope = half + 0.5 * pre * (1.0 - tanh_val * tanh_val) * root_two_pi * (
        1.0 + 3.0 * gelu_coef * square
    )
    return pre * half, slope


IN_HBM = pl.BlockSpec(memory_space=pltpu.HBM)


def piece_place(place_ref, i, step, k):
    me = {"z": place_ref[0], "y": place_ref[1], "x": place_ref[2]}
    direction = place_ref[3]
    first, second, third = RING_AXES[i]

    def source(axis, distance):
        return (me[axis] - distance * direction + RING) & (RING - 1)

    zero = k - k
    at = {
        first: source(first, k & (RING - 1)),
        second: source(second, k >> 2),
        third: source(third, step + zero),
    }
    group = (at["z"] * 4 + at["y"]) * 2 + (at["x"] >> 1)
    return at["x"] & 1, group * SHARD


def each(count, one, unroll=4):
    def step(k, carry):
        one(k)
        return carry

    lax.fori_loop(0, count, step, 0, unroll=unroll)


def wait_all(ref, sem):
    pltpu.make_async_copy(ref, ref, sem).wait()


def start_piece(i, source, quarter, row, up, down, sem, matrices=(0, 1)):
    hidden = source.shape[1]
    cols = pl.ds(pl.multiple_of(quarter * hidden, 128), hidden)
    if i < 2:
        target = (up, down)[i].at[pl.ds(row, PIECE), cols]
        pltpu.make_async_copy(source, target, sem).start()
    else:
        for n in matrices:
            rows = pl.ds(pl.multiple_of(row + PIECE, 32), REST)
            target = (up, down)[n].at[rows, cols]
            pltpu.make_async_copy(source.at[pl.ds(n * REST, REST)], target, sem).start()


def load_body(place_ref, table, u_mine, u_other, adapt_in, adapt, *refs):
    slots, (up_out, down_out, partial, low, up, down, u, sems) = refs[:9], refs[9:]
    for n, slot in enumerate(slots):
        step, i = n // 3, n % 3

        def one(k, slot=slot, step=step, i=i, n=n):
            quarter, row = piece_place(place_ref, i, step, k)
            start_piece(i, slot.at[k], quarter, pl.multiple_of(row, 32), up, down, sems.at[n])

        each(RING * RING, one)
    rows, pieces = u_mine.shape[0], RING * RING
    u[:rows] = u_mine[...]
    u[rows:] = u_other[...]
    low[...] = dot(u[...], adapt_in[...], NT).astype(low.dtype)
    hidden = up.shape[1] // 2

    def clear(k):
        for i, first, count in ((0, 0, PIECE), (2, PIECE, REST)):
            place = pl.ds(pl.multiple_of(table[1, i * pieces + k] + first, 32), count)
            cols = pl.ds(pl.multiple_of(table[0, i * pieces + k] * hidden, 128), hidden)
            up[place, cols] = jnp.zeros((count, hidden), up.dtype)

    each(pieces, clear, 2)
    for n, slot in enumerate(slots):
        if n % 3 != 1:
            wait_all(slot, sems.at[n])
    up_copy = pltpu.make_async_copy(up, up_out, sems.at[9])
    up_copy.start()
    for n, slot in enumerate(slots):
        if n % 3 == 1:
            wait_all(slot, sems.at[n])
    down_copy = pltpu.make_async_copy(down, down_out, sems.at[10])
    down_copy.start()

    def hidden_tile(n):
        cols = tile_at(n)
        partial[:, cols] = dot(u[...], up[:, cols]) + dot(low[...], adapt[:, cols])

    each(up.shape[1] // TILE, hidden_tile, 1)
    up_copy.wait()
    down_copy.wait()


def load_weights(coords, table, u_mine, u_other, adapt_in, adapt, slots):
    rows, width = u_mine.shape
    group, rank, hidden = 2 * rows, adapt_in.shape[0], adapt.shape[1]
    f32, bf16 = jnp.float32, jnp.bfloat16
    flat = [
        slots[i][step].reshape(RING * RING, PIECE, hidden // 2) for step in range(3) for i in range(3)
    ]
    shape = jax.ShapeDtypeStruct((width, hidden), bf16)
    return pl.pallas_call(
        load_body,
        out_shape=(
            shape,
            shape,
            jax.ShapeDtypeStruct((group, hidden), f32),
            jax.ShapeDtypeStruct((group, rank), bf16),
        ),
        in_specs=[IN_SMEM] * 2 + [IN_VMEM] * 4 + [IN_HBM] * 9,
        out_specs=(IN_HBM, IN_HBM, IN_VMEM, IN_VMEM),
        scratch_shapes=[
            pltpu.VMEM(shape.shape, bf16),
            pltpu.VMEM(shape.shape, bf16),
            pltpu.VMEM((group, width), bf16),
            pltpu.SemaphoreType.DMA((11,)),
        ],
        compiler_params=pltpu.CompilerParams(vmem_limit_bytes=46 * MIB),
        cost_estimate=pl.CostEstimate(
            flops=2 * group * width * hidden, bytes_accessed=16 * width * hidden, transcendentals=0
        ),
        name="load_weights",
    )(coords, table, u_mine, u_other, adapt_in, adapt, *flat)


def column_copy(source, target, sems, n):
    cols = pl.ds(pl.multiple_of(n * TILE, TILE), TILE)
    return pltpu.make_async_copy(source.at[:, cols], target.at[:, cols], sems.at[n])


def row_copy(source, target, sems, n):
    rows = pl.ds(pl.multiple_of(n * TILE, TILE), TILE)
    return pltpu.make_async_copy(source.at[rows], target.at[rows], sems.at[n])


def start_ahead(place, segments):
    ahead = place + WINDOW
    for count, copy in segments:

        @pl.when((ahead >= 0) & (ahead < count))
        def _(ahead=ahead, copy=copy):
            copy(ahead).start()

        ahead = ahead - count


def tile_at(n):
    return pl.ds(pl.multiple_of(n * TILE, TILE), TILE)


def gen_body(table, u_columns, partial, *refs):
    slots, (up_in, down_in, up_out, down_out, slope, mine, other) = refs[:3], refs[3:10]
    down, last, u_first, u_rest, up_rest, act, sems, down_sems = refs[10:]
    rows = mine.shape[0]
    pieces = RING * RING
    hidden = last.shape[3]
    fetches = [pltpu.make_async_copy(slots[i], last.at[i], sems.at[i]) for i in range(3)]

    def down_copy(n):
        part = pl.ds(pl.multiple_of(n * BLOCK, BLOCK), BLOCK)
        return pltpu.make_async_copy(down_in.at[part], down.at[part], down_sems.at[n])

    blocks = down.shape[0] // BLOCK
    for i in (0, 2, 1):
        fetches[i].start()
    for n in range(blocks):
        down_copy(n).start()

    def spot(i, k):
        return table[0, i * pieces + k], pl.multiple_of(table[1, i * pieces + k], 32)

    for k in range(pieces):
        u_first[k * PIECE : (k + 1) * PIECE] = u_columns[pl.ds(spot(0, k)[1], PIECE), :]
        at = pl.ds(k // 2 * REST, REST)
        u_rest[k % 2, at] = u_columns[pl.ds(pl.multiple_of(spot(2, k)[1] + PIECE, 32), REST), :]
    fetches[0].wait()
    fetches[2].wait()
    for k in range(pieces):
        up_rest[k % 2, pl.ds(k // 2 * REST, REST)] = last[2, k, :REST]
    first_quarter, rest_quarter = table[0, 0], table[0, 2 * pieces]

    def hidden_tile(quarter, n, with_first):
        part = tile_at(n)
        cols = pl.ds(pl.multiple_of(quarter * hidden + n * TILE, TILE), TILE)
        side = jnp.where(quarter == rest_quarter, 0, 1)
        pre = partial[:, cols] + dot(u_rest[side], up_rest[side, :, part], TN)
        if with_first:
            pre = pre + dot(u_first[...], last[0, :, :, part].reshape(pieces * PIECE, TILE), TN)
        value, slope[:, cols] = gelu_and_slope(pre)
        act[:, cols] = value.astype(act.dtype)

    tiles = hidden // TILE
    each(tiles, lambda n: hidden_tile(first_quarter, n, True), 1)
    each(tiles, lambda n: hidden_tile(1 - first_quarter, n, False), 1)

    def store(i, matrices):
        def one(k):
            quarter, row = spot(i, k)
            start_piece(i, last.at[i, k], quarter, row, up_out, down_out, sems.at[3 + i], matrices)

        each(pieces, one)

    fetches[1].wait()
    store(0, (0,))
    store(2, (0,))

    for n in range(blocks):
        down_copy(n).wait()
        if n == blocks - 1:
            store(1, (1,))
            store(2, (1,))

        def place_down(k, n=n):
            for i in (1, 2):
                quarter, row = spot(i, k)
                cols = pl.ds(pl.multiple_of(quarter * hidden, 128), hidden)

                @pl.when(table[2, i * pieces + k] == n)
                def _(i=i, row=row, cols=cols):
                    if i == 1:
                        down[pl.ds(row, PIECE), cols] = last[1, k]
                    else:
                        down[pl.ds(pl.multiple_of(row + PIECE, 32), REST), cols] = last[2, k, REST:]

        each(pieces, place_down, 2)
        cols = pl.ds(n * BLOCK, BLOCK)
        out = dot(act[...], down[cols, :], NT)
        mine[:, cols] = out[:rows]
        other[:, cols] = out[rows:].astype(other.dtype)
    for i in range(3):
        wait_all(last.at[i], sems.at[3 + i])


def gen_forward(table, u_columns, partial, slots, up, down):
    width, group = u_columns.shape
    hidden = up.shape[1]
    rows, rest = group // 2, RING * RING * REST // 2
    f32, bf16 = jnp.float32, jnp.bfloat16
    shape = jax.ShapeDtypeStruct((width, hidden), bf16)
    last = [slots[i][3].reshape(RING * RING, PIECE, hidden // 2) for i in range(3)]
    return pl.pallas_call(
        gen_body,
        out_shape=(
            shape,
            shape,
            jax.ShapeDtypeStruct((group, hidden), f32),
            jax.ShapeDtypeStruct((rows, width), f32),
            jax.ShapeDtypeStruct((rows, width), bf16),
        ),
        in_specs=[IN_SMEM] + [IN_VMEM] * 2 + [IN_HBM] * 5,
        out_specs=(IN_HBM, IN_HBM) + (IN_VMEM,) * 3,
        scratch_shapes=[
            pltpu.VMEM(shape.shape, bf16),
            pltpu.VMEM((3, RING * RING, PIECE, hidden // 2), bf16),
            pltpu.VMEM((RING * RING * PIECE, group), bf16),
            pltpu.VMEM((2, rest, group), bf16),
            pltpu.VMEM((2, rest, hidden // 2), bf16),
            pltpu.VMEM((group, hidden), bf16),
            pltpu.SemaphoreType.DMA((6,)),
            pltpu.SemaphoreType.DMA((width // BLOCK,)),
        ],
        input_output_aliases={6: 0, 7: 1},
        compiler_params=pltpu.CompilerParams(vmem_limit_bytes=46 * MIB),
        cost_estimate=pl.CostEstimate(
            flops=3 * group * width * hidden,
            bytes_accessed=40 * MIB,
            transcendentals=group * hidden,
        ),
        name="gen_forward",
    )(table, u_columns, partial, *last, up, down)


def score_body(
    u_mine, u_other, adapt_in, adapt_out, up_in, down_in, slope, low, real, fake, others, *scratch
):
    u, act, up, down, up_sems, down_sems = scratch
    hidden_tiles, width_tiles = up.shape[1] // TILE, down.shape[0] // TILE
    segments = (
        (hidden_tiles, functools.partial(column_copy, up_in, up, up_sems)),
        (width_tiles, functools.partial(row_copy, down_in, down, down_sems)),
    )
    for n in range(WINDOW):
        column_copy(up_in, up, up_sems, n).start()
    rows = u_mine.shape[0]
    group = 2 * rows
    u[:rows] = u_mine[...]
    u[rows:] = u_other[...]
    low[...] = dot(u[...], adapt_in[...], NT).astype(low.dtype)

    def hidden_tile(n):
        column_copy(up_in, up, up_sems, n).wait()
        start_ahead(n, segments)
        cols = tile_at(n)
        pre_real = dot(u[...], up[:, cols])
        pre_fake = pre_real + dot(low[...], adapt_out[:, cols])
        act[:group, cols] = gelu_value(pre_real).astype(act.dtype)
        value, slope[:, cols] = gelu_and_slope(pre_fake)
        act[group:, cols] = value.astype(act.dtype)

    each(hidden_tiles, hidden_tile, 1)

    def width_tile(n):
        row_copy(down_in, down, down_sems, n).wait()
        start_ahead(hidden_tiles + n, segments)
        cols = tile_at(n)
        out = dot(act[...], down[cols, :], NT)
        real[:, cols] = out[:rows]
        others[:rows, cols] = out[rows:group].astype(others.dtype)
        fake[:, cols] = out[group : group + rows]
        others[rows:, cols] = out[group + rows :].astype(others.dtype)

    each(width_tiles, width_tile, 1)


def score_forward(u_mine, u_other, adapt_in, adapt_out, up, down):
    rows, width = u_mine.shape
    hidden = up.shape[1]
    group = 2 * rows
    f32, bf16 = jnp.float32, jnp.bfloat16
    return pl.pallas_call(
        score_body,
        out_shape=(
            jax.ShapeDtypeStruct((group, hidden), f32),
            jax.ShapeDtypeStruct((group, adapt_in.shape[0]), bf16),
            jax.ShapeDtypeStruct((rows, width), f32),
            jax.ShapeDtypeStruct((rows, width), f32),
            jax.ShapeDtypeStruct((group, width), bf16),
        ),
        in_specs=[IN_VMEM] * 4 + [IN_HBM] * 2,
        out_specs=(IN_VMEM,) * 5,
        scratch_shapes=[
            pltpu.VMEM((group, width), bf16),
            pltpu.VMEM((2 * group, hidden), bf16),
            pltpu.VMEM(up.shape, bf16),
            pltpu.VMEM(down.shape, bf16),
            pltpu.SemaphoreType.DMA((hidden // TILE,)),
            pltpu.SemaphoreType.DMA((width // TILE,)),
        ],
        compiler_params=pltpu.CompilerParams(vmem_limit_bytes=56 * MIB),
        cost_estimate=pl.CostEstimate(
            flops=6 * group * width * hidden,
            bytes_accessed=50 * MIB,
            transcendentals=2 * group * hidden,
        ),
        name="score_forward",
    )(u_mine, u_other, adapt_in, adapt_out, up, down)


def back_body(
    cots_mine, cots_other, slope_gen, slope_fake, low_gen, low_fake, gen_out, fake_out, down_in, grads, mix, *scratch
):
    cots, down, sems = scratch
    tiles = down.shape[1] // TILE
    for n in range(WINDOW):
        column_copy(down_in, down, sems, n).start()
    group = cots_mine.shape[0]
    rows = group // 2
    for i in range(2):
        cots[i * group : i * group + rows] = cots_mine[i * rows : (i + 1) * rows]
        cots[i * group + rows : (i + 1) * group] = cots_other[i * rows : (i + 1) * rows]
    mix[...] = jnp.zeros_like(mix)

    def hidden_tile(n):
        column_copy(down_in, down, sems, n).wait()
        start_ahead(n, ((tiles, functools.partial(column_copy, down_in, down, sems)),))
        cols = tile_at(n)
        raw = dot(cots[...], down[:, cols])
        back_gen = (raw[:group] * slope_gen[:, cols]).astype(jnp.bfloat16)
        back_fake = (raw[group:] * slope_fake[:, cols]).astype(jnp.bfloat16)
        grads[0, :, cols] = dot(low_gen[...], back_gen, TN).astype(grads.dtype)
        grads[1, :, cols] = dot(low_fake[...], back_fake, TN).astype(grads.dtype)
        mix[0] += dot(back_gen, gen_out[:, cols], NT)
        mix[1] += dot(back_fake, fake_out[:, cols], NT)

    each(tiles, hidden_tile, 1)


def backward(cots_mine, cots_other, slope_gen, slope_fake, low_gen, low_fake, gen_out, fake_out, down):
    group, width = cots_mine.shape
    hidden = down.shape[1]
    rank = low_gen.shape[1]
    f32, bf16 = jnp.float32, jnp.bfloat16
    return pl.pallas_call(
        back_body,
        out_shape=(
            jax.ShapeDtypeStruct((2, rank, hidden), bf16),
            jax.ShapeDtypeStruct((2, group, rank), f32),
        ),
        in_specs=[IN_VMEM] * 8 + [IN_HBM],
        out_specs=(IN_VMEM,) * 2,
        scratch_shapes=[
            pltpu.VMEM((2 * group, width), bf16),
            pltpu.VMEM(down.shape, bf16),
            pltpu.SemaphoreType.DMA((hidden // TILE,)),
        ],
        compiler_params=pltpu.CompilerParams(vmem_limit_bytes=40 * MIB),
        cost_estimate=pl.CostEstimate(
            flops=4 * group * width * hidden, bytes_accessed=30 * MIB, transcendentals=0
        ),
        name="backward",
    )(cots_mine, cots_other, slope_gen, slope_fake, low_gen, low_fake, gen_out, fake_out, down)


STRIP = 16


def embed_body(ends, steps, given, scale_ref, shift_ref, u_ref, mods_ref):
    half = given.shape[1] // 2
    place = lax.broadcasted_iota(jnp.int32, (1, half), 1).astype(jnp.float32)
    frequency = jnp.exp(-math.log(10000.0) * place / half)
    row = lax.broadcasted_iota(jnp.int32, (4, 1), 0)
    column = jnp.where(
        row < 2, jnp.where(row == 0, steps[0], steps[1]), jnp.where(row == 2, steps[2], steps[3])
    )
    phase = column * frequency
    embed = jnp.concatenate([jnp.sin(phase), jnp.cos(phase)], axis=1)
    scale = 1.0 + scale_ref[...] * embed
    shift = shift_ref[...] * embed
    mods_ref[0:2] = scale[2:4]
    mods_ref[2:4] = shift[2:4]

    def strip(n, carry):
        rows = pl.ds(pl.multiple_of(n * STRIP, STRIP), STRIP)
        in_last = n * STRIP + lax.broadcasted_iota(jnp.int32, (STRIP, 1), 0) >= ends[0]
        u_ref[rows] = modulate(
            given[rows],
            jnp.where(in_last, scale[1:2], scale[0:1]),
            jnp.where(in_last, shift[1:2], shift[0:1]),
        )
        return carry

    lax.fori_loop(0, given.shape[0] // STRIP, strip, 0)


def first_modulation(ends, steps, given, scale, shift):
    width = given.shape[1]
    return pl.pallas_call(
        embed_body,
        out_shape=(
            jax.ShapeDtypeStruct(given.shape, given.dtype),
            jax.ShapeDtypeStruct((4, width), jnp.float32),
        ),
        in_specs=[IN_SMEM] * 2 + [IN_VMEM] * 3,
        out_specs=(IN_VMEM,) * 2,
        compiler_params=pltpu.CompilerParams(vmem_limit_bytes=8 * MIB),
        cost_estimate=pl.CostEstimate(flops=0, bytes_accessed=2 * MIB, transcendentals=0),
        name="first_modulation",
    )(ends, steps, given, scale.reshape(1, width), shift.reshape(1, width))


def noise_body(ends, blends, given, noise, mine, other, mods, gate, latents_ref, noised_ref, u_ref):
    f32 = jnp.float32

    def strip(n, carry):
        rows = pl.ds(pl.multiple_of(n * STRIP, STRIP), STRIP)
        in_last = n * STRIP + lax.broadcasted_iota(jnp.int32, (STRIP, 1), 0) >= ends[0]
        out = mine[rows] + other[rows].astype(f32)
        latents = (given[rows].astype(f32) + gate[...] * out).astype(latents_ref.dtype)
        latents_ref[rows] = latents
        blend = jnp.where(in_last, blends[1], blends[0])
        noised = (
            (1.0 - blend) * latents.astype(f32) + blend * noise[rows].astype(f32)
        ).astype(noised_ref.dtype)
        noised_ref[rows] = noised
        scale = jnp.where(in_last, mods[1:2], mods[0:1])
        shift = jnp.where(in_last, mods[3:4], mods[2:3])
        u_ref[rows] = modulate(noised, scale, shift)
        return carry

    lax.fori_loop(0, given.shape[0] // STRIP, strip, 0)


def add_noise(ends, blends, given, noise, mine, other, mods, gate):
    shape = jax.ShapeDtypeStruct(given.shape, given.dtype)
    return pl.pallas_call(
        noise_body,
        out_shape=(shape,) * 3,
        in_specs=[IN_SMEM] * 2 + [IN_VMEM] * 6,
        out_specs=(IN_VMEM,) * 3,
        compiler_params=pltpu.CompilerParams(vmem_limit_bytes=10 * MIB),
        cost_estimate=pl.CostEstimate(flops=0, bytes_accessed=6 * MIB, transcendentals=0),
        name="add_noise",
    )(ends, blends, given, noise, mine, other, mods, gate)


def cotangent_body(scale, real, fake, others, gate_ref, noise, latents, noised, diff_ref, cots):
    f32 = jnp.float32
    count = real.shape[0]

    def strip(n, carry):
        start = pl.multiple_of(n * STRIP, STRIP)
        rows, second = pl.ds(start, STRIP), pl.ds(count + start, STRIP)
        gate = gate_ref[...]
        out_real = real[rows] + others[rows].astype(f32)
        out_fake = fake[rows] + others[second].astype(f32)
        diff = (gate * (out_fake - out_real)).astype(diff_ref.dtype)
        diff_ref[rows] = diff
        cots[rows] = (gate * diff.astype(f32) * scale).astype(cots.dtype)
        target = noise[rows].astype(f32) - latents[rows].astype(f32)
        cots[second] = (
            gate * (noised[rows].astype(f32) + gate * out_fake - target) * scale
        ).astype(cots.dtype)
        return carry

    lax.fori_loop(0, count // STRIP, strip, 0)


def cotangents(scale, real, fake, others, gate, noise, latents, noised):
    rows, width = real.shape
    return pl.pallas_call(
        functools.partial(cotangent_body, scale),
        out_shape=(
            jax.ShapeDtypeStruct((rows, width), noise.dtype),
            jax.ShapeDtypeStruct((2 * rows, width), noise.dtype),
        ),
        in_specs=[IN_VMEM] * 7,
        out_specs=(IN_VMEM,) * 2,
        compiler_params=pltpu.CompilerParams(vmem_limit_bytes=12 * MIB),
        cost_estimate=pl.CostEstimate(flops=0, bytes_accessed=8 * MIB, transcendentals=0),
        name="cotangents",
    )(real, fake, others, gate, noise, latents, noised)


def three_terms(value):
    high = lax.reduce_precision(value, 8, 7)
    rest = value - high
    middle = lax.reduce_precision(rest, 8, 7)
    low = rest - middle
    return jnp.concatenate([high, middle, low], axis=1).astype(jnp.bfloat16)


def local(
    gen_input,
    noise_score,
    gen_steps,
    score_steps,
    base_up,
    base_down,
    gen_adapt_in,
    gen_adapt_out,
    fake_adapt_in,
    fake_adapt_out,
    modulation_scale,
    modulation_shift,
    output_gate,
):
    bf16, f32 = jnp.bfloat16, jnp.float32
    shard_rows, width = gen_input.shape
    hidden = base_up.shape[1]
    rank = gen_adapt_in.shape[1]
    image_count = gen_steps.shape[0]
    loss_scale = 1.0 / math.sqrt(image_count * IMG_TOK)
    core = lax.axis_index("core")
    xl = lax.axis_index("xl")
    first_row = lax.axis_index(AXES) * shard_rows
    first_image = first_row // IMG_TOK
    last_image = (first_row + shard_rows - 1) // IMG_TOK
    def two_steps(steps):
        return jnp.stack([steps[first_image], steps[last_image]])

    def both_quarters(mine):
        theirs = lax.ppermute(mine, "xl", [(0, 1), (1, 0)])
        quarters = [jnp.where(xl == 0, mine, theirs), jnp.where(xl == 0, theirs, mine)]
        return jnp.concatenate(quarters, axis=1)

    blends = (two_steps(score_steps).astype(f32) + 0.5) / 1000.0
    ends = (last_image * IMG_TOK - first_row).astype(jnp.int32).reshape(1)
    steps = jnp.concatenate([two_steps(gen_steps), two_steps(score_steps)]).astype(f32)
    place = [lax.axis_index("z"), lax.axis_index("y"), lax.axis_index("xh") * 2 + xl, 1 - 2 * core]
    coords = jnp.stack(place).astype(jnp.int32)
    spots = [piece_place(coords, i, 3, jnp.arange(RING * RING, dtype=jnp.int32)) for i in range(3)]
    quarters, rows = [jnp.concatenate([spot[n] for spot in spots]) for n in range(2)]
    table = jnp.stack([quarters, rows, rows // BLOCK])

    def prepare(given):
        u_mine, mods = first_modulation(ends, steps, given, modulation_scale, modulation_shift)
        u_other = swap_cores(u_mine)
        u_columns = jnp.concatenate([u_mine, u_other], axis=0).T
        return u_mine, u_other, u_columns, mods, blends, coords, table

    down_rows = base_down.T
    slots, adapt_out, prepared = ring_slots(
        [
            base_up[:PIECE],
            down_rows[:PIECE],
            jnp.concatenate([base_up[PIECE:], down_rows[PIECE:]], axis=0),
        ],
        jnp.concatenate([gen_adapt_out, fake_adapt_out], axis=0),
        both_quarters,
        (gen_input,),
        prepare,
    )
    u_gen, u_gen_other, u_columns, mods, blends, coords, table = prepared
    gen_out, fake_out = adapt_out[:rank], adapt_out[rank:]
    up_part, down_part, partial, low_gen = load_weights(
        coords, table, u_gen, u_gen_other, gen_adapt_in.T, gen_out, slots
    )
    up_all, down_all, slope_gen, out_mine, out_other = gen_forward(
        table, u_columns, partial, slots, up_part, down_part
    )
    gate = output_gate.reshape(1, width)
    latents, noised, u_score = add_noise(
        ends, blends, gen_input, noise_score, out_mine, swap_cores(out_other), mods, gate
    )
    u_score_other = swap_cores(u_score)
    slope_fake, low_fake, out_real, out_fake, outs_other = score_forward(
        u_score, u_score_other, fake_adapt_in.T, fake_out, up_all, down_all
    )
    score_diff, cots = cotangents(
        loss_scale, out_real, out_fake, swap_cores(outs_other), gate, noise_score, latents, noised
    )
    out_grads, mix = backward(
        cots, swap_cores(cots), slope_gen, slope_fake, low_gen, low_fake, gen_out, fake_out, down_all
    )
    mix = jnp.concatenate([mix[0], mix[1]], axis=1)
    mix_other = swap_cores(mix)
    mix = mix + jnp.concatenate([mix_other[shard_rows:], mix_other[:shard_rows]], axis=0)

    def in_grad(u, mix_part):
        product = contract(u, three_terms(mix_part), 0, 0)
        total = product[:, :rank] + product[:, rank : 2 * rank] + product[:, 2 * rank :]
        chips = total.reshape(-1, 2, width // 128, rank)
        return jnp.where(core == 0, chips[:, 0], chips[:, 1])

    u_gen_group = jnp.concatenate([u_gen, u_gen_other], axis=0)
    u_score_group = jnp.concatenate([u_score, u_score_other], axis=0)
    in_grads = jnp.concatenate(
        [in_grad(u_gen_group, mix[:, :rank]), in_grad(u_score_group, mix[:, rank:])], axis=2
    )
    chips, in_rows = in_grads.shape[0], in_grads.shape[1]
    groups = chips // 2
    out_grads = out_grads.reshape(2, groups, rank // groups, 2, hidden).transpose(1, 3, 0, 2, 4)
    out_rows = 2 * (rank // groups) * hidden // 128
    packed = jnp.concatenate(
        [in_grads.astype(bf16), out_grads.reshape(chips, out_rows, 128)], axis=1
    )
    received = lax.all_to_all(packed, CHIPS, 0, 0, tiled=True)
    summed = jnp.sum(received.astype(f32), axis=0)
    gen_grad_in, fake_grad_in = summed[:in_rows, :rank], summed[:in_rows, rank:]
    grads_out = summed[in_rows:].reshape(2, rank // groups, hidden)
    return (score_diff, gen_grad_in, grads_out[0], fake_grad_in, grads_out[1])


def solution(mesh):
    fine = Mesh(mesh.devices.reshape(4, 4, 2, 2, 2), AXES)
    dp, mp = ("z", "y", "xh"), ("xl", "core")
    return jax.shard_map(
        local,
        mesh=fine,
        in_specs=(
            P(AXES, None),
            P(AXES, None),
            P(),
            P(),
            P(dp, mp),
            P(mp, dp),
            P(),
            P(None, mp),
            P(),
            P(None, mp),
            P(),
            P(),
            P(),
        ),
        out_specs=(
            P(AXES, None),
            P(AXES, None),
            P(dp, mp),
            P(AXES, None),
            P(dp, mp),
        ),
        check_vma=False,
    )
```

```python
import functools
import math

import jax
import jax.numpy as jnp
from jax import lax
from jax.experimental import pallas as pl
from jax.experimental.pallas import tpu as pltpu
from jax.sharding import Mesh
from jax.sharding import PartitionSpec as P

IMG_TOK = 1024
AXES = ("z", "y", "xh", "xl", "core")
CHIPS = ("z", "y", "xh", "xl")

gelu_coef = 0.044715
root_two_pi = math.sqrt(2.0 / math.pi)


def gelu_value(pre):
    inner_arg = root_two_pi * (pre + gelu_coef * pre * pre * pre)
    return 0.5 * pre * (1.0 + jnp.tanh(inner_arg))


def gelu_slope(pre):
    tanh_val = jnp.tanh(root_two_pi * (pre + gelu_coef * pre * pre * pre))
    return 0.5 * (1.0 + tanh_val) + 0.5 * pre * (1.0 - tanh_val * tanh_val) * root_two_pi * (
        1.0 + 3.0 * gelu_coef * pre * pre
    )


def modulate(rows, scale_rows, shift_rows):
    widened = rows.astype(jnp.float32)
    normed = widened * lax.rsqrt(jnp.mean(widened * widened, axis=1, keepdims=True) + 1e-06)
    return (normed * scale_rows + shift_rows).astype(jnp.bfloat16)


def matmul(left, right):
    return jnp.dot(left, right, preferred_element_type=jnp.float32)


def contract(left, right, left_dim, right_dim):
    return lax.dot_general(
        left, right, (((left_dim,), (right_dim,)), ((), ())), preferred_element_type=jnp.float32
    )


def swap_cores(value):
    return lax.ppermute(value, "core", [(0, 1), (1, 0)])


RING_AXES = (("y", "z", "x"), ("z", "x", "y"), ("x", "y", "z"))
RING = 4


def chip_ring(axis):
    pairs = []
    for device in range(128):
        place = {"z": device // 32, "y": device // 8 % 4, "x": device // 2 % 4, "core": device % 2}
        step = 1 if place["core"] == 0 else -1
        place[axis] = (place[axis] + step) % RING
        target = place["z"] * 32 + place["y"] * 8 + place["x"] * 2 + place["core"]
        pairs.append((device, target))
    return pairs


def send(piece, i, phase):
    return lax.ppermute(piece, AXES, chip_ring(RING_AXES[i][phase]))


def gathered(pieces, phase):
    rows = pieces[0].shape[0]
    whole = [jnp.zeros((RING * rows, piece.shape[1]), piece.dtype) for piece in pieces]
    for step in range(RING):
        if step:
            pieces = [send(piece, i, phase) for i, piece in enumerate(pieces)]
        whole = [
            lax.dynamic_update_slice(buffer, piece, (step * rows, 0))
            for buffer, piece in zip(whole, pieces)
        ]
    return whole


def ring_slots(pieces, adapters, exchange, inputs, prepare):
    pieces = gathered(pieces, 0)
    pieces[2], adapters = lax.optimization_barrier((pieces[2], adapters))
    exchanged = exchange(adapters)
    pieces = gathered(pieces, 1)
    pieces[2], exchanged = lax.optimization_barrier((pieces[2], exchanged))
    slots = [[piece] for piece in pieces]
    for step in range(1, RING):
        if step == RING - 1:
            slots[2][-1], prepared = lax.optimization_barrier((slots[2][-1], prepared))
        for i in range(3):
            slots[i].append(send(slots[i][-1], i, 2))
        if step == 1:
            arrived = [slots[i][1] for i in range(3)]
            _, inputs = lax.optimization_barrier((arrived, inputs))
            prepared = prepare(*inputs)
    return slots, exchanged, prepared


SHARD = 96
PIECE = 64
REST = SHARD - PIECE
TILE = 512
BLOCK = 8 * SHARD
MIB = 2**20
ANYWHERE = pl.BlockSpec(memory_space=pl.ANY)
IN_VMEM = pl.BlockSpec(memory_space=pltpu.VMEM)
IN_SMEM = pl.BlockSpec(memory_space=pltpu.SMEM)
NT = (((1,), (1,)), ((), ()))
TN = (((0,), (0,)), ((), ()))


def dot(left, right, dims=(((1,), (0,)), ((), ()))):
    return lax.dot_general(left, right, dims, preferred_element_type=jnp.float32)


def gelu_and_slope(pre):
    square = pre * pre
    tanh_val = jnp.tanh(root_two_pi * (pre + gelu_coef * square * pre))
    half = 0.5 * (1.0 + tanh_val)
    slope = half + 0.5 * pre * (1.0 - tanh_val * tanh_val) * root_two_pi * (
        1.0 + 3.0 * gelu_coef * square
    )
    return pre * half, slope


IN_HBM = pl.BlockSpec(memory_space=pltpu.HBM)


def piece_place(place_ref, i, step, k):
    me = {"z": place_ref[0], "y": place_ref[1], "x": place_ref[2]}
    direction = place_ref[3]
    first, second, third = RING_AXES[i]

    def source(axis, distance):
        return (me[axis] - distance * direction + RING) & (RING - 1)

    zero = k - k
    at = {
        first: source(first, k & (RING - 1)),
        second: source(second, k >> 2),
        third: source(third, step + zero),
    }
    group = (at["z"] * 4 + at["y"]) * 2 + (at["x"] >> 1)
    return at["x"] & 1, group * SHARD


def each(count, one, unroll=4):
    def step(k, carry):
        one(k)
        return carry

    lax.fori_loop(0, count, step, 0, unroll=unroll)


def wait_all(ref, sem):
    pltpu.make_async_copy(ref, ref, sem).wait()


def start_piece(i, source, quarter, row, up, down, sem, matrices=(0, 1)):
    hidden = source.shape[1]
    cols = pl.ds(pl.multiple_of(quarter * hidden, 128), hidden)
    if i < 2:
        target = (up, down)[i].at[pl.ds(row, PIECE), cols]
        pltpu.make_async_copy(source, target, sem).start()
    else:
        for n in matrices:
            rows = pl.ds(pl.multiple_of(row + PIECE, 32), REST)
            target = (up, down)[n].at[rows, cols]
            pltpu.make_async_copy(source.at[pl.ds(n * REST, REST)], target, sem).start()


def load_body(place_ref, table, u_mine, u_other, adapt_in, adapt, *refs):
    slots, (up_out, down_out, partial, low, up, down, u, sems) = refs[:9], refs[9:]
    for n, slot in enumerate(slots):
        step, i = n // 3, n % 3

        def one(k, slot=slot, step=step, i=i, n=n):
            quarter, row = piece_place(place_ref, i, step, k)
            start_piece(i, slot.at[k], quarter, pl.multiple_of(row, 32), up, down, sems.at[n])

        each(RING * RING, one)
    rows, pieces = u_mine.shape[0], RING * RING
    u[:rows] = u_mine[...]
    u[rows:] = u_other[...]
    low[...] = dot(u[...], adapt_in[...], NT).astype(low.dtype)
    hidden = up.shape[1] // 2

    def clear(k):
        for i, first, count in ((0, 0, PIECE), (2, PIECE, REST)):
            place = pl.ds(pl.multiple_of(table[1, i * pieces + k] + first, 32), count)
            cols = pl.ds(pl.multiple_of(table[0, i * pieces + k] * hidden, 128), hidden)
            up[place, cols] = jnp.zeros((count, hidden), up.dtype)

    each(pieces, clear, 2)
    for n, slot in enumerate(slots):
        if n % 3 != 1:
            wait_all(slot, sems.at[n])
    up_copy = pltpu.make_async_copy(up, up_out, sems.at[9])
    up_copy.start()
    for n, slot in enumerate(slots):
        if n % 3 == 1:
            wait_all(slot, sems.at[n])
    down_copy = pltpu.make_async_copy(down, down_out, sems.at[10])
    down_copy.start()

    def hidden_tile(n):
        cols = tile_at(n)
        partial[:, cols] = dot(u[...], up[:, cols]) + dot(low[...], adapt[:, cols])

    each(up.shape[1] // TILE, hidden_tile, 1)
    up_copy.wait()
    down_copy.wait()


def load_weights(coords, table, u_mine, u_other, adapt_in, adapt, slots):
    rows, width = u_mine.shape
    group, rank, hidden = 2 * rows, adapt_in.shape[0], adapt.shape[1]
    f32, bf16 = jnp.float32, jnp.bfloat16
    flat = [
        slots[i][step].reshape(RING * RING, PIECE, hidden // 2) for step in range(3) for i in range(3)
    ]
    shape = jax.ShapeDtypeStruct((width, hidden), bf16)
    return pl.pallas_call(
        load_body,
        out_shape=(
            shape,
            shape,
            jax.ShapeDtypeStruct((group, hidden), f32),
            jax.ShapeDtypeStruct((group, rank), bf16),
        ),
        in_specs=[IN_SMEM] * 2 + [IN_VMEM] * 4 + [IN_HBM] * 9,
        out_specs=(IN_HBM, IN_HBM, IN_VMEM, IN_VMEM),
        scratch_shapes=[
            pltpu.VMEM(shape.shape, bf16),
            pltpu.VMEM(shape.shape, bf16),
            pltpu.VMEM((group, width), bf16),
            pltpu.SemaphoreType.DMA((11,)),
        ],
        compiler_params=pltpu.CompilerParams(vmem_limit_bytes=46 * MIB),
        cost_estimate=pl.CostEstimate(
            flops=2 * group * width * hidden, bytes_accessed=16 * width * hidden, transcendentals=0
        ),
        name="load_weights",
    )(coords, table, u_mine, u_other, adapt_in, adapt, *flat)


def column_copy(source, target, sems, n):
    cols = pl.ds(pl.multiple_of(n * TILE, TILE), TILE)
    return pltpu.make_async_copy(source.at[:, cols], target.at[:, cols], sems.at[n])


def row_copy(source, target, sems, n):
    rows = pl.ds(pl.multiple_of(n * TILE, TILE), TILE)
    return pltpu.make_async_copy(source.at[rows], target.at[rows], sems.at[n])


def tile_at(n):
    return pl.ds(pl.multiple_of(n * TILE, TILE), TILE)


def gen_body(table, u_columns, partial, *refs):
    slots, (up_in, down_in, up_out, down_out, slope, mine, other) = refs[:3], refs[3:10]
    down, last, u_first, u_rest, up_rest, act, sems, down_sems = refs[10:]
    rows = mine.shape[0]
    pieces = RING * RING
    hidden = last.shape[3]
    fetches = [pltpu.make_async_copy(slots[i], last.at[i], sems.at[i]) for i in range(3)]

    def down_copy(n):
        part = pl.ds(pl.multiple_of(n * BLOCK, BLOCK), BLOCK)
        return pltpu.make_async_copy(down_in.at[part], down.at[part], down_sems.at[n])

    blocks = down.shape[0] // BLOCK
    fetches[0].start()
    fetches[2].start()

    def spot(i, k):
        return table[0, i * pieces + k], pl.multiple_of(table[1, i * pieces + k], 32)

    for k in range(pieces):
        u_first[k * PIECE : (k + 1) * PIECE] = u_columns[pl.ds(spot(0, k)[1], PIECE), :]
        at = pl.ds(k // 2 * REST, REST)
        u_rest[k % 2, at] = u_columns[pl.ds(pl.multiple_of(spot(2, k)[1] + PIECE, 32), REST), :]
    fetches[0].wait()
    fetches[2].wait()
    fetches[1].start()
    for n in range(blocks):
        down_copy(n).start()
    for k in range(pieces):
        up_rest[k % 2, pl.ds(k // 2 * REST, REST)] = last[2, k, :REST]
    first_quarter, rest_quarter = table[0, 0], table[0, 2 * pieces]

    def hidden_tile(quarter, n, with_first):
        part = tile_at(n)
        cols = pl.ds(pl.multiple_of(quarter * hidden + n * TILE, TILE), TILE)
        side = jnp.where(quarter == rest_quarter, 0, 1)
        pre = partial[:, cols] + dot(u_rest[side], up_rest[side, :, part], TN)
        if with_first:
            pre = pre + dot(u_first[...], last[0, :, :, part].reshape(pieces * PIECE, TILE), TN)
        value, slope[:, cols] = gelu_and_slope(pre)
        act[:, cols] = value.astype(act.dtype)

    tiles = hidden // TILE
    each(tiles, lambda n: hidden_tile(first_quarter, n, True), 1)
    each(tiles, lambda n: hidden_tile(1 - first_quarter, n, False), 1)

    def store(i, matrices):
        def one(k):
            quarter, row = spot(i, k)
            start_piece(i, last.at[i, k], quarter, row, up_out, down_out, sems.at[3 + i], matrices)

        each(pieces, one)

    fetches[1].wait()
    store(0, (0,))
    store(2, (0,))

    for n in range(blocks):
        down_copy(n).wait()
        if n == blocks - 1:
            store(1, (1,))
            store(2, (1,))

        def place_down(k, n=n):
            for i in (1, 2):
                quarter, row = spot(i, k)
                cols = pl.ds(pl.multiple_of(quarter * hidden, 128), hidden)

                @pl.when(table[2, i * pieces + k] == n)
                def _(i=i, row=row, cols=cols):
                    if i == 1:
                        down[pl.ds(row, PIECE), cols] = last[1, k]
                    else:
                        down[pl.ds(pl.multiple_of(row + PIECE, 32), REST), cols] = last[2, k, REST:]

        each(pieces, place_down, 2)
        cols = pl.ds(n * BLOCK, BLOCK)
        out = dot(act[...], down[cols, :], NT)
        mine[:, cols] = out[:rows]
        other[:, cols] = out[rows:].astype(other.dtype)
    for i in range(3):
        wait_all(last.at[i], sems.at[3 + i])


def gen_forward(table, u_columns, partial, slots, up, down):
    width, group = u_columns.shape
    hidden = up.shape[1]
    rows, rest = group // 2, RING * RING * REST // 2
    f32, bf16 = jnp.float32, jnp.bfloat16
    shape = jax.ShapeDtypeStruct((width, hidden), bf16)
    last = [slots[i][3].reshape(RING * RING, PIECE, hidden // 2) for i in range(3)]
    return pl.pallas_call(
        gen_body,
        out_shape=(
            shape,
            shape,
            jax.ShapeDtypeStruct((group, hidden), f32),
            jax.ShapeDtypeStruct((rows, width), f32),
            jax.ShapeDtypeStruct((rows, width), bf16),
        ),
        in_specs=[IN_SMEM] + [IN_VMEM] * 2 + [IN_HBM] * 5,
        out_specs=(IN_HBM, IN_HBM) + (IN_VMEM,) * 3,
        scratch_shapes=[
            pltpu.VMEM(shape.shape, bf16),
            pltpu.VMEM((3, RING * RING, PIECE, hidden // 2), bf16),
            pltpu.VMEM((RING * RING * PIECE, group), bf16),
            pltpu.VMEM((2, rest, group), bf16),
            pltpu.VMEM((2, rest, hidden // 2), bf16),
            pltpu.VMEM((group, hidden), bf16),
            pltpu.SemaphoreType.DMA((6,)),
            pltpu.SemaphoreType.DMA((width // BLOCK,)),
        ],
        input_output_aliases={6: 0, 7: 1},
        compiler_params=pltpu.CompilerParams(vmem_limit_bytes=46 * MIB),
        cost_estimate=pl.CostEstimate(
            flops=3 * group * width * hidden,
            bytes_accessed=40 * MIB,
            transcendentals=group * hidden,
        ),
        name="gen_forward",
    )(table, u_columns, partial, *last, up, down)


def score_body(
    u_mine, u_other, adapt_in, adapt_out, up_in, down_in, slope, low, real, fake, others, *scratch
):
    u, act, up, down, up_sems, down_sems = scratch
    hidden_tiles, width_tiles = up.shape[1] // TILE, down.shape[0] // TILE
    each(hidden_tiles, lambda n: column_copy(up_in, up, up_sems, n).start(), 1)
    each(width_tiles, lambda n: row_copy(down_in, down, down_sems, n).start(), 1)
    rows = u_mine.shape[0]
    group = 2 * rows
    u[:rows] = u_mine[...]
    u[rows:] = u_other[...]
    low[...] = dot(u[...], adapt_in[...], NT).astype(low.dtype)

    def hidden_tile(n):
        column_copy(up_in, up, up_sems, n).wait()
        cols = tile_at(n)
        pre_real = dot(u[...], up[:, cols])
        pre_fake = pre_real + dot(low[...], adapt_out[:, cols])
        act[:group, cols] = gelu_value(pre_real).astype(act.dtype)
        value, slope[:, cols] = gelu_and_slope(pre_fake)
        act[group:, cols] = value.astype(act.dtype)

    each(hidden_tiles, hidden_tile, 1)

    def width_tile(n):
        row_copy(down_in, down, down_sems, n).wait()
        cols = tile_at(n)
        out = dot(act[...], down[cols, :], NT)
        real[:, cols] = out[:rows]
        others[:rows, cols] = out[rows:group].astype(others.dtype)
        fake[:, cols] = out[group : group + rows]
        others[rows:, cols] = out[group + rows :].astype(others.dtype)

    each(width_tiles, width_tile, 1)


def score_forward(u_mine, u_other, adapt_in, adapt_out, up, down):
    rows, width = u_mine.shape
    hidden = up.shape[1]
    group = 2 * rows
    f32, bf16 = jnp.float32, jnp.bfloat16
    return pl.pallas_call(
        score_body,
        out_shape=(
            jax.ShapeDtypeStruct((group, hidden), f32),
            jax.ShapeDtypeStruct((group, adapt_in.shape[0]), bf16),
            jax.ShapeDtypeStruct((rows, width), f32),
            jax.ShapeDtypeStruct((rows, width), f32),
            jax.ShapeDtypeStruct((group, width), bf16),
        ),
        in_specs=[IN_VMEM] * 4 + [IN_HBM] * 2,
        out_specs=(IN_VMEM,) * 5,
        scratch_shapes=[
            pltpu.VMEM((group, width), bf16),
            pltpu.VMEM((2 * group, hidden), bf16),
            pltpu.VMEM(up.shape, bf16),
            pltpu.VMEM(down.shape, bf16),
            pltpu.SemaphoreType.DMA((hidden // TILE,)),
            pltpu.SemaphoreType.DMA((width // TILE,)),
        ],
        compiler_params=pltpu.CompilerParams(vmem_limit_bytes=50 * MIB),
        cost_estimate=pl.CostEstimate(
            flops=6 * group * width * hidden,
            bytes_accessed=50 * MIB,
            transcendentals=2 * group * hidden,
        ),
        name="score_forward",
    )(u_mine, u_other, adapt_in, adapt_out, up, down)


def back_body(
    cots_mine, cots_other, slope_gen, slope_fake, low_gen, low_fake, gen_out, fake_out, down_in, grads, mix, *scratch
):
    cots, down, sems = scratch
    tiles = down.shape[1] // TILE
    each(tiles, lambda n: column_copy(down_in, down, sems, n).start(), 1)
    group = cots_mine.shape[0]
    rows = group // 2
    for i in range(2):
        cots[i * group : i * group + rows] = cots_mine[i * rows : (i + 1) * rows]
        cots[i * group + rows : (i + 1) * group] = cots_other[i * rows : (i + 1) * rows]
    mix[...] = jnp.zeros_like(mix)

    def hidden_tile(n):
        column_copy(down_in, down, sems, n).wait()
        cols = tile_at(n)
        raw = dot(cots[...], down[:, cols])
        back_gen = (raw[:group] * slope_gen[:, cols]).astype(jnp.bfloat16)
        back_fake = (raw[group:] * slope_fake[:, cols]).astype(jnp.bfloat16)
        grads[0, :, cols] = dot(low_gen[...], back_gen, TN).astype(grads.dtype)
        grads[1, :, cols] = dot(low_fake[...], back_fake, TN).astype(grads.dtype)
        mix[0] += dot(back_gen, gen_out[:, cols], NT)
        mix[1] += dot(back_fake, fake_out[:, cols], NT)

    each(tiles, hidden_tile, 1)


def backward(cots_mine, cots_other, slope_gen, slope_fake, low_gen, low_fake, gen_out, fake_out, down):
    group, width = cots_mine.shape
    hidden = down.shape[1]
    rank = low_gen.shape[1]
    f32, bf16 = jnp.float32, jnp.bfloat16
    return pl.pallas_call(
        back_body,
        out_shape=(
            jax.ShapeDtypeStruct((2, rank, hidden), bf16),
            jax.ShapeDtypeStruct((2, group, rank), f32),
        ),
        in_specs=[IN_VMEM] * 8 + [IN_HBM],
        out_specs=(IN_VMEM,) * 2,
        scratch_shapes=[
            pltpu.VMEM((2 * group, width), bf16),
            pltpu.VMEM(down.shape, bf16),
            pltpu.SemaphoreType.DMA((hidden // TILE,)),
        ],
        compiler_params=pltpu.CompilerParams(vmem_limit_bytes=40 * MIB),
        cost_estimate=pl.CostEstimate(
            flops=4 * group * width * hidden, bytes_accessed=30 * MIB, transcendentals=0
        ),
        name="backward",
    )(cots_mine, cots_other, slope_gen, slope_fake, low_gen, low_fake, gen_out, fake_out, down)


STRIP = 16


def embed_body(ends, steps, given, scale_ref, shift_ref, u_ref, mods_ref):
    half = given.shape[1] // 2
    place = lax.broadcasted_iota(jnp.int32, (1, half), 1).astype(jnp.float32)
    frequency = jnp.exp(-math.log(10000.0) * place / half)
    row = lax.broadcasted_iota(jnp.int32, (4, 1), 0)
    column = jnp.where(
        row < 2, jnp.where(row == 0, steps[0], steps[1]), jnp.where(row == 2, steps[2], steps[3])
    )
    phase = column * frequency
    embed = jnp.concatenate([jnp.sin(phase), jnp.cos(phase)], axis=1)
    scale = 1.0 + scale_ref[...] * embed
    shift = shift_ref[...] * embed
    mods_ref[0:2] = scale[2:4]
    mods_ref[2:4] = shift[2:4]

    def strip(n, carry):
        rows = pl.ds(pl.multiple_of(n * STRIP, STRIP), STRIP)
        in_last = n * STRIP + lax.broadcasted_iota(jnp.int32, (STRIP, 1), 0) >= ends[0]
        u_ref[rows] = modulate(
            given[rows],
            jnp.where(in_last, scale[1:2], scale[0:1]),
            jnp.where(in_last, shift[1:2], shift[0:1]),
        )
        return carry

    lax.fori_loop(0, given.shape[0] // STRIP, strip, 0)


def first_modulation(ends, steps, given, scale, shift):
    width = given.shape[1]
    return pl.pallas_call(
        embed_body,
        out_shape=(
            jax.ShapeDtypeStruct(given.shape, given.dtype),
            jax.ShapeDtypeStruct((4, width), jnp.float32),
        ),
        in_specs=[IN_SMEM] * 2 + [IN_VMEM] * 3,
        out_specs=(IN_VMEM,) * 2,
        compiler_params=pltpu.CompilerParams(vmem_limit_bytes=8 * MIB),
        cost_estimate=pl.CostEstimate(flops=0, bytes_accessed=2 * MIB, transcendentals=0),
        name="first_modulation",
    )(ends, steps, given, scale.reshape(1, width), shift.reshape(1, width))


def noise_body(ends, blends, given, noise, mine, other, mods, gate, latents_ref, noised_ref, u_ref):
    f32 = jnp.float32

    def strip(n, carry):
        rows = pl.ds(pl.multiple_of(n * STRIP, STRIP), STRIP)
        in_last = n * STRIP + lax.broadcasted_iota(jnp.int32, (STRIP, 1), 0) >= ends[0]
        out = mine[rows] + other[rows].astype(f32)
        latents = (given[rows].astype(f32) + gate[...] * out).astype(latents_ref.dtype)
        latents_ref[rows] = latents
        blend = jnp.where(in_last, blends[1], blends[0])
        noised = (
            (1.0 - blend) * latents.astype(f32) + blend * noise[rows].astype(f32)
        ).astype(noised_ref.dtype)
        noised_ref[rows] = noised
        scale = jnp.where(in_last, mods[1:2], mods[0:1])
        shift = jnp.where(in_last, mods[3:4], mods[2:3])
        u_ref[rows] = modulate(noised, scale, shift)
        return carry

    lax.fori_loop(0, given.shape[0] // STRIP, strip, 0)


def add_noise(ends, blends, given, noise, mine, other, mods, gate):
    shape = jax.ShapeDtypeStruct(given.shape, given.dtype)
    return pl.pallas_call(
        noise_body,
        out_shape=(shape,) * 3,
        in_specs=[IN_SMEM] * 2 + [IN_VMEM] * 6,
        out_specs=(IN_VMEM,) * 3,
        compiler_params=pltpu.CompilerParams(vmem_limit_bytes=10 * MIB),
        cost_estimate=pl.CostEstimate(flops=0, bytes_accessed=6 * MIB, transcendentals=0),
        name="add_noise",
    )(ends, blends, given, noise, mine, other, mods, gate)


def cotangent_body(scale, real, fake, others, gate_ref, noise, latents, noised, diff_ref, cots):
    f32 = jnp.float32
    count = real.shape[0]

    def strip(n, carry):
        start = pl.multiple_of(n * STRIP, STRIP)
        rows, second = pl.ds(start, STRIP), pl.ds(count + start, STRIP)
        gate = gate_ref[...]
        out_real = real[rows] + others[rows].astype(f32)
        out_fake = fake[rows] + others[second].astype(f32)
        diff = (gate * (out_fake - out_real)).astype(diff_ref.dtype)
        diff_ref[rows] = diff
        cots[rows] = (gate * diff.astype(f32) * scale).astype(cots.dtype)
        target = noise[rows].astype(f32) - latents[rows].astype(f32)
        cots[second] = (
            gate * (noised[rows].astype(f32) + gate * out_fake - target) * scale
        ).astype(cots.dtype)
        return carry

    lax.fori_loop(0, count // STRIP, strip, 0)


def cotangents(scale, real, fake, others, gate, noise, latents, noised):
    rows, width = real.shape
    return pl.pallas_call(
        functools.partial(cotangent_body, scale),
        out_shape=(
            jax.ShapeDtypeStruct((rows, width), noise.dtype),
            jax.ShapeDtypeStruct((2 * rows, width), noise.dtype),
        ),
        in_specs=[IN_VMEM] * 7,
        out_specs=(IN_VMEM,) * 2,
        compiler_params=pltpu.CompilerParams(vmem_limit_bytes=12 * MIB),
        cost_estimate=pl.CostEstimate(flops=0, bytes_accessed=8 * MIB, transcendentals=0),
        name="cotangents",
    )(real, fake, others, gate, noise, latents, noised)


def three_terms(value):
    high = lax.reduce_precision(value, 8, 7)
    rest = value - high
    middle = lax.reduce_precision(rest, 8, 7)
    low = rest - middle
    return jnp.concatenate([high, middle, low], axis=1).astype(jnp.bfloat16)


def local(
    gen_input,
    noise_score,
    gen_steps,
    score_steps,
    base_up,
    base_down,
    gen_adapt_in,
    gen_adapt_out,
    fake_adapt_in,
    fake_adapt_out,
    modulation_scale,
    modulation_shift,
    output_gate,
):
    bf16, f32 = jnp.bfloat16, jnp.float32
    shard_rows, width = gen_input.shape
    hidden = base_up.shape[1]
    rank = gen_adapt_in.shape[1]
    image_count = gen_steps.shape[0]
    loss_scale = 1.0 / math.sqrt(image_count * IMG_TOK)
    core = lax.axis_index("core")
    xl = lax.axis_index("xl")
    first_row = lax.axis_index(AXES) * shard_rows
    first_image = first_row // IMG_TOK
    last_image = (first_row + shard_rows - 1) // IMG_TOK
    def two_steps(steps):
        return jnp.stack([steps[first_image], steps[last_image]])

    def both_quarters(mine):
        theirs = lax.ppermute(mine, "xl", [(0, 1), (1, 0)])
        quarters = [jnp.where(xl == 0, mine, theirs), jnp.where(xl == 0, theirs, mine)]
        return jnp.concatenate(quarters, axis=1)

    blends = (two_steps(score_steps).astype(f32) + 0.5) / 1000.0
    ends = (last_image * IMG_TOK - first_row).astype(jnp.int32).reshape(1)
    steps = jnp.concatenate([two_steps(gen_steps), two_steps(score_steps)]).astype(f32)
    place = [lax.axis_index("z"), lax.axis_index("y"), lax.axis_index("xh") * 2 + xl, 1 - 2 * core]
    coords = jnp.stack(place).astype(jnp.int32)
    spots = [piece_place(coords, i, 3, jnp.arange(RING * RING, dtype=jnp.int32)) for i in range(3)]
    quarters, rows = [jnp.concatenate([spot[n] for spot in spots]) for n in range(2)]
    table = jnp.stack([quarters, rows, rows // BLOCK])

    def prepare(given):
        u_mine, mods = first_modulation(ends, steps, given, modulation_scale, modulation_shift)
        u_other = swap_cores(u_mine)
        u_columns = jnp.concatenate([u_mine, u_other], axis=0).T
        return u_mine, u_other, u_columns, mods, blends, coords, table

    down_rows = base_down.T
    slots, adapt_out, prepared = ring_slots(
        [
            base_up[:PIECE],
            down_rows[:PIECE],
            jnp.concatenate([base_up[PIECE:], down_rows[PIECE:]], axis=0),
        ],
        jnp.concatenate([gen_adapt_out, fake_adapt_out], axis=0),
        both_quarters,
        (gen_input,),
        prepare,
    )
    u_gen, u_gen_other, u_columns, mods, blends, coords, table = prepared
    gen_out, fake_out = adapt_out[:rank], adapt_out[rank:]
    up_part, down_part, partial, low_gen = load_weights(
        coords, table, u_gen, u_gen_other, gen_adapt_in.T, gen_out, slots
    )
    up_all, down_all, slope_gen, out_mine, out_other = gen_forward(
        table, u_columns, partial, slots, up_part, down_part
    )
    gate = output_gate.reshape(1, width)
    latents, noised, u_score = add_noise(
        ends, blends, gen_input, noise_score, out_mine, swap_cores(out_other), mods, gate
    )
    u_score_other = swap_cores(u_score)
    slope_fake, low_fake, out_real, out_fake, outs_other = score_forward(
        u_score, u_score_other, fake_adapt_in.T, fake_out, up_all, down_all
    )
    score_diff, cots = cotangents(
        loss_scale, out_real, out_fake, swap_cores(outs_other), gate, noise_score, latents, noised
    )
    out_grads, mix = backward(
        cots, swap_cores(cots), slope_gen, slope_fake, low_gen, low_fake, gen_out, fake_out, down_all
    )
    mix = jnp.concatenate([mix[0], mix[1]], axis=1)
    mix_other = swap_cores(mix)
    mix = mix + jnp.concatenate([mix_other[shard_rows:], mix_other[:shard_rows]], axis=0)

    def in_grad(u, mix_part):
        product = contract(u, three_terms(mix_part), 0, 0)
        total = product[:, :rank] + product[:, rank : 2 * rank] + product[:, 2 * rank :]
        chips = total.reshape(-1, 2, width // 128, rank)
        return jnp.where(core == 0, chips[:, 0], chips[:, 1])

    u_gen_group = jnp.concatenate([u_gen, u_gen_other], axis=0)
    u_score_group = jnp.concatenate([u_score, u_score_other], axis=0)
    in_grads = jnp.concatenate(
        [in_grad(u_gen_group, mix[:, :rank]), in_grad(u_score_group, mix[:, rank:])], axis=2
    )
    chips, in_rows = in_grads.shape[0], in_grads.shape[1]
    groups = chips // 2
    out_grads = out_grads.reshape(2, groups, rank // groups, 2, hidden).transpose(1, 3, 0, 2, 4)
    out_rows = 2 * (rank // groups) * hidden // 128
    packed = jnp.concatenate(
        [in_grads.astype(bf16), out_grads.reshape(chips, out_rows, 128)], axis=1
    )
    received = lax.all_to_all(packed, CHIPS, 0, 0, tiled=True)
    summed = jnp.sum(received.astype(f32), axis=0)
    gen_grad_in, fake_grad_in = summed[:in_rows, :rank], summed[:in_rows, rank:]
    grads_out = summed[in_rows:].reshape(2, rank // groups, hidden)
    return (score_diff, gen_grad_in, grads_out[0], fake_grad_in, grads_out[1])


def solution(mesh):
    fine = Mesh(mesh.devices.reshape(4, 4, 2, 2, 2), AXES)
    dp, mp = ("z", "y", "xh"), ("xl", "core")
    return jax.shard_map(
        local,
        mesh=fine,
        in_specs=(
            P(AXES, None),
            P(AXES, None),
            P(),
            P(),
            P(dp, mp),
            P(mp, dp),
            P(),
            P(None, mp),
            P(),
            P(None, mp),
            P(),
            P(),
            P(),
        ),
        out_specs=(
            P(AXES, None),
            P(AXES, None),
            P(dp, mp),
            P(AXES, None),
            P(dp, mp),
        ),
        check_vma=False,
    )
```

```python
import functools
import math

import jax
import jax.numpy as jnp
from jax import lax
from jax.experimental import pallas as pl
from jax.experimental.pallas import tpu as pltpu
from jax.sharding import Mesh
from jax.sharding import PartitionSpec as P

IMG_TOK = 1024
AXES = ("z", "y", "xh", "xl", "core")
CHIPS = ("z", "y", "xh", "xl")

gelu_coef = 0.044715
root_two_pi = math.sqrt(2.0 / math.pi)


def gelu_value(pre):
    inner_arg = root_two_pi * (pre + gelu_coef * pre * pre * pre)
    return 0.5 * pre * (1.0 + jnp.tanh(inner_arg))


def gelu_slope(pre):
    tanh_val = jnp.tanh(root_two_pi * (pre + gelu_coef * pre * pre * pre))
    return 0.5 * (1.0 + tanh_val) + 0.5 * pre * (1.0 - tanh_val * tanh_val) * root_two_pi * (
        1.0 + 3.0 * gelu_coef * pre * pre
    )


def modulate(rows, scale_rows, shift_rows):
    widened = rows.astype(jnp.float32)
    normed = widened * lax.rsqrt(jnp.mean(widened * widened, axis=1, keepdims=True) + 1e-06)
    return (normed * scale_rows + shift_rows).astype(jnp.bfloat16)


def matmul(left, right):
    return jnp.dot(left, right, preferred_element_type=jnp.float32)


def contract(left, right, left_dim, right_dim):
    return lax.dot_general(
        left, right, (((left_dim,), (right_dim,)), ((), ())), preferred_element_type=jnp.float32
    )


def swap_cores(value):
    return lax.ppermute(value, "core", [(0, 1), (1, 0)])


RING_AXES = (("y", "z", "x"), ("z", "x", "y"), ("x", "y", "z"))
RING = 4


def chip_ring(axis):
    pairs = []
    for device in range(128):
        place = {"z": device // 32, "y": device // 8 % 4, "x": device // 2 % 4, "core": device % 2}
        step = 1 if place["core"] == 0 else -1
        place[axis] = (place[axis] + step) % RING
        target = place["z"] * 32 + place["y"] * 8 + place["x"] * 2 + place["core"]
        pairs.append((device, target))
    return pairs


def send(piece, i, phase):
    return lax.ppermute(piece, AXES, chip_ring(RING_AXES[i][phase]))


def gathered(pieces, phase):
    rows = pieces[0].shape[0]
    whole = [jnp.zeros((RING * rows, piece.shape[1]), piece.dtype) for piece in pieces]
    for step in range(RING):
        if step:
            pieces = [send(piece, i, phase) for i, piece in enumerate(pieces)]
        whole = [
            lax.dynamic_update_slice(buffer, piece, (step * rows, 0))
            for buffer, piece in zip(whole, pieces)
        ]
    return whole


def ring_slots(pieces, adapters, exchange, inputs, prepare):
    pieces = gathered(pieces, 0)
    pieces[2], adapters = lax.optimization_barrier((pieces[2], adapters))
    exchanged = exchange(adapters)
    pieces = gathered(pieces, 1)
    pieces[2], exchanged = lax.optimization_barrier((pieces[2], exchanged))
    slots = [[piece] for piece in pieces]
    for step in range(1, RING):
        if step == RING - 1:
            slots[2][-1], prepared = lax.optimization_barrier((slots[2][-1], prepared))
        for i in range(3):
            slots[i].append(send(slots[i][-1], i, 2))
        if step == 1:
            arrived = [slots[i][1] for i in range(3)]
            _, inputs = lax.optimization_barrier((arrived, inputs))
            prepared = prepare(*inputs)
    return slots, exchanged, prepared


SHARD = 96
PIECE = 64
REST = SHARD - PIECE
TILE = 512
BLOCK = 8 * SHARD
MIB = 2**20
ANYWHERE = pl.BlockSpec(memory_space=pl.ANY)
IN_VMEM = pl.BlockSpec(memory_space=pltpu.VMEM)
IN_SMEM = pl.BlockSpec(memory_space=pltpu.SMEM)
NT = (((1,), (1,)), ((), ()))
TN = (((0,), (0,)), ((), ()))


def dot(left, right, dims=(((1,), (0,)), ((), ()))):
    return lax.dot_general(left, right, dims, preferred_element_type=jnp.float32)


def gelu_and_slope(pre):
    square = pre * pre
    tanh_val = jnp.tanh(root_two_pi * (pre + gelu_coef * square * pre))
    half = 0.5 * (1.0 + tanh_val)
    slope = half + 0.5 * pre * (1.0 - tanh_val * tanh_val) * root_two_pi * (
        1.0 + 3.0 * gelu_coef * square
    )
    return pre * half, slope


IN_HBM = pl.BlockSpec(memory_space=pltpu.HBM)


def piece_place(place_ref, i, step, k):
    me = {"z": place_ref[0], "y": place_ref[1], "x": place_ref[2]}
    direction = place_ref[3]
    first, second, third = RING_AXES[i]

    def source(axis, distance):
        return (me[axis] - distance * direction + RING) & (RING - 1)

    zero = k - k
    at = {
        first: source(first, k & (RING - 1)),
        second: source(second, k >> 2),
        third: source(third, step + zero),
    }
    group = (at["z"] * 4 + at["y"]) * 2 + (at["x"] >> 1)
    return at["x"] & 1, group * SHARD


def each(count, one, unroll=4):
    def step(k, carry):
        one(k)
        return carry

    lax.fori_loop(0, count, step, 0, unroll=unroll)


def wait_all(ref, sem):
    pltpu.make_async_copy(ref, ref, sem).wait()


def start_piece(i, source, quarter, row, up, down, sem, matrices=(0, 1)):
    hidden = source.shape[1]
    cols = pl.ds(pl.multiple_of(quarter * hidden, 128), hidden)
    if i < 2:
        target = (up, down)[i].at[pl.ds(row, PIECE), cols]
        pltpu.make_async_copy(source, target, sem).start()
    else:
        for n in matrices:
            rows = pl.ds(pl.multiple_of(row + PIECE, 32), REST)
            target = (up, down)[n].at[rows, cols]
            pltpu.make_async_copy(source.at[pl.ds(n * REST, REST)], target, sem).start()


def load_body(place_ref, table, u_mine, u_other, adapt_in, adapt, *refs):
    slots, (up_out, down_out, partial, low, up, down, u, sems) = refs[:9], refs[9:]
    for n, slot in enumerate(slots):
        step, i = n // 3, n % 3

        def one(k, slot=slot, step=step, i=i, n=n):
            quarter, row = piece_place(place_ref, i, step, k)
            start_piece(i, slot.at[k], quarter, pl.multiple_of(row, 32), up, down, sems.at[n])

        each(RING * RING, one)
    rows, pieces = u_mine.shape[0], RING * RING
    u[:rows] = u_mine[...]
    u[rows:] = u_other[...]
    low[...] = dot(u[...], adapt_in[...], NT).astype(low.dtype)
    hidden = up.shape[1] // 2

    def clear(k):
        for i, first, count in ((0, 0, PIECE), (2, PIECE, REST)):
            place = pl.ds(pl.multiple_of(table[1, i * pieces + k] + first, 32), count)
            cols = pl.ds(pl.multiple_of(table[0, i * pieces + k] * hidden, 128), hidden)
            up[place, cols] = jnp.zeros((count, hidden), up.dtype)

    each(pieces, clear, 2)
    for n, slot in enumerate(slots):
        if n % 3 != 1:
            wait_all(slot, sems.at[n])
    up_copy = pltpu.make_async_copy(up, up_out, sems.at[9])
    up_copy.start()
    for n, slot in enumerate(slots):
        if n % 3 == 1:
            wait_all(slot, sems.at[n])
    down_copy = pltpu.make_async_copy(down, down_out, sems.at[10])
    down_copy.start()

    def hidden_tile(n):
        cols = tile_at(n)
        partial[:, cols] = dot(u[...], up[:, cols]) + dot(low[...], adapt[:, cols])

    each(up.shape[1] // TILE, hidden_tile, 1)
    up_copy.wait()
    down_copy.wait()


def load_weights(coords, table, u_mine, u_other, adapt_in, adapt, slots):
    rows, width = u_mine.shape
    group, rank, hidden = 2 * rows, adapt_in.shape[0], adapt.shape[1]
    f32, bf16 = jnp.float32, jnp.bfloat16
    flat = [
        slots[i][step].reshape(RING * RING, PIECE, hidden // 2) for step in range(3) for i in range(3)
    ]
    shape = jax.ShapeDtypeStruct((width, hidden), bf16)
    return pl.pallas_call(
        load_body,
        out_shape=(
            shape,
            shape,
            jax.ShapeDtypeStruct((group, hidden), f32),
            jax.ShapeDtypeStruct((group, rank), bf16),
        ),
        in_specs=[IN_SMEM] * 2 + [IN_VMEM] * 4 + [IN_HBM] * 9,
        out_specs=(IN_HBM, IN_HBM, IN_VMEM, IN_VMEM),
        scratch_shapes=[
            pltpu.VMEM(shape.shape, bf16),
            pltpu.VMEM(shape.shape, bf16),
            pltpu.VMEM((group, width), bf16),
            pltpu.SemaphoreType.DMA((11,)),
        ],
        compiler_params=pltpu.CompilerParams(vmem_limit_bytes=46 * MIB),
        cost_estimate=pl.CostEstimate(
            flops=2 * group * width * hidden, bytes_accessed=16 * width * hidden, transcendentals=0
        ),
        name="load_weights",
    )(coords, table, u_mine, u_other, adapt_in, adapt, *flat)


def column_copy(source, target, sems, n):
    cols = pl.ds(pl.multiple_of(n * TILE, TILE), TILE)
    return pltpu.make_async_copy(source.at[:, cols], target.at[:, cols], sems.at[n])


def row_copy(source, target, sems, n):
    rows = pl.ds(pl.multiple_of(n * TILE, TILE), TILE)
    return pltpu.make_async_copy(source.at[rows], target.at[rows], sems.at[n])


def tile_at(n):
    return pl.ds(pl.multiple_of(n * TILE, TILE), TILE)


def gen_body(table, u_columns, partial, *refs):
    slots, (up_in, down_in, up_out, down_out, slope, mine, other) = refs[:3], refs[3:10]
    down, last, u_first, u_rest, up_rest, act, sems, down_sems = refs[10:]
    rows = mine.shape[0]
    pieces = RING * RING
    hidden = last.shape[3]
    fetches = [pltpu.make_async_copy(slots[i], last.at[i], sems.at[i]) for i in range(3)]

    def down_copy(n):
        part = pl.ds(pl.multiple_of(n * BLOCK, BLOCK), BLOCK)
        return pltpu.make_async_copy(down_in.at[part], down.at[part], down_sems.at[n])

    blocks = down.shape[0] // BLOCK
    fetches[0].start()
    fetches[2].start()

    def spot(i, k):
        return table[0, i * pieces + k], pl.multiple_of(table[1, i * pieces + k], 32)

    for k in range(pieces):
        u_first[k * PIECE : (k + 1) * PIECE] = u_columns[pl.ds(spot(0, k)[1], PIECE), :]
        at = pl.ds(k // 2 * REST, REST)
        u_rest[k % 2, at] = u_columns[pl.ds(pl.multiple_of(spot(2, k)[1] + PIECE, 32), REST), :]
    fetches[0].wait()
    fetches[2].wait()
    fetches[1].start()
    for n in range(blocks):
        down_copy(n).start()
    for k in range(pieces):
        up_rest[k % 2, pl.ds(k // 2 * REST, REST)] = last[2, k, :REST]
    first_quarter, rest_quarter = table[0, 0], table[0, 2 * pieces]

    def hidden_tile(quarter, n, with_first):
        part = tile_at(n)
        cols = pl.ds(pl.multiple_of(quarter * hidden + n * TILE, TILE), TILE)
        side = jnp.where(quarter == rest_quarter, 0, 1)
        pre = partial[:, cols] + dot(u_rest[side], up_rest[side, :, part], TN)
        if with_first:
            pre = pre + dot(u_first[...], last[0, :, :, part].reshape(pieces * PIECE, TILE), TN)
        value, slope[:, cols] = gelu_and_slope(pre)
        act[:, cols] = value.astype(act.dtype)

    tiles = hidden // TILE
    each(tiles, lambda n: hidden_tile(first_quarter, n, True), 1)
    each(tiles, lambda n: hidden_tile(1 - first_quarter, n, False), 1)

    def store(i, matrices):
        def one(k):
            quarter, row = spot(i, k)
            start_piece(i, last.at[i, k], quarter, row, up_out, down_out, sems.at[3 + i], matrices)

        each(pieces, one)

    fetches[1].wait()
    store(0, (0,))
    store(2, (0,))

    for n in range(blocks):
        down_copy(n).wait()
        if n == blocks - 1:
            store(1, (1,))
            store(2, (1,))

        def place_down(k, n=n):
            for i in (1, 2):
                quarter, row = spot(i, k)
                cols = pl.ds(pl.multiple_of(quarter * hidden, 128), hidden)

                @pl.when(table[2, i * pieces + k] == n)
                def _(i=i, row=row, cols=cols):
                    if i == 1:
                        down[pl.ds(row, PIECE), cols] = last[1, k]
                    else:
                        down[pl.ds(pl.multiple_of(row + PIECE, 32), REST), cols] = last[2, k, REST:]

        each(pieces, place_down, 2)
        cols = pl.ds(n * BLOCK, BLOCK)
        out = dot(act[...], down[cols, :], NT)
        mine[:, cols] = out[:rows]
        other[:, cols] = out[rows:].astype(other.dtype)
    for i in range(3):
        wait_all(last.at[i], sems.at[3 + i])


def gen_forward(table, u_columns, partial, slots, up, down):
    width, group = u_columns.shape
    hidden = up.shape[1]
    rows, rest = group // 2, RING * RING * REST // 2
    f32, bf16 = jnp.float32, jnp.bfloat16
    shape = jax.ShapeDtypeStruct((width, hidden), bf16)
    last = [slots[i][3].reshape(RING * RING, PIECE, hidden // 2) for i in range(3)]
    return pl.pallas_call(
        gen_body,
        out_shape=(
            shape,
            shape,
            jax.ShapeDtypeStruct((group, hidden), f32),
            jax.ShapeDtypeStruct((rows, width), f32),
            jax.ShapeDtypeStruct((rows, width), bf16),
        ),
        in_specs=[IN_SMEM] + [IN_VMEM] * 2 + [IN_HBM] * 5,
        out_specs=(IN_HBM, IN_HBM) + (IN_VMEM,) * 3,
        scratch_shapes=[
            pltpu.VMEM(shape.shape, bf16),
            pltpu.VMEM((3, RING * RING, PIECE, hidden // 2), bf16),
            pltpu.VMEM((RING * RING * PIECE, group), bf16),
            pltpu.VMEM((2, rest, group), bf16),
            pltpu.VMEM((2, rest, hidden // 2), bf16),
            pltpu.VMEM((group, hidden), bf16),
            pltpu.SemaphoreType.DMA((6,)),
            pltpu.SemaphoreType.DMA((width // BLOCK,)),
        ],
        input_output_aliases={6: 0, 7: 1},
        compiler_params=pltpu.CompilerParams(vmem_limit_bytes=46 * MIB),
        cost_estimate=pl.CostEstimate(
            flops=3 * group * width * hidden,
            bytes_accessed=40 * MIB,
            transcendentals=group * hidden,
        ),
        name="gen_forward",
    )(table, u_columns, partial, *last, up, down)


def score_body(
    u_mine, u_other, adapt_in, adapt_out, up_in, down_in, slope, low, real, fake, others, *scratch
):
    u, act, up, down, up_sems, down_sems = scratch
    hidden_tiles, width_tiles = up.shape[1] // TILE, down.shape[0] // TILE
    each(hidden_tiles, lambda n: column_copy(up_in, up, up_sems, n).start(), 1)
    each(width_tiles, lambda n: row_copy(down_in, down, down_sems, n).start(), 1)
    rows = u_mine.shape[0]
    group = 2 * rows
    u[:rows] = u_mine[...]
    u[rows:] = u_other[...]
    low[...] = dot(u[...], adapt_in[...], NT).astype(low.dtype)

    def hidden_tile(n):
        column_copy(up_in, up, up_sems, n).wait()
        cols = tile_at(n)
        pre_real = dot(u[...], up[:, cols])
        pre_fake = pre_real + dot(low[...], adapt_out[:, cols])
        act[:group, cols] = gelu_value(pre_real).astype(act.dtype)
        value, slope[:, cols] = gelu_and_slope(pre_fake)
        act[group:, cols] = value.astype(act.dtype)

    each(hidden_tiles, hidden_tile, 1)

    def width_tile(n):
        row_copy(down_in, down, down_sems, n).wait()
        cols = tile_at(n)
        out = dot(act[...], down[cols, :], NT)
        real[:, cols] = out[:rows]
        others[:rows, cols] = out[rows:group].astype(others.dtype)
        fake[:, cols] = out[group : group + rows]
        others[rows:, cols] = out[group + rows :].astype(others.dtype)

    each(width_tiles, width_tile, 1)


def score_forward(u_mine, u_other, adapt_in, adapt_out, up, down):
    rows, width = u_mine.shape
    hidden = up.shape[1]
    group = 2 * rows
    f32, bf16 = jnp.float32, jnp.bfloat16
    return pl.pallas_call(
        score_body,
        out_shape=(
            jax.ShapeDtypeStruct((group, hidden), f32),
            jax.ShapeDtypeStruct((group, adapt_in.shape[0]), bf16),
            jax.ShapeDtypeStruct((rows, width), f32),
            jax.ShapeDtypeStruct((rows, width), f32),
            jax.ShapeDtypeStruct((group, width), bf16),
        ),
        in_specs=[IN_VMEM] * 4 + [IN_HBM] * 2,
        out_specs=(IN_VMEM,) * 5,
        scratch_shapes=[
            pltpu.VMEM((group, width), bf16),
            pltpu.VMEM((2 * group, hidden), bf16),
            pltpu.VMEM(up.shape, bf16),
            pltpu.VMEM(down.shape, bf16),
            pltpu.SemaphoreType.DMA((hidden // TILE,)),
            pltpu.SemaphoreType.DMA((width // TILE,)),
        ],
        compiler_params=pltpu.CompilerParams(vmem_limit_bytes=50 * MIB),
        cost_estimate=pl.CostEstimate(
            flops=6 * group * width * hidden,
            bytes_accessed=50 * MIB,
            transcendentals=2 * group * hidden,
        ),
        name="score_forward",
    )(u_mine, u_other, adapt_in, adapt_out, up, down)


def back_body(
    cots_mine, cots_other, slope_gen, slope_fake, low_gen, low_fake, gen_out, fake_out, down_in, grads, mix, *scratch
):
    cots, down, sems = scratch
    tiles = down.shape[1] // TILE
    each(tiles, lambda n: column_copy(down_in, down, sems, n).start(), 1)
    group = cots_mine.shape[0]
    rows = group // 2
    for i in range(2):
        cots[i * group : i * group + rows] = cots_mine[i * rows : (i + 1) * rows]
        cots[i * group + rows : (i + 1) * group] = cots_other[i * rows : (i + 1) * rows]
    mix[...] = jnp.zeros_like(mix)

    def hidden_tile(n):
        column_copy(down_in, down, sems, n).wait()
        cols = tile_at(n)
        raw = dot(cots[...], down[:, cols])
        back_gen = (raw[:group] * slope_gen[:, cols]).astype(jnp.bfloat16)
        back_fake = (raw[group:] * slope_fake[:, cols]).astype(jnp.bfloat16)
        grads[0, :, cols] = dot(low_gen[...], back_gen, TN).astype(grads.dtype)
        grads[1, :, cols] = dot(low_fake[...], back_fake, TN).astype(grads.dtype)
        mix[0] += dot(back_gen, gen_out[:, cols], NT)
        mix[1] += dot(back_fake, fake_out[:, cols], NT)

    each(tiles, hidden_tile, 1)


def backward(cots_mine, cots_other, slope_gen, slope_fake, low_gen, low_fake, gen_out, fake_out, down):
    group, width = cots_mine.shape
    hidden = down.shape[1]
    rank = low_gen.shape[1]
    f32, bf16 = jnp.float32, jnp.bfloat16
    return pl.pallas_call(
        back_body,
        out_shape=(
            jax.ShapeDtypeStruct((2, rank, hidden), bf16),
            jax.ShapeDtypeStruct((2, group, rank), f32),
        ),
        in_specs=[IN_VMEM] * 8 + [IN_HBM],
        out_specs=(IN_VMEM,) * 2,
        scratch_shapes=[
            pltpu.VMEM((2 * group, width), bf16),
            pltpu.VMEM(down.shape, bf16),
            pltpu.SemaphoreType.DMA((hidden // TILE,)),
        ],
        compiler_params=pltpu.CompilerParams(vmem_limit_bytes=40 * MIB),
        cost_estimate=pl.CostEstimate(
            flops=4 * group * width * hidden, bytes_accessed=30 * MIB, transcendentals=0
        ),
        name="backward",
    )(cots_mine, cots_other, slope_gen, slope_fake, low_gen, low_fake, gen_out, fake_out, down)


STRIP = 16


def embed_body(ends, steps, given, scale_ref, shift_ref, u_ref, mods_ref):
    half = given.shape[1] // 2
    place = lax.broadcasted_iota(jnp.int32, (1, half), 1).astype(jnp.float32)
    frequency = jnp.exp(-math.log(10000.0) * place / half)
    row = lax.broadcasted_iota(jnp.int32, (4, 1), 0)
    column = jnp.where(
        row < 2, jnp.where(row == 0, steps[0], steps[1]), jnp.where(row == 2, steps[2], steps[3])
    )
    phase = column * frequency
    embed = jnp.concatenate([jnp.sin(phase), jnp.cos(phase)], axis=1)
    scale = 1.0 + scale_ref[...] * embed
    shift = shift_ref[...] * embed
    mods_ref[0:2] = scale[2:4]
    mods_ref[2:4] = shift[2:4]

    def strip(n, carry):
        rows = pl.ds(pl.multiple_of(n * STRIP, STRIP), STRIP)
        in_last = n * STRIP + lax.broadcasted_iota(jnp.int32, (STRIP, 1), 0) >= ends[0]
        u_ref[rows] = modulate(
            given[rows],
            jnp.where(in_last, scale[1:2], scale[0:1]),
            jnp.where(in_last, shift[1:2], shift[0:1]),
        )
        return carry

    lax.fori_loop(0, given.shape[0] // STRIP, strip, 0)


def first_modulation(ends, steps, given, scale, shift):
    width = given.shape[1]
    return pl.pallas_call(
        embed_body,
        out_shape=(
            jax.ShapeDtypeStruct(given.shape, given.dtype),
            jax.ShapeDtypeStruct((4, width), jnp.float32),
        ),
        in_specs=[IN_SMEM] * 2 + [IN_VMEM] * 3,
        out_specs=(IN_VMEM,) * 2,
        compiler_params=pltpu.CompilerParams(vmem_limit_bytes=8 * MIB),
        cost_estimate=pl.CostEstimate(flops=0, bytes_accessed=2 * MIB, transcendentals=0),
        name="first_modulation",
    )(ends, steps, given, scale.reshape(1, width), shift.reshape(1, width))


def noise_body(ends, blends, given, noise, mine, other, mods, gate, latents_ref, noised_ref, u_ref):
    f32 = jnp.float32

    def strip(n, carry):
        rows = pl.ds(pl.multiple_of(n * STRIP, STRIP), STRIP)
        in_last = n * STRIP + lax.broadcasted_iota(jnp.int32, (STRIP, 1), 0) >= ends[0]
        out = mine[rows] + other[rows].astype(f32)
        latents = (given[rows].astype(f32) + gate[...] * out).astype(latents_ref.dtype)
        latents_ref[rows] = latents
        blend = jnp.where(in_last, blends[1], blends[0])
        noised = (
            (1.0 - blend) * latents.astype(f32) + blend * noise[rows].astype(f32)
        ).astype(noised_ref.dtype)
        noised_ref[rows] = noised
        scale = jnp.where(in_last, mods[1:2], mods[0:1])
        shift = jnp.where(in_last, mods[3:4], mods[2:3])
        u_ref[rows] = modulate(noised, scale, shift)
        return carry

    lax.fori_loop(0, given.shape[0] // STRIP, strip, 0)


def add_noise(ends, blends, given, noise, mine, other, mods, gate):
    shape = jax.ShapeDtypeStruct(given.shape, given.dtype)
    return pl.pallas_call(
        noise_body,
        out_shape=(shape,) * 3,
        in_specs=[IN_SMEM] * 2 + [IN_VMEM] * 6,
        out_specs=(IN_VMEM,) * 3,
        compiler_params=pltpu.CompilerParams(vmem_limit_bytes=10 * MIB),
        cost_estimate=pl.CostEstimate(flops=0, bytes_accessed=6 * MIB, transcendentals=0),
        name="add_noise",
    )(ends, blends, given, noise, mine, other, mods, gate)


def cotangent_body(scale, real, fake, others, gate_ref, noise, latents, noised, diff_ref, cots):
    f32 = jnp.float32
    count = real.shape[0]

    def strip(n, carry):
        start = pl.multiple_of(n * STRIP, STRIP)
        rows, second = pl.ds(start, STRIP), pl.ds(count + start, STRIP)
        gate = gate_ref[...]
        out_real = real[rows] + others[rows].astype(f32)
        out_fake = fake[rows] + others[second].astype(f32)
        diff = (gate * (out_fake - out_real)).astype(diff_ref.dtype)
        diff_ref[rows] = diff
        cots[rows] = (gate * diff.astype(f32) * scale).astype(cots.dtype)
        target = noise[rows].astype(f32) - latents[rows].astype(f32)
        cots[second] = (
            gate * (noised[rows].astype(f32) + gate * out_fake - target) * scale
        ).astype(cots.dtype)
        return carry

    lax.fori_loop(0, count // STRIP, strip, 0)


def cotangents(scale, real, fake, others, gate, noise, latents, noised):
    rows, width = real.shape
    return pl.pallas_call(
        functools.partial(cotangent_body, scale),
        out_shape=(
            jax.ShapeDtypeStruct((rows, width), noise.dtype),
            jax.ShapeDtypeStruct((2 * rows, width), noise.dtype),
        ),
        in_specs=[IN_VMEM] * 7,
        out_specs=(IN_VMEM,) * 2,
        compiler_params=pltpu.CompilerParams(vmem_limit_bytes=12 * MIB),
        cost_estimate=pl.CostEstimate(flops=0, bytes_accessed=8 * MIB, transcendentals=0),
        name="cotangents",
    )(real, fake, others, gate, noise, latents, noised)


def three_terms(value):
    high = lax.reduce_precision(value, 8, 7)
    rest = value - high
    middle = lax.reduce_precision(rest, 8, 7)
    low = rest - middle
    return jnp.concatenate([high, middle, low], axis=1).astype(jnp.bfloat16)


def local(
    gen_input,
    noise_score,
    gen_steps,
    score_steps,
    base_up,
    base_down,
    gen_adapt_in,
    gen_adapt_out,
    fake_adapt_in,
    fake_adapt_out,
    modulation_scale,
    modulation_shift,
    output_gate,
):
    bf16, f32 = jnp.bfloat16, jnp.float32
    shard_rows, width = gen_input.shape
    hidden = base_up.shape[1]
    rank = gen_adapt_in.shape[1]
    image_count = gen_steps.shape[0]
    loss_scale = 1.0 / math.sqrt(image_count * IMG_TOK)
    core = lax.axis_index("core")
    xl = lax.axis_index("xl")
    first_row = lax.axis_index(AXES) * shard_rows
    first_image = first_row // IMG_TOK
    last_image = (first_row + shard_rows - 1) // IMG_TOK
    def two_steps(steps):
        return jnp.stack([steps[first_image], steps[last_image]])

    def swap_quarters(mine):
        return lax.ppermute(mine, "xl", [(0, 1), (1, 0)])

    blends = (two_steps(score_steps).astype(f32) + 0.5) / 1000.0
    ends = (last_image * IMG_TOK - first_row).astype(jnp.int32).reshape(1)
    steps = jnp.concatenate([two_steps(gen_steps), two_steps(score_steps)]).astype(f32)
    place = [lax.axis_index("z"), lax.axis_index("y"), lax.axis_index("xh") * 2 + xl, 1 - 2 * core]
    coords = jnp.stack(place).astype(jnp.int32)
    spots = [piece_place(coords, i, 3, jnp.arange(RING * RING, dtype=jnp.int32)) for i in range(3)]
    quarters, rows = [jnp.concatenate([spot[n] for spot in spots]) for n in range(2)]
    table = jnp.stack([quarters, rows, rows // BLOCK])

    def prepare(given):
        u_mine, mods = first_modulation(ends, steps, given, modulation_scale, modulation_shift)
        u_other = swap_cores(u_mine)
        u_columns = jnp.concatenate([u_mine, u_other], axis=0).T
        return u_mine, u_other, u_columns, mods, blends, coords, table

    down_rows = base_down.T
    adapters = jnp.concatenate([gen_adapt_out, fake_adapt_out], axis=0)
    slots, theirs, prepared = ring_slots(
        [
            base_up[:PIECE],
            down_rows[:PIECE],
            jnp.concatenate([base_up[PIECE:], down_rows[PIECE:]], axis=0),
        ],
        adapters,
        swap_quarters,
        (gen_input,),
        prepare,
    )
    u_gen, u_gen_other, u_columns, mods, blends, coords, table = prepared
    quarters = [jnp.where(xl == 0, adapters, theirs), jnp.where(xl == 0, theirs, adapters)]
    adapt_out = jnp.concatenate(quarters, axis=1)
    gen_out, fake_out = adapt_out[:rank], adapt_out[rank:]
    up_part, down_part, partial, low_gen = load_weights(
        coords, table, u_gen, u_gen_other, gen_adapt_in.T, gen_out, slots
    )
    up_all, down_all, slope_gen, out_mine, out_other = gen_forward(
        table, u_columns, partial, slots, up_part, down_part
    )
    gate = output_gate.reshape(1, width)
    latents, noised, u_score = add_noise(
        ends, blends, gen_input, noise_score, out_mine, swap_cores(out_other), mods, gate
    )
    u_score_other = swap_cores(u_score)
    slope_fake, low_fake, out_real, out_fake, outs_other = score_forward(
        u_score, u_score_other, fake_adapt_in.T, fake_out, up_all, down_all
    )
    score_diff, cots = cotangents(
        loss_scale, out_real, out_fake, swap_cores(outs_other), gate, noise_score, latents, noised
    )
    out_grads, mix = backward(
        cots, swap_cores(cots), slope_gen, slope_fake, low_gen, low_fake, gen_out, fake_out, down_all
    )
    mix = jnp.concatenate([mix[0], mix[1]], axis=1)
    mix_other = swap_cores(mix)
    mix = mix + jnp.concatenate([mix_other[shard_rows:], mix_other[:shard_rows]], axis=0)

    def in_grad(u, mix_part):
        product = contract(u, three_terms(mix_part), 0, 0)
        total = product[:, :rank] + product[:, rank : 2 * rank] + product[:, 2 * rank :]
        chips = total.reshape(-1, 2, width // 128, rank)
        return jnp.where(core == 0, chips[:, 0], chips[:, 1])

    u_gen_group = jnp.concatenate([u_gen, u_gen_other], axis=0)
    u_score_group = jnp.concatenate([u_score, u_score_other], axis=0)
    in_grads = jnp.concatenate(
        [in_grad(u_gen_group, mix[:, :rank]), in_grad(u_score_group, mix[:, rank:])], axis=2
    )
    chips, in_rows = in_grads.shape[0], in_grads.shape[1]
    groups = chips // 2
    out_grads = out_grads.reshape(2, groups, rank // groups, 2, hidden).transpose(1, 3, 0, 2, 4)
    out_rows = 2 * (rank // groups) * hidden // 128
    packed = jnp.concatenate(
        [in_grads.astype(bf16), out_grads.reshape(chips, out_rows, 128)], axis=1
    )
    received = lax.all_to_all(packed, CHIPS, 0, 0, tiled=True)
    summed = jnp.sum(received.astype(f32), axis=0)
    gen_grad_in, fake_grad_in = summed[:in_rows, :rank], summed[:in_rows, rank:]
    grads_out = summed[in_rows:].reshape(2, rank // groups, hidden)
    return (score_diff, gen_grad_in, grads_out[0], fake_grad_in, grads_out[1])


def solution(mesh):
    fine = Mesh(mesh.devices.reshape(4, 4, 2, 2, 2), AXES)
    dp, mp = ("z", "y", "xh"), ("xl", "core")
    return jax.shard_map(
        local,
        mesh=fine,
        in_specs=(
            P(AXES, None),
            P(AXES, None),
            P(),
            P(),
            P(dp, mp),
            P(mp, dp),
            P(),
            P(None, mp),
            P(),
            P(None, mp),
            P(),
            P(),
            P(),
        ),
        out_specs=(
            P(AXES, None),
            P(AXES, None),
            P(dp, mp),
            P(AXES, None),
            P(dp, mp),
        ),
        check_vma=False,
    )
```
